32 devices in a mesh: groups: 2 (over y), tp: 8 (over z, x), dp: 2 (over core).
Axes of the slice: x: 2, y: 2, z: 4, core: 2. Of those that a mesh axis runs over, the one named last changes fastest.
Arguments:
- tokens: bfloat16 [4, 2, 8, 5120], P(('groups', 'dp'), None, 'tp'), parts along dimension 0, may hold values from -400 to 400
- norm_gain: float32 [5120], replicated, may hold values from 0.5 to 1.5
- gate_weight: bfloat16 [5120, 12800], P(None, 'tp'), may hold values from -0.125 to 0.125
- up_weight: bfloat16 [5120, 12800], P(None, 'tp'), may hold values from -0.125 to 0.125
- down_weight: bfloat16 [12800, 5120], P('tp'), may hold values from -0.0546875 to 0.0546875
- cotangent: bfloat16 [4, 2, 8, 5120], P(('groups', 'dp'), None, 'tp'), parts along dimension 0, may hold values from -6 to 6
Outputs:
- input_grad: bfloat16 [4, 2, 8, 5120], P(('groups', 'dp'), None, 'tp'), parts along dimension 0
- gain_grad: float32 [10240], P('groups'), parts along dimension 0
- gate_grad: bfloat16 [10240, 12800], P(('groups', 'dp'), 'tp'), parts along dimension 0
- up_grad: bfloat16 [10240, 12800], P(('groups', 'dp'), 'tp'), parts along dimension 0
- down_grad: bfloat16 [12800, 10240], P('tp', ('groups', 'dp')), parts along dimension 1
The draws below stay inside these ranges and needn't reach their ends.
There are 2 independent parts, one for each index of `groups`. The reference program is written for one: setup_inputs(seed, part) draws one part's arguments, and reference() takes and returns one part's arrays. A program takes and returns all parts, laid end to end along the dimension named above; an argument that names none is the same for every part. Nothing has to cross between parts.
All inputs are finite; a program needn't handle non-finite values.
Results may differ from the reference program's by a relative error of at most 0.0074.
Values may be sent and summed in bfloat16 or wider, within the bound.
No kernel may reach another device: no remote copies, remote signals or barrier semaphores. Data moves between devices by JAX's collectives and lax.ppermute only.
A program may use at most 256 MiB of HBM per device.

```python
import math
import jax
import jax.numpy as jnp
from jax import lax

D = 5120
FFW = 12800
MICRO = 2
SEQ = 8
N_DP = 2


def draw_tokens(key, part):
    key = jax.random.fold_in(key, 11)
    first, second, third = jax.random.split(key, 3)
    shape = (N_DP, MICRO, SEQ, D)
    base = jnp.clip(jax.random.normal(first, shape, jnp.float32), -4.0, 4.0)
    row_scale = jnp.exp(jax.random.uniform(second, (N_DP, MICRO, SEQ, 1), jnp.float32, 0.0, math.log(10.0)))
    column_scale = jnp.exp(jax.random.uniform(third, (D,), jnp.float32, 0.0, math.log(10.0)))
    return (base * row_scale * column_scale).astype(jnp.bfloat16)


def strengthened(entries, rng, source, target, parts, factor):
    def block_of(axis_at):
        return (jnp.arange(entries.shape[axis_at]) // (entries.shape[axis_at] // parts)).reshape((-1,) + (1,) * (entries.ndim - 1 - axis_at))

    near = jax.random.permutation(rng, parts)[block_of(target)]
    other_side = (block_of(target) + parts // 2) % parts
    return jnp.where((block_of(source) == near) | (block_of(source) == other_side), factor * entries, entries)


def levels(rng, dims, cuts, least, top_value):
    loudness = 1.0
    for axis_at, parts in cuts:
        heights = jax.random.uniform(jax.random.fold_in(jax.random.fold_in(rng, 6), axis_at), (parts,), jnp.float32, least / len(cuts), top_value / len(cuts))
        loudness = loudness * jnp.repeat(jnp.exp(heights), dims[axis_at] // parts).reshape((-1,) + (1,) * (len(dims) - 1 - axis_at))
    return loudness


def gaussian(key, extent, deviation, most, cuts=(), kind=jnp.bfloat16):
    factor_of = levels(key, extent, cuts, -0.22, 0.18) if cuts else 1.0
    array = jax.random.normal(key, extent, jnp.float32) * deviation * factor_of
    return jnp.minimum(jnp.maximum(array, -most), most).astype(kind)


def bell_draw_with(own_key, dims, spread, bound, pieces, heavy, kind=jnp.bfloat16):
    array = spread * jax.random.normal(own_key, dims, jnp.float32)
    if pieces:
        array = array * levels(own_key, dims, pieces, -0.22, 0.18)
    return jnp.clip(strengthened(array, jax.random.fold_in(own_key, 3), *heavy), -bound, bound).astype(kind)


def setup_inputs(seed: int = 0, part: int = 0) -> dict:
    key_list = jax.random.split(jax.random.key(seed), 7)
    own_keys = jax.random.split(jax.random.fold_in(key_list[6], part), 7)
    tokens = draw_tokens(jax.random.fold_in(jax.random.fold_in(key_list[6], part), 71), part)
    norm_gain = jnp.clip(1.0 + 0.1 * jax.random.normal(key_list[1], (D,), jnp.float32), 0.5, 1.5)
    gate_weight = bell_draw_with(key_list[2], (D, FFW), D ** -0.5, 0.125, ((1, 8),), (1, 0, 8, 2.0))
    up_weight = bell_draw_with(key_list[3], (D, FFW), D ** -0.5, 0.125, ((1, 8),), (1, 0, 8, 2.0))
    down_weight = gaussian(key_list[4], (FFW, D), FFW ** -0.5, 0.0546875, ((0, 8),))
    cotangent = gaussian(own_keys[5], (N_DP, MICRO, SEQ, D), 1.0, 6.0, ((0, 2), (2, 8)))
    return {"tokens": tokens, "norm_gain": norm_gain, "gate_weight": gate_weight, "up_weight": up_weight, "down_weight": down_weight, "cotangent": cotangent}


EPSILON = 1e-06

def rounded(value):
    return lax.optimization_barrier(value.astype(jnp.bfloat16)).astype(jnp.float32)

def reference(tokens, norm_gain, gate_weight, up_weight, down_weight, cotangent):
    model_width = tokens.shape[-1]
    grad_list = []
    gain_total = jnp.zeros((model_width,), jnp.float32)
    gate_total = jnp.zeros(gate_weight.shape, jnp.float32)
    up_total = jnp.zeros(up_weight.shape, jnp.float32)
    down_total = jnp.zeros(down_weight.shape, jnp.float32)
    for dp_index in range(N_DP):
        values = tokens[dp_index].reshape(-1, model_width).astype(jnp.float32)
        inverse = lax.rsqrt(lax.optimization_barrier(jnp.mean(values * values, axis=-1, keepdims=True)) + EPSILON)
        scaled = values * inverse
        normed = (scaled * norm_gain).astype(jnp.bfloat16)
        incoming = cotangent[dp_index].reshape(-1, model_width)
        gate_value = jnp.dot(normed, gate_weight, preferred_element_type=jnp.float32)
        up_value = jnp.dot(normed, up_weight, preferred_element_type=jnp.float32)
        sigmoid_gate = jax.nn.sigmoid(gate_value)
        active = gate_value * sigmoid_gate
        hidden = (active * up_value).astype(jnp.bfloat16)
        grad_hidden = jnp.dot(incoming, down_weight.T, preferred_element_type=jnp.float32)
        grad_gate = (grad_hidden * up_value * sigmoid_gate * (1.0 + gate_value * (1.0 - sigmoid_gate))).astype(jnp.bfloat16)
        grad_up = (grad_hidden * active).astype(jnp.bfloat16)
        grad_normed = jnp.dot(grad_gate, gate_weight.T, preferred_element_type=jnp.float32)
        grad_normed = grad_normed + jnp.dot(grad_up, up_weight.T, preferred_element_type=jnp.float32)
        grad_scaled = grad_normed * norm_gain
        projected = lax.optimization_barrier(jnp.mean(grad_scaled * scaled, axis=-1, keepdims=True))
        input_rows = incoming.astype(jnp.float32) + inverse * (grad_scaled - scaled * projected)
        grad_list.append(input_rows.astype(jnp.bfloat16).reshape(tokens.shape[1:]))
        gain_total = gain_total + lax.optimization_barrier(jnp.sum(grad_normed * scaled, axis=0))
        gate_total = gate_total + rounded(jnp.dot(normed.T, grad_gate, preferred_element_type=jnp.float32))
        up_total = up_total + rounded(jnp.dot(normed.T, grad_up, preferred_element_type=jnp.float32))
        down_total = down_total + rounded(jnp.dot(hidden.T, incoming, preferred_element_type=jnp.float32))
    return (jnp.stack(grad_list), gain_total, gate_total.astype(jnp.bfloat16), up_total.astype(jnp.bfloat16), down_total.astype(jnp.bfloat16))
```

```python
import functools

import jax
import jax.numpy as jnp
from jax import lax
from jax.experimental import pallas as pl
from jax.experimental.pallas import tpu as pltpu
from jax.sharding import PartitionSpec as P

EPSILON = 1e-06
LANES = 128
MIB = 1 << 20


def contract(left, right, left_dim, right_dim):
    return lax.dot_general(
        left, right, (((left_dim,), (right_dim,)), ((), ())), preferred_element_type=jnp.float32
    )


def norm_tokens(values_in, norm_gain):
    values = values_in.astype(jnp.float32)
    inverse = lax.rsqrt(jnp.mean(values * values, axis=-1, keepdims=True) + EPSILON)
    scaled = values * inverse
    return (scaled, inverse, (scaled * norm_gain).astype(jnp.bfloat16))


def local_pass(normed_all, grads_all, gate_weight, up_weight, down_weight):
    gate_value = jnp.dot(normed_all, gate_weight, preferred_element_type=jnp.float32)
    up_value = jnp.dot(normed_all, up_weight, preferred_element_type=jnp.float32)
    sigmoid_gate = jax.nn.sigmoid(gate_value)
    active = gate_value * sigmoid_gate
    hidden = (active * up_value).astype(jnp.bfloat16)
    grad_hidden = contract(grads_all, down_weight, 1, 1)
    grad_gate = (
        grad_hidden * up_value * sigmoid_gate * (1.0 + gate_value * (1.0 - sigmoid_gate))
    ).astype(jnp.bfloat16)
    grad_up = (grad_hidden * active).astype(jnp.bfloat16)
    partial_value = contract(grad_gate, gate_weight, 1, 1) + contract(grad_up, up_weight, 1, 1)
    gate_term = contract(normed_all, grad_gate, 0, 0)
    up_term = contract(normed_all, grad_up, 0, 0)
    down_term = contract(hidden, grads_all, 0, 0)
    return (partial_value, gate_term, up_term, down_term)


def general_body(tokens, norm_gain, gate_weight, up_weight, down_weight, cotangent):
    micro_count, own_tokens, model_width = (tokens.shape[1], tokens.shape[2], tokens.shape[3])
    tp_count = lax.axis_size("tp")
    scaled, inverse, normed = norm_tokens(tokens[0], norm_gain)
    normed_all, grads_all = (
        lax.all_gather(normed, "tp", axis=1, tiled=True),
        lax.all_gather(cotangent[0], "tp", axis=1, tiled=True),
    )
    partial_value, gate_term, up_term, down_term = local_pass(
        normed_all.reshape(-1, model_width),
        grads_all.reshape(-1, model_width),
        gate_weight,
        up_weight,
        down_weight,
    )
    pieces = lax.all_to_all(
        partial_value.reshape(micro_count, tp_count, own_tokens, model_width),
        "tp",
        split_axis=1,
        concat_axis=1,
        tiled=True,
    )
    grad_normed = jnp.sum(pieces, axis=1)
    grad_scaled = grad_normed * norm_gain
    projected = jnp.mean(grad_scaled * scaled, axis=-1, keepdims=True)
    input_rows = cotangent[0].astype(jnp.float32) + inverse * (grad_scaled - scaled * projected)
    gain_term = jnp.sum((grad_normed * scaled).reshape(-1, model_width), axis=0)
    gain_grad = lax.psum(gain_term, ("tp", "dp"))
    gate_grad, up_grad, down_grad = (
        lax.psum_scatter(gate_term.astype(jnp.bfloat16), "dp", scatter_dimension=0, tiled=True),
        lax.psum_scatter(up_term.astype(jnp.bfloat16), "dp", scatter_dimension=0, tiled=True),
        lax.psum_scatter(down_term.astype(jnp.bfloat16), "dp", scatter_dimension=1, tiled=True),
    )
    return (input_rows.astype(jnp.bfloat16)[None], gain_grad, gate_grad, up_grad, down_grad)


VMEM_SPEC = pl.BlockSpec(memory_space=pltpu.VMEM)
ANY_SPEC = pl.BlockSpec(memory_space=pl.ANY)


def exchange(value, axis, bits):
    count = lax.axis_size(axis)
    return lax.ppermute(value, axis, [(i, i ^ bits) for i in range(count)])


def gather_kernel(rows, *refs):
    pieces, out_ref, held = refs[:-2], refs[-2], refs[-1]
    count = len(pieces)
    for k, piece in enumerate(pieces):
        value = piece[...].astype(jnp.float32)
        held[rows * k : rows * (k + 1), :] = value[:rows]
        held[rows * (count + k) : rows * (count + k + 1), :] = value[rows:]
    out_ref[...] = held[...].astype(jnp.bfloat16)


def gather_rows(pieces, rows):
    width = pieces[0].shape[1]
    total = 2 * rows * len(pieces)
    return pl.pallas_call(
        functools.partial(gather_kernel, rows),
        out_shape=jax.ShapeDtypeStruct((total, width), jnp.bfloat16),
        in_specs=[VMEM_SPEC] * len(pieces),
        out_specs=VMEM_SPEC,
        scratch_shapes=[pltpu.VMEM((total, width), jnp.float32)],
        compiler_params=pltpu.CompilerParams(vmem_limit_bytes=8 * MIB),
        name="gather_rows",
    )(*pieces)


def hidden_kernel(
    chunks, own_ref, peer_ref, gain_ref, gate_hbm, up_hbm, down_hbm,
    packed_ref, mine_ref, theirs_ref, gain_part_ref, rows_ref,
    gate_buf, up_buf, down_buf, x_buf, c_buf, inverse_buf, acc_g, acc_u, acc_h, left_buf, sems,
):
    half = acc_g.shape[0]
    toks = x_buf.shape[1]
    each = toks // 2
    width = x_buf.shape[2]
    first = pl.multiple_of(lax.axis_index("dp") * half, 16)
    weights = ((gate_hbm, gate_buf), (up_hbm, up_buf), (down_hbm, down_buf))

    def fetch(c, w):
        source, target = weights[w]
        at = pl.ds(pl.multiple_of(c * width, LANES), width)
        return pltpu.make_async_copy(
            source.at[pl.ds(first, half), at], target.at[c], sems.at[w, c]
        )

    for c in range(chunks):
        for w in range(3):
            fetch(c, w).start()

    squares = jnp.zeros((toks, 1), jnp.float32)
    for c in range(chunks):
        at = slice(c * width, (c + 1) * width)
        value = jnp.concatenate([own_ref[:each, at], peer_ref[:each, at]], axis=0)
        value = value.astype(jnp.float32)
        squares = squares + jnp.sum(value * value, axis=-1, keepdims=True)
    inverse = lax.rsqrt(squares / (chunks * width) + EPSILON)
    inverse_buf[...] = jnp.broadcast_to(inverse, inverse_buf.shape)
    for c in range(chunks):
        at = slice(c * width, (c + 1) * width)
        value = jnp.concatenate([own_ref[:each, at], peer_ref[:each, at]], axis=0)
        normed = (value.astype(jnp.float32) * inverse * gain_ref[:, at]).astype(jnp.bfloat16)
        incoming = jnp.concatenate([own_ref[each:, at], peer_ref[each:, at]], axis=0)
        x_buf[c] = normed
        c_buf[c] = incoming
        rows_ref[:toks, at] = normed
        rows_ref[toks:, at] = incoming
    acc_g[...] = jnp.zeros_like(acc_g)
    acc_u[...] = jnp.zeros_like(acc_u)
    acc_h[...] = jnp.zeros_like(acc_h)

    def forward(c, carry):
        for w in range(3):
            fetch(c, w).wait()
        acc_g[...] += contract(gate_buf[c], x_buf[c], 1, 1)
        acc_u[...] += contract(up_buf[c], x_buf[c], 1, 1)
        acc_h[...] += contract(down_buf[c], c_buf[c], 1, 1)
        return carry

    lax.fori_loop(0, chunks, forward, 0)

    step = 80 if half % 80 == 0 else 16

    def pointwise(i, carry):
        at = pl.ds(pl.multiple_of(i * step, 16), step)
        gate, up, grad = acc_g[at, :], acc_u[at, :], acc_h[at, :]
        sigmoid = jax.nn.sigmoid(gate)
        active = gate * sigmoid
        grad_gate = grad * up * sigmoid * (1.0 + gate * (1.0 - sigmoid))
        parts = [grad_gate, grad * active, active * up, jnp.zeros_like(active)]
        packed_ref[at, :] = jnp.concatenate(parts, axis=1).astype(jnp.bfloat16)
        return carry

    lax.fori_loop(0, half // step, pointwise, 0)
    left_buf[...] = packed_ref[...].astype(jnp.float32).T.astype(jnp.bfloat16)

    def backward(c, carry):
        at = pl.ds(pl.multiple_of(c * width, LANES), width)
        part = jnp.dot(left_buf[:toks, :], gate_buf[c], preferred_element_type=jnp.float32)
        part += jnp.dot(
            left_buf[toks : 2 * toks, :], up_buf[c], preferred_element_type=jnp.float32
        )
        value = jnp.concatenate([own_ref[:each, at], peer_ref[:each, at]], axis=0)
        scaled = value.astype(jnp.float32) * inverse_buf[:, :1]
        gain_part_ref[:, at] = jnp.sum(part * scaled, axis=0, keepdims=True)
        mine_ref[:, at] = part[:each]
        theirs_ref[:, at] = part[each:].astype(jnp.bfloat16)
        return carry

    lax.fori_loop(0, chunks, backward, 0)


def hidden_pass(own, peer, gain, gate_t, up_t, down):
    ffw, model = down.shape
    half, toks = ffw // 2, own.shape[0]
    each = toks // 2
    chunks = model // 512
    width = model // chunks
    big = pltpu.VMEM((chunks, half, width), jnp.bfloat16)
    small = pltpu.VMEM((chunks, toks, width), jnp.bfloat16)
    acc = pltpu.VMEM((half, toks), jnp.float32)
    return pl.pallas_call(
        functools.partial(hidden_kernel, chunks),
        out_shape=(
            jax.ShapeDtypeStruct((half, LANES), jnp.bfloat16),
            jax.ShapeDtypeStruct((each, model), jnp.float32),
            jax.ShapeDtypeStruct((each, model), jnp.bfloat16),
            jax.ShapeDtypeStruct((1, model), jnp.float32),
            jax.ShapeDtypeStruct((2 * toks, model), jnp.bfloat16),
        ),
        in_specs=[VMEM_SPEC] * 3 + [ANY_SPEC] * 3,
        out_specs=(VMEM_SPEC,) * 5,
        scratch_shapes=[
            big, big, big, small, small,
            pltpu.VMEM((toks, LANES), jnp.float32),
            acc, acc, acc,
            pltpu.VMEM((LANES, half), jnp.bfloat16),
            pltpu.SemaphoreType.DMA((3, chunks)),
        ],
        compiler_params=pltpu.CompilerParams(vmem_limit_bytes=48 * MIB),
        cost_estimate=pl.CostEstimate(
            flops=10 * toks * half * model, bytes_accessed=6 * half * model, transcendentals=half * toks
        ),
        name="hidden_pass",
    )(own, peer, gain, gate_t, up_t, down)


def weight_kernel(toks, swapped, place_ref, packed_ref, rows_ref, *refs):
    outs = refs[-3:]
    width = rows_ref.shape[1]
    each = toks // 2
    normed, incoming = rows_ref[:toks, :], rows_ref[toks:, :]
    if swapped:
        normed = jnp.concatenate([normed[each:], normed[:each]], axis=0)
        incoming = jnp.concatenate([incoming[each:], incoming[:each]], axis=0)
    for k, right in enumerate((normed, normed, incoming)):
        left = packed_ref[:, k * toks : (k + 1) * toks]
        outs[k][...] = jnp.dot(left, right, preferred_element_type=jnp.float32).astype(jnp.bfloat16)


def weight_pass(place, packed, rows, ffw, swapped, before=()):
    half, toks, model = packed.shape[0], rows.shape[0] // 2, rows.shape[1]
    own_width = model // 2
    width = 512 if own_width % 512 == 0 else LANES
    steps = own_width // width
    row = (lambda place: 1 - place[0]) if swapped else (lambda place: place[0])
    out = jax.ShapeDtypeStruct((ffw, own_width), jnp.bfloat16)
    return pl.pallas_call(
        functools.partial(weight_kernel, toks, swapped),
        out_shape=(out,) * 3,
        grid_spec=pltpu.PrefetchScalarGridSpec(
            num_scalar_prefetch=1,
            grid=(steps,),
            in_specs=[
                pl.BlockSpec((half, LANES), lambda j, place: (0, 0)),
                pl.BlockSpec((2 * toks, width), lambda j, place: (0, place[0] * steps + j)),
            ]
            + [ANY_SPEC] * len(before),
            out_specs=(pl.BlockSpec((half, width), lambda j, place: (row(place), j)),) * 3,
        ),
        input_output_aliases={3 + i: i for i in range(len(before))},
        compiler_params=pltpu.CompilerParams(vmem_limit_bytes=24 * MIB),
        cost_estimate=pl.CostEstimate(
            flops=6 * toks * half * own_width, bytes_accessed=6 * half * own_width, transcendentals=0
        ),
        name="weight_pass",
    )(place, packed, rows, *before)


def split_kernel(rows, mine_ref, theirs_ref, gain_ref, their_gain_ref, own_ref, gain_out_ref, *refs):
    outs, held = refs[:-1], refs[-1]
    held[...] = mine_ref[...] + theirs_ref[...].astype(jnp.float32)
    gain = gain_ref[...] + their_gain_ref[...]
    high = gain.astype(jnp.bfloat16)
    low = (gain - high.astype(jnp.float32)).astype(jnp.bfloat16)
    own_ref[...] = held[:rows, :]
    gain_out_ref[...] = gain
    for k, out in enumerate(outs):
        piece = held[rows * (k + 1) : rows * (k + 2), :]
        out[:rows, :] = piece.astype(jnp.bfloat16)
        out[rows : rows + 1, :] = high
        out[rows + 1 : rows + 2, :] = low


def split_rows(rows, mine, theirs, gain, their_gain):
    total, model = mine.shape
    count = total // rows
    f32, bf16 = jnp.float32, jnp.bfloat16
    return pl.pallas_call(
        functools.partial(split_kernel, rows),
        out_shape=(
            jax.ShapeDtypeStruct((rows, model), f32),
            jax.ShapeDtypeStruct((1, model), f32),
        )
        + (jax.ShapeDtypeStruct((rows + 2, model), bf16),) * (count - 1),
        in_specs=[VMEM_SPEC] * 4,
        out_specs=(VMEM_SPEC,) * (count + 1),
        scratch_shapes=[pltpu.VMEM((total, model), f32)],
        compiler_params=pltpu.CompilerParams(vmem_limit_bytes=8 * MIB),
        name="split_rows",
    )(mine, theirs, gain, their_gain)


def finish_kernel(rows, tokens_ref, incoming_ref, norm_gain_ref, own_ref, gain_ref, *refs):
    pieces, input_ref, gain_out_ref = refs[:-2], refs[-2], refs[-1]
    grad_normed, gain = own_ref[...], gain_ref[...]
    for piece in pieces:
        value = piece[...].astype(jnp.float32)
        grad_normed = grad_normed + value[:rows]
        gain = gain + (value[rows : rows + 1] + value[rows + 1 : rows + 2])
    gain_out_ref[...] = gain
    values = tokens_ref[...].astype(jnp.float32)
    inverse = lax.rsqrt(jnp.mean(values * values, axis=-1, keepdims=True) + EPSILON)
    scaled = values * inverse
    grad_scaled = grad_normed * norm_gain_ref[...]
    projected = jnp.mean(grad_scaled * scaled, axis=-1, keepdims=True)
    result = incoming_ref[...].astype(jnp.float32) + inverse * (grad_scaled - scaled * projected)
    input_ref[...] = result.astype(jnp.bfloat16)


def finish(rows, tokens, incoming, norm_gain, own, gain, pieces):
    model = tokens.shape[1]
    return pl.pallas_call(
        functools.partial(finish_kernel, rows),
        out_shape=(
            jax.ShapeDtypeStruct((rows, model), jnp.bfloat16),
            jax.ShapeDtypeStruct((1, model), jnp.float32),
        ),
        in_specs=[VMEM_SPEC] * (5 + len(pieces)),
        out_specs=(VMEM_SPEC,) * 2,
        compiler_params=pltpu.CompilerParams(vmem_limit_bytes=8 * MIB),
        name="finish",
    )(tokens, incoming, norm_gain, own, gain, *pieces)


def small_body(tokens, norm_gain, gate_weight, up_weight, down_weight, cotangent):
    rows, model = tokens.shape[1] * tokens.shape[2], tokens.shape[3]
    ffw = down_weight.shape[0]
    tp_count = lax.axis_size("tp")
    place = lax.axis_index("dp").astype(jnp.int32).reshape(1)
    own_tokens, own_incoming = tokens.reshape(rows, model), cotangent.reshape(rows, model)
    gain_row = norm_gain.reshape(1, model)

    piece = jnp.concatenate([own_tokens, own_incoming], axis=0)
    pieces = [piece] + [exchange(piece, "tp", k) for k in range(1, tp_count)]
    own = gather_rows(pieces, rows)
    peer = exchange(own, "dp", 1)
    packed, mine, theirs, gain_part, all_rows = hidden_pass(
        own, peer, gain_row, gate_weight.T, up_weight.T, down_weight
    )
    peer_packed = exchange(packed, "dp", 1)
    from_peer, gain_from_peer = exchange(theirs, "dp", 1), exchange(gain_part, "dp", 1)
    grads = weight_pass(place, packed, all_rows, ffw, False)
    own_sum, gain_sum, *sends = split_rows(rows, mine, from_peer, gain_part, gain_from_peer)
    received = [exchange(send, "tp", k + 1) for k, send in enumerate(sends)]
    gate_t, up_t, down_grad = weight_pass(place, peer_packed, all_rows, ffw, True, grads)
    input_rows, gain_grad = finish(
        rows, own_tokens, own_incoming, gain_row, own_sum, gain_sum, received
    )
    return (
        input_rows.reshape(tokens.shape),
        gain_grad.reshape(model),
        gate_t.T,
        up_t.T,
        down_grad,
    )


def body(tokens, norm_gain, gate_weight, up_weight, down_weight, cotangent):
    tp_count, dp_count = lax.axis_size("tp"), lax.axis_size("dp")
    ffw, model = down_weight.shape
    toks = tokens.shape[1] * tokens.shape[2] * tp_count * dp_count
    small = (
        dp_count == 2
        and tp_count & (tp_count - 1) == 0
        and toks == 32
        and model % 1024 == 0
        and ffw % 32 == 0
        and 3 * ffw * model <= 40 * MIB
    )
    chosen = small_body if small else general_body
    return chosen(tokens, norm_gain, gate_weight, up_weight, down_weight, cotangent)


def solution(mesh):
    placed = (
        P(("groups", "dp"), None, "tp", None),
        P(),
        P(None, "tp"),
        P(None, "tp"),
        P("tp", None),
        P(("groups", "dp"), None, "tp", None),
    )
    return jax.shard_map(
        body,
        mesh=mesh,
        in_specs=placed,
        out_specs=(
            P(("groups", "dp"), None, "tp", None),
            P("groups"),
            P(("groups", "dp"), "tp"),
            P(("groups", "dp"), "tp"),
            P("tp", ("groups", "dp")),
        ),
        check_vma=False,
    )
```

```python
import functools

import jax
import jax.numpy as jnp
from jax import lax
from jax.experimental import pallas as pl
from jax.experimental.pallas import tpu as pltpu
from jax.sharding import PartitionSpec as P

EPSILON = 1e-06
LANES = 128
MIB = 1 << 20


def contract(left, right, left_dim, right_dim):
    return lax.dot_general(
        left, right, (((left_dim,), (right_dim,)), ((), ())), preferred_element_type=jnp.float32
    )


def norm_tokens(values_in, norm_gain):
    values = values_in.astype(jnp.float32)
    inverse = lax.rsqrt(jnp.mean(values * values, axis=-1, keepdims=True) + EPSILON)
    scaled = values * inverse
    return (scaled, inverse, (scaled * norm_gain).astype(jnp.bfloat16))


def local_pass(normed_all, grads_all, gate_weight, up_weight, down_weight):
    gate_value = jnp.dot(normed_all, gate_weight, preferred_element_type=jnp.float32)
    up_value = jnp.dot(normed_all, up_weight, preferred_element_type=jnp.float32)
    sigmoid_gate = jax.nn.sigmoid(gate_value)
    active = gate_value * sigmoid_gate
    hidden = (active * up_value).astype(jnp.bfloat16)
    grad_hidden = contract(grads_all, down_weight, 1, 1)
    grad_gate = (
        grad_hidden * up_value * sigmoid_gate * (1.0 + gate_value * (1.0 - sigmoid_gate))
    ).astype(jnp.bfloat16)
    grad_up = (grad_hidden * active).astype(jnp.bfloat16)
    partial_value = contract(grad_gate, gate_weight, 1, 1) + contract(grad_up, up_weight, 1, 1)
    gate_term = contract(normed_all, grad_gate, 0, 0)
    up_term = contract(normed_all, grad_up, 0, 0)
    down_term = contract(hidden, grads_all, 0, 0)
    return (partial_value, gate_term, up_term, down_term)


def general_body(tokens, norm_gain, gate_weight, up_weight, down_weight, cotangent):
    micro_count, own_tokens, model_width = (tokens.shape[1], tokens.shape[2], tokens.shape[3])
    tp_count = lax.axis_size("tp")
    scaled, inverse, normed = norm_tokens(tokens[0], norm_gain)
    normed_all, grads_all = (
        lax.all_gather(normed, "tp", axis=1, tiled=True),
        lax.all_gather(cotangent[0], "tp", axis=1, tiled=True),
    )
    partial_value, gate_term, up_term, down_term = local_pass(
        normed_all.reshape(-1, model_width),
        grads_all.reshape(-1, model_width),
        gate_weight,
        up_weight,
        down_weight,
    )
    pieces = lax.all_to_all(
        partial_value.reshape(micro_count, tp_count, own_tokens, model_width),
        "tp",
        split_axis=1,
        concat_axis=1,
        tiled=True,
    )
    grad_normed = jnp.sum(pieces, axis=1)
    grad_scaled = grad_normed * norm_gain
    projected = jnp.mean(grad_scaled * scaled, axis=-1, keepdims=True)
    input_rows = cotangent[0].astype(jnp.float32) + inverse * (grad_scaled - scaled * projected)
    gain_term = jnp.sum((grad_normed * scaled).reshape(-1, model_width), axis=0)
    gain_grad = lax.psum(gain_term, ("tp", "dp"))
    gate_grad, up_grad, down_grad = (
        lax.psum_scatter(gate_term.astype(jnp.bfloat16), "dp", scatter_dimension=0, tiled=True),
        lax.psum_scatter(up_term.astype(jnp.bfloat16), "dp", scatter_dimension=0, tiled=True),
        lax.psum_scatter(down_term.astype(jnp.bfloat16), "dp", scatter_dimension=1, tiled=True),
    )
    return (input_rows.astype(jnp.bfloat16)[None], gain_grad, gate_grad, up_grad, down_grad)


VMEM_SPEC = pl.BlockSpec(memory_space=pltpu.VMEM)
ANY_SPEC = pl.BlockSpec(memory_space=pl.ANY)


def exchange(value, axis, bits):
    count = lax.axis_size(axis)
    return lax.ppermute(value, axis, [(i, i ^ bits) for i in range(count)])


def high_part(value):
    return value.astype(jnp.bfloat16)


def low_part(value):
    return (value - value.astype(jnp.bfloat16).astype(jnp.float32)).astype(jnp.bfloat16)


def join_kernel(first_ref, second_ref, out_ref, held):
    count = first_ref.shape[0]
    held[:count, :] = first_ref[...].astype(jnp.float32)
    held[count:, :] = second_ref[...].astype(jnp.float32)
    out_ref[...] = held[...].astype(jnp.bfloat16)


def sort_kernel(rows, first_ref, second_ref, out_ref, held):
    pieces = first_ref.shape[0] // (2 * rows)
    for half, ref in enumerate((first_ref, second_ref)):
        value = ref[...].astype(jnp.float32)
        for k in range(pieces):
            at = rows * (pieces * half + k)
            held[at : at + rows, :] = value[2 * rows * k : 2 * rows * k + rows]
            at += 2 * rows * pieces
            held[at : at + rows, :] = value[2 * rows * k + rows : 2 * rows * (k + 1)]
    out_ref[...] = held[...].astype(jnp.bfloat16)


def stack_rows(kernel, first, second, name):
    shape = (2 * first.shape[0], first.shape[1])
    return pl.pallas_call(
        kernel,
        out_shape=jax.ShapeDtypeStruct(shape, jnp.bfloat16),
        in_specs=[VMEM_SPEC] * 2,
        out_specs=VMEM_SPEC,
        scratch_shapes=[pltpu.VMEM(shape, jnp.float32)],
        compiler_params=pltpu.CompilerParams(vmem_limit_bytes=8 * MIB),
        name=name,
    )(first, second)


def hidden_kernel(
    chunks, own_ref, peer_ref, gain_hbm, gate_hbm, up_hbm, down_hbm,
    packed_ref, mine_ref, theirs_ref, gain_part_ref, rows_ref,
    gate_buf, up_buf, down_buf, x_buf, c_buf, inverse_buf, acc_g, acc_u, acc_h, left_buf, gain_ref,
    sems, gain_sem,
):
    half = acc_g.shape[0]
    toks = x_buf.shape[1]
    each = toks // 2
    width = x_buf.shape[2]
    first = pl.multiple_of(lax.axis_index("dp") * half, 16)
    weights = ((gate_hbm, gate_buf), (up_hbm, up_buf), (down_hbm, down_buf))

    def fetch(c, w):
        source, target = weights[w]
        at = pl.ds(pl.multiple_of(c * width, LANES), width)
        return pltpu.make_async_copy(
            source.at[pl.ds(first, half), at], target.at[c], sems.at[w, c]
        )

    gain_copy = pltpu.make_async_copy(gain_hbm, gain_ref, gain_sem)
    gain_copy.start()
    for c in range(chunks):
        for w in range(3):
            fetch(c, w).start()

    squares = jnp.zeros((toks, 1), jnp.float32)
    for c in range(chunks):
        at = slice(c * width, (c + 1) * width)
        value = jnp.concatenate([own_ref[:each, at], peer_ref[:each, at]], axis=0)
        value = value.astype(jnp.float32)
        squares = squares + jnp.sum(value * value, axis=-1, keepdims=True)
    inverse = lax.rsqrt(squares / (chunks * width) + EPSILON)
    inverse_buf[...] = jnp.broadcast_to(inverse, inverse_buf.shape)
    gain_copy.wait()
    for c in range(chunks):
        at = slice(c * width, (c + 1) * width)
        value = jnp.concatenate([own_ref[:each, at], peer_ref[:each, at]], axis=0)
        normed = (value.astype(jnp.float32) * inverse * gain_ref[:, at]).astype(jnp.bfloat16)
        incoming = jnp.concatenate([own_ref[each:, at], peer_ref[each:, at]], axis=0)
        x_buf[c] = normed
        c_buf[c] = incoming
        rows_ref[:toks, at] = normed
        rows_ref[toks:, at] = incoming
    acc_g[...] = jnp.zeros_like(acc_g)
    acc_u[...] = jnp.zeros_like(acc_u)
    acc_h[...] = jnp.zeros_like(acc_h)

    def forward(c, carry):
        for w in range(3):
            fetch(c, w).wait()
        acc_g[...] += contract(gate_buf[c], x_buf[c], 1, 1)
        acc_u[...] += contract(up_buf[c], x_buf[c], 1, 1)
        acc_h[...] += contract(down_buf[c], c_buf[c], 1, 1)
        return carry

    lax.fori_loop(0, chunks, forward, 0)

    step = 80 if half % 80 == 0 else 16

    def pointwise(i, carry):
        at = pl.ds(pl.multiple_of(i * step, 16), step)
        gate, up, grad = acc_g[at, :], acc_u[at, :], acc_h[at, :]
        sigmoid = jax.nn.sigmoid(gate)
        active = gate * sigmoid
        grad_gate = grad * up * sigmoid * (1.0 + gate * (1.0 - sigmoid))
        parts = [grad_gate, grad * active, active * up, jnp.zeros_like(active)]
        packed_ref[at, :] = jnp.concatenate(parts, axis=1).astype(jnp.bfloat16)
        return carry

    lax.fori_loop(0, half // step, pointwise, 0)
    left_buf[...] = packed_ref[...].astype(jnp.float32).T.astype(jnp.bfloat16)

    def backward(c, carry):
        at = pl.ds(pl.multiple_of(c * width, LANES), width)
        part = jnp.dot(left_buf[:toks, :], gate_buf[c], preferred_element_type=jnp.float32)
        part += jnp.dot(
            left_buf[toks : 2 * toks, :], up_buf[c], preferred_element_type=jnp.float32
        )
        value = jnp.concatenate([own_ref[:each, at], peer_ref[:each, at]], axis=0)
        scaled = value.astype(jnp.float32) * inverse_buf[:, :1]
        gain = jnp.sum(part * scaled, axis=0, keepdims=True)
        gain_part_ref[:, at] = gain
        mine_ref[:, at] = part[:each]
        theirs_ref[:each, at] = part[each:].astype(jnp.bfloat16)
        theirs_ref[each : each + 1, at] = high_part(gain)
        theirs_ref[each + 1 : each + 2, at] = low_part(gain)
        return carry

    lax.fori_loop(0, chunks, backward, 0)


def hidden_pass(own, peer, gain, gate_t, up_t, down):
    ffw, model = down.shape
    half, toks = ffw // 2, own.shape[0]
    each = toks // 2
    chunks = model // 512
    width = model // chunks
    big = pltpu.VMEM((chunks, half, width), jnp.bfloat16)
    small = pltpu.VMEM((chunks, toks, width), jnp.bfloat16)
    acc = pltpu.VMEM((half, toks), jnp.float32)
    return pl.pallas_call(
        functools.partial(hidden_kernel, chunks),
        out_shape=(
            jax.ShapeDtypeStruct((half, LANES), jnp.bfloat16),
            jax.ShapeDtypeStruct((each, model), jnp.float32),
            jax.ShapeDtypeStruct((each + 2, model), jnp.bfloat16),
            jax.ShapeDtypeStruct((1, model), jnp.float32),
            jax.ShapeDtypeStruct((2 * toks, model), jnp.bfloat16),
        ),
        in_specs=[VMEM_SPEC] * 2 + [ANY_SPEC] * 4,
        out_specs=(VMEM_SPEC,) * 5,
        scratch_shapes=[
            big, big, big, small, small,
            pltpu.VMEM((toks, LANES), jnp.float32),
            acc, acc, acc,
            pltpu.VMEM((LANES, half), jnp.bfloat16),
            pltpu.VMEM((1, model), jnp.float32),
            pltpu.SemaphoreType.DMA((3, chunks)),
            pltpu.SemaphoreType.DMA(()),
        ],
        compiler_params=pltpu.CompilerParams(vmem_limit_bytes=48 * MIB),
        cost_estimate=pl.CostEstimate(
            flops=10 * toks * half * model, bytes_accessed=6 * half * model, transcendentals=half * toks
        ),
        name="hidden_pass",
    )(own, peer, gain, gate_t, up_t, down)


def weight_kernel(toks, swapped, first, place_ref, packed_ref, rows_ref, *refs):
    outs, written_ref = refs[-4:-1], refs[-1]
    width = outs[0].shape[1]
    each = toks // 2
    written_ref[...] = jnp.zeros_like(written_ref)
    own_width = rows_ref.shape[1] // 2
    start = place_ref[0] * own_width + (first + pl.program_id(0)) * width
    at = pl.ds(pl.multiple_of(start, LANES), width)
    normed, incoming = rows_ref[:toks, at], rows_ref[toks:, at]
    if swapped:
        normed = jnp.concatenate([normed[each:], normed[:each]], axis=0)
        incoming = jnp.concatenate([incoming[each:], incoming[:each]], axis=0)
    for k, right in enumerate((normed, normed, incoming)):
        left = packed_ref[:, k * toks : (k + 1) * toks]
        outs[k][...] = jnp.dot(left, right, preferred_element_type=jnp.float32).astype(jnp.bfloat16)


def weight_pass(place, packed, rows, ffw, swapped, part, parts, before=(), after=()):
    half, toks, model = packed.shape[0], rows.shape[0] // 2, rows.shape[1]
    own_width = model // 2
    width = 256
    steps = own_width // width // parts
    first = part * steps
    row = (lambda place: 1 - place[0]) if swapped else (lambda place: place[0])
    out = jax.ShapeDtypeStruct((ffw, own_width), jnp.bfloat16)
    return pl.pallas_call(
        functools.partial(weight_kernel, toks, swapped, first),
        out_shape=(out,) * 3 + (jax.ShapeDtypeStruct((8, LANES), jnp.float32),),
        grid_spec=pltpu.PrefetchScalarGridSpec(
            num_scalar_prefetch=1,
            grid=(steps,),
            in_specs=[VMEM_SPEC] * 2 + [ANY_SPEC] * (len(before) + len(after)),
            out_specs=(pl.BlockSpec((half, width), lambda j, place: (row(place), first + j)),) * 3
            + (pl.BlockSpec((8, LANES), lambda j, place: (0, 0)),),
        ),
        input_output_aliases={3 + i: i for i in range(len(before))},
        compiler_params=pltpu.CompilerParams(vmem_limit_bytes=16 * MIB),
        cost_estimate=pl.CostEstimate(
            flops=6 * toks * half * own_width // parts,
            bytes_accessed=6 * half * own_width // parts,
            transcendentals=0,
        ),
        name="weight_pass",
    )(place, packed, rows, *before, *after)


def fold_kernel(kept_ref, gain_ref, arrived_ref, _, keep_ref, gain_out_ref, send_ref, held):
    count = kept_ref.shape[0]
    arrived = arrived_ref[...].astype(jnp.float32)
    gain = gain_ref[...] + (arrived[count : count + 1] + arrived[count + 1 : count + 2])
    held[...] = kept_ref[...] + arrived[:count]
    keep_ref[...] = held[: count // 2, :]
    gain_out_ref[...] = gain
    send_ref[: count // 2, :] = held[count // 2 :, :].astype(jnp.bfloat16)
    send_ref[count // 2 : count // 2 + 1, :] = high_part(gain)
    send_ref[count // 2 + 1 :, :] = low_part(gain)


def fold(kept, gain, arrived, written):
    count, model = kept.shape
    return pl.pallas_call(
        fold_kernel,
        out_shape=(
            jax.ShapeDtypeStruct((count // 2, model), jnp.float32),
            jax.ShapeDtypeStruct((1, model), jnp.float32),
            jax.ShapeDtypeStruct((count // 2 + 2, model), jnp.bfloat16),
        ),
        in_specs=[VMEM_SPEC] * 3 + [ANY_SPEC],
        out_specs=(VMEM_SPEC,) * 3,
        scratch_shapes=[pltpu.VMEM((count, model), jnp.float32)],
        compiler_params=pltpu.CompilerParams(vmem_limit_bytes=8 * MIB),
        name="fold",
    )(kept, gain, arrived, written)


def finish_kernel(rows, tokens_ref, incoming_ref, norm_gain_ref, own_ref, gain_ref, *refs):
    pieces, input_ref, gain_out_ref = refs[:-2], refs[-2], refs[-1]
    grad_normed, gain = own_ref[...], gain_ref[...]
    for piece in pieces:
        value = piece[...].astype(jnp.float32)
        grad_normed = grad_normed + value[:rows]
        gain = gain + (value[rows : rows + 1] + value[rows + 1 : rows + 2])
    gain_out_ref[...] = gain
    values = tokens_ref[...].astype(jnp.float32)
    inverse = lax.rsqrt(jnp.mean(values * values, axis=-1, keepdims=True) + EPSILON)
    scaled = values * inverse
    grad_scaled = grad_normed * norm_gain_ref[...]
    projected = jnp.mean(grad_scaled * scaled, axis=-1, keepdims=True)
    result = incoming_ref[...].astype(jnp.float32) + inverse * (grad_scaled - scaled * projected)
    input_ref[...] = result.astype(jnp.bfloat16)


def finish(rows, tokens, incoming, norm_gain, own, gain, pieces):
    model = tokens.shape[1]
    return pl.pallas_call(
        functools.partial(finish_kernel, rows),
        out_shape=(
            jax.ShapeDtypeStruct((rows, model), jnp.bfloat16),
            jax.ShapeDtypeStruct((1, model), jnp.float32),
        ),
        in_specs=[VMEM_SPEC] * (5 + len(pieces)),
        out_specs=(VMEM_SPEC,) * 2,
        compiler_params=pltpu.CompilerParams(vmem_limit_bytes=8 * MIB),
        name="finish",
    )(tokens, incoming, norm_gain, own, gain, *pieces)


def small_body(tokens, norm_gain, gate_weight, up_weight, down_weight, cotangent):
    rows, model = tokens.shape[1] * tokens.shape[2], tokens.shape[3]
    ffw = down_weight.shape[0]
    tp_count = lax.axis_size("tp")
    place = lax.axis_index("dp").astype(jnp.int32).reshape(1)
    own_tokens, own_incoming = tokens.reshape(rows, model), cotangent.reshape(rows, model)
    gain_row = norm_gain.reshape(1, model)

    held = jnp.concatenate([own_tokens, own_incoming], axis=0)
    bits = tp_count // 2
    while bits:
        arrived = exchange(held, "tp", bits)
        bits //= 2
        kernel = join_kernel if bits else functools.partial(sort_kernel, rows)
        held = stack_rows(kernel, held, arrived, "join_rows" if bits else "sort_rows")
    peer = exchange(held, "dp", 1)
    packed, kept, send, gain, all_rows = hidden_pass(
        held, peer, gain_row, gate_weight.T, up_weight.T, down_weight
    )
    peer_packed = exchange(packed, "dp", 1)
    arrived = exchange(send, "dp", 1)
    *grads, written = weight_pass(place, packed, all_rows, ffw, False, 0, 2)
    bits, part = 1, 1
    while bits < tp_count:
        kept, gain, send = fold(kept, gain, arrived, written)
        arrived = exchange(send, "tp", bits)
        source = packed if part < 2 else peer_packed
        *grads, written = weight_pass(
            place, source, all_rows, ffw, part >= 2, part % 2, 2, grads, (send,)
        )
        bits, part = bits * 2, part + 1
    gate_t, up_t, down_grad = grads
    input_rows, gain_grad = finish(
        rows, own_tokens, own_incoming, gain_row, kept, gain, [arrived]
    )
    return (
        input_rows.reshape(tokens.shape),
        gain_grad.reshape(model),
        gate_t.T,
        up_t.T,
        down_grad,
    )


def body(tokens, norm_gain, gate_weight, up_weight, down_weight, cotangent):
    tp_count, dp_count = lax.axis_size("tp"), lax.axis_size("dp")
    ffw, model = down_weight.shape
    toks = tokens.shape[1] * tokens.shape[2] * tp_count * dp_count
    small = (
        dp_count == 2
        and tp_count == 8
        and toks == 32
        and model % 1024 == 0
        and ffw % 32 == 0
        and 3 * ffw * model <= 40 * MIB
    )
    chosen = small_body if small else general_body
    return chosen(tokens, norm_gain, gate_weight, up_weight, down_weight, cotangent)


def solution(mesh):
    placed = (
        P(("groups", "dp"), None, "tp", None),
        P(),
        P(None, "tp"),
        P(None, "tp"),
        P("tp", None),
        P(("groups", "dp"), None, "tp", None),
    )
    return jax.shard_map(
        body,
        mesh=mesh,
        in_specs=placed,
        out_specs=(
            P(("groups", "dp"), None, "tp", None),
            P("groups"),
            P(("groups", "dp"), "tp"),
            P(("groups", "dp"), "tp"),
            P("tp", ("groups", "dp")),
        ),
        check_vma=False,
    )
```

```python
import functools

import jax
import jax.numpy as jnp
from jax import lax
from jax.experimental import pallas as pl
from jax.experimental.pallas import tpu as pltpu
from jax.sharding import PartitionSpec as P

EPSILON = 1e-06
LANES = 128
MIB = 1 << 20
CHUNK = 512
BLOCK = 256
ALONG_Z = (2, 4, 6)


def contract(left, right, left_dim, right_dim):
    return lax.dot_general(
        left, right, (((left_dim,), (right_dim,)), ((), ())), preferred_element_type=jnp.float32
    )


def norm_tokens(values_in, norm_gain):
    values = values_in.astype(jnp.float32)
    inverse = lax.rsqrt(jnp.mean(values * values, axis=-1, keepdims=True) + EPSILON)
    scaled = values * inverse
    return (scaled, inverse, (scaled * norm_gain).astype(jnp.bfloat16))


def local_pass(normed_all, grads_all, gate_weight, up_weight, down_weight):
    gate_value = jnp.dot(normed_all, gate_weight, preferred_element_type=jnp.float32)
    up_value = jnp.dot(normed_all, up_weight, preferred_element_type=jnp.float32)
    sigmoid_gate = jax.nn.sigmoid(gate_value)
    active = gate_value * sigmoid_gate
    hidden = (active * up_value).astype(jnp.bfloat16)
    grad_hidden = contract(grads_all, down_weight, 1, 1)
    grad_gate = (
        grad_hidden * up_value * sigmoid_gate * (1.0 + gate_value * (1.0 - sigmoid_gate))
    ).astype(jnp.bfloat16)
    grad_up = (grad_hidden * active).astype(jnp.bfloat16)
    partial_value = contract(grad_gate, gate_weight, 1, 1) + contract(grad_up, up_weight, 1, 1)
    gate_term = contract(normed_all, grad_gate, 0, 0)
    up_term = contract(normed_all, grad_up, 0, 0)
    down_term = contract(hidden, grads_all, 0, 0)
    return (partial_value, gate_term, up_term, down_term)


def general_body(tokens, norm_gain, gate_weight, up_weight, down_weight, cotangent):
    micro_count, own_tokens, model_width = (tokens.shape[1], tokens.shape[2], tokens.shape[3])
    tp_count = lax.axis_size("tp")
    scaled, inverse, normed = norm_tokens(tokens[0], norm_gain)
    normed_all, grads_all = (
        lax.all_gather(normed, "tp", axis=1, tiled=True),
        lax.all_gather(cotangent[0], "tp", axis=1, tiled=True),
    )
    partial_value, gate_term, up_term, down_term = local_pass(
        normed_all.reshape(-1, model_width),
        grads_all.reshape(-1, model_width),
        gate_weight,
        up_weight,
        down_weight,
    )
    pieces = lax.all_to_all(
        partial_value.reshape(micro_count, tp_count, own_tokens, model_width),
        "tp",
        split_axis=1,
        concat_axis=1,
        tiled=True,
    )
    grad_normed = jnp.sum(pieces, axis=1)
    grad_scaled = grad_normed * norm_gain
    projected = jnp.mean(grad_scaled * scaled, axis=-1, keepdims=True)
    input_rows = cotangent[0].astype(jnp.float32) + inverse * (grad_scaled - scaled * projected)
    gain_term = jnp.sum((grad_normed * scaled).reshape(-1, model_width), axis=0)
    gain_grad = lax.psum(gain_term, ("tp", "dp"))
    gate_grad, up_grad, down_grad = (
        lax.psum_scatter(gate_term.astype(jnp.bfloat16), "dp", scatter_dimension=0, tiled=True),
        lax.psum_scatter(up_term.astype(jnp.bfloat16), "dp", scatter_dimension=0, tiled=True),
        lax.psum_scatter(down_term.astype(jnp.bfloat16), "dp", scatter_dimension=1, tiled=True),
    )
    return (input_rows.astype(jnp.bfloat16)[None], gain_grad, gate_grad, up_grad, down_grad)


VMEM_SPEC = pl.BlockSpec(memory_space=pltpu.VMEM)
ANY_SPEC = pl.BlockSpec(memory_space=pl.ANY)


def exchange(value, axis, bits):
    count = lax.axis_size(axis)
    return lax.ppermute(value, axis, [(i, i ^ bits) for i in range(count)])


def high_part(value):
    return value.astype(jnp.bfloat16)


def low_part(value):
    return (value - value.astype(jnp.bfloat16).astype(jnp.float32)).astype(jnp.bfloat16)


def relay_kernel(*refs):
    count = len(refs) // 2
    for source, target in zip(refs[:count], refs[count + 1 :]):
        target[...] = source[...]


def relay(pieces, fetched):
    return pl.pallas_call(
        relay_kernel,
        out_shape=tuple(jax.ShapeDtypeStruct(piece.shape, piece.dtype) for piece in pieces),
        in_specs=[VMEM_SPEC] * len(pieces) + [ANY_SPEC],
        out_specs=(VMEM_SPEC,) * len(pieces),
        compiler_params=pltpu.CompilerParams(vmem_limit_bytes=4 * MIB),
        name="relay",
    )(*pieces, fetched)


def sort_kernel(rows, *refs):
    pieces, out_ref, held = refs[:-3], refs[-2], refs[-1]
    count = len(pieces)
    for k, piece in enumerate(pieces):
        value = piece[...].astype(jnp.float32)
        held[rows * k : rows * (k + 1), :] = value[:rows]
        held[rows * (count + k) : rows * (count + k + 1), :] = value[rows:]
    out_ref[...] = held[...].astype(jnp.bfloat16)


def sort_rows(rows, pieces, fetched):
    shape = (2 * rows * len(pieces), pieces[0].shape[1])
    return pl.pallas_call(
        functools.partial(sort_kernel, rows),
        out_shape=jax.ShapeDtypeStruct(shape, jnp.bfloat16),
        in_specs=[VMEM_SPEC] * len(pieces) + [ANY_SPEC],
        out_specs=VMEM_SPEC,
        scratch_shapes=[pltpu.VMEM(shape, jnp.float32)],
        compiler_params=pltpu.CompilerParams(vmem_limit_bytes=8 * MIB),
        name="sort_rows",
    )(*pieces, fetched)


def fetch_kernel(first, *refs):
    sources, gain_hbm = refs[:3], refs[3]
    targets, gain_ref, done_ref, sems, gain_sem = refs[-7:-4], *refs[-4:]
    chunks, half, width = targets[0].shape
    top = pl.multiple_of(lax.axis_index("dp") * half, 16)
    copies = [pltpu.make_async_copy(gain_hbm, gain_ref, gain_sem)]
    for c in range(chunks):
        at = slice((first + c) * width, (first + c + 1) * width)
        for w, (source, target) in enumerate(zip(sources, targets)):
            block = source.at[pl.ds(top, half), at]
            copies.append(pltpu.make_async_copy(block, target.at[c], sems.at[w, c]))
    for copy in copies:
        copy.start()
    done_ref[...] = jnp.zeros_like(done_ref)
    for copy in copies:
        copy.wait()


def fetch_weights(weights, gain, first, chunks, width, after=()):
    ffw = weights[0].shape[0]
    fixed = [pltpu.with_memory_space_constraint(x, pltpu.HBM) for x in (*weights, gain)]
    *fetched, gain, done = pl.pallas_call(
        functools.partial(fetch_kernel, first),
        out_shape=(pltpu.VMEM((chunks, ffw // 2, width), jnp.bfloat16),) * 3
        + (pltpu.VMEM(gain.shape, gain.dtype), pltpu.VMEM((8, LANES), jnp.float32)),
        in_specs=[ANY_SPEC] * (4 + len(after)),
        out_specs=(VMEM_SPEC,) * 5,
        scratch_shapes=[pltpu.SemaphoreType.DMA((3, chunks)), pltpu.SemaphoreType.DMA(())],
        compiler_params=pltpu.CompilerParams(vmem_limit_bytes=4 * MIB),
        cost_estimate=pl.CostEstimate(
            flops=0, bytes_accessed=3 * ffw * chunks * width, transcendentals=0
        ),
        name="fetch_weights",
    )(*fixed, *after)
    return fetched, gain, done


def hidden_kernel(
    parts, own_ref, peer_ref, gain_ref, *refs
):
    weights, refs = refs[: 3 * parts], refs[3 * parts :]
    (packed_ref, mine_ref, theirs_ref, gain_part_ref, rows_ref,
     x_buf, c_buf, inverse_buf, acc_g, acc_u, acc_h, left_buf) = refs
    half = acc_g.shape[0]
    chunks, toks, width = x_buf.shape
    each = toks // 2
    part_chunks = chunks // parts

    squares = jnp.zeros((toks, 1), jnp.float32)
    for c in range(chunks):
        at = slice(c * width, (c + 1) * width)
        value = jnp.concatenate([own_ref[:each, at], peer_ref[:each, at]], axis=0)
        value = value.astype(jnp.float32)
        squares = squares + jnp.sum(value * value, axis=-1, keepdims=True)
    inverse = lax.rsqrt(squares / (chunks * width) + EPSILON)
    inverse_buf[...] = jnp.broadcast_to(inverse, inverse_buf.shape)
    for c in range(chunks):
        at = slice(c * width, (c + 1) * width)
        value = jnp.concatenate([own_ref[:each, at], peer_ref[:each, at]], axis=0)
        normed = (value.astype(jnp.float32) * inverse * gain_ref[:, at]).astype(jnp.bfloat16)
        incoming = jnp.concatenate([own_ref[each:, at], peer_ref[each:, at]], axis=0)
        x_buf[c] = normed
        c_buf[c] = incoming
        rows_ref[:toks, at] = normed
        rows_ref[toks:, at] = incoming
    acc_g[...] = jnp.zeros_like(acc_g)
    acc_u[...] = jnp.zeros_like(acc_u)
    acc_h[...] = jnp.zeros_like(acc_h)

    for part in range(parts):
        gate_buf, up_buf, down_buf = weights[3 * part : 3 * part + 3]

        def forward(c, carry):
            at = part * part_chunks + c
            acc_g[...] += contract(gate_buf[c], x_buf[at], 1, 1)
            acc_u[...] += contract(up_buf[c], x_buf[at], 1, 1)
            acc_h[...] += contract(down_buf[c], c_buf[at], 1, 1)
            return carry

        lax.fori_loop(0, part_chunks, forward, 0)

    step = 80 if half % 80 == 0 else 16

    def pointwise(i, carry):
        at = pl.ds(pl.multiple_of(i * step, 16), step)
        gate, up, grad = acc_g[at, :], acc_u[at, :], acc_h[at, :]
        sigmoid = jax.nn.sigmoid(gate)
        active = gate * sigmoid
        grad_gate = grad * up * sigmoid * (1.0 + gate * (1.0 - sigmoid))
        parts = [grad_gate, grad * active, active * up, jnp.zeros_like(active)]
        packed_ref[at, :] = jnp.concatenate(parts, axis=1).astype(jnp.bfloat16)
        return carry

    lax.fori_loop(0, half // step, pointwise, 0)
    left_buf[...] = packed_ref[...].astype(jnp.float32).T.astype(jnp.bfloat16)

    for part in range(parts):
        gate_buf, up_buf = weights[3 * part : 3 * part + 2]

        def backward(c, carry):
            at = pl.ds(pl.multiple_of((part * part_chunks + c) * width, LANES), width)
            total = jnp.dot(left_buf[:toks, :], gate_buf[c], preferred_element_type=jnp.float32)
            total += jnp.dot(
                left_buf[toks : 2 * toks, :], up_buf[c], preferred_element_type=jnp.float32
            )
            value = jnp.concatenate([own_ref[:each, at], peer_ref[:each, at]], axis=0)
            scaled = value.astype(jnp.float32) * inverse_buf[:, :1]
            gain = jnp.sum(total * scaled, axis=0, keepdims=True)
            gain_part_ref[:, at] = gain
            mine_ref[:, at] = total[:each]
            theirs_ref[:each, at] = total[each:].astype(jnp.bfloat16)
            theirs_ref[each : each + 1, at] = high_part(gain)
            theirs_ref[each + 1 : each + 2, at] = low_part(gain)
            return carry

        lax.fori_loop(0, part_chunks, backward, 0)


def hidden_pass(own, peer, gain, fetched):
    toks, model = own.shape
    each, parts = toks // 2, len(fetched)
    part_chunks, half, width = fetched[0][0].shape
    small = pltpu.VMEM((parts * part_chunks, toks, width), jnp.bfloat16)
    acc = pltpu.VMEM((half, toks), jnp.float32)
    weights = [pltpu.with_memory_space_constraint(w, pltpu.VMEM) for part in fetched for w in part]
    return pl.pallas_call(
        functools.partial(hidden_kernel, parts),
        out_shape=(
            jax.ShapeDtypeStruct((half, LANES), jnp.bfloat16),
            jax.ShapeDtypeStruct((each, model), jnp.float32),
            jax.ShapeDtypeStruct((each + 2, model), jnp.bfloat16),
            jax.ShapeDtypeStruct((1, model), jnp.float32),
            jax.ShapeDtypeStruct((2 * toks, model), jnp.bfloat16),
        ),
        in_specs=[VMEM_SPEC] * (3 + len(weights)),
        out_specs=(VMEM_SPEC,) * 5,
        scratch_shapes=[
            small, small, pltpu.VMEM((toks, LANES), jnp.float32), acc, acc, acc,
            pltpu.VMEM((LANES, half), jnp.bfloat16),
        ],
        compiler_params=pltpu.CompilerParams(vmem_limit_bytes=16 * MIB),
        cost_estimate=pl.CostEstimate(
            flops=10 * toks * half * model, bytes_accessed=6 * half * model, transcendentals=half * toks
        ),
        name="hidden_pass",
    )(own, peer, gain, *weights)


def weight_kernel(toks, spans, packs, *refs):
    rows_ref, refs = refs[packs], refs[:packs] + refs[packs + 1 :]
    outs, written_ref, buf, sems = refs[-6:-3], refs[-3], refs[-2], refs[-1]
    slots, _, half, width = buf.shape
    each = toks // 2
    place = lax.axis_index("dp")
    own_width = rows_ref.shape[1] // 2
    written_ref[...] = jnp.zeros_like(written_ref)

    def copy(k, slot, row, block):
        at = pl.ds(pl.multiple_of(block * width, LANES), width)
        target = outs[k].at[pl.ds(pl.multiple_of(row, 16), half), at]
        return pltpu.make_async_copy(buf.at[slot, k], target, sems.at[slot, k])

    done = 0
    for packed_ref, (swapped, first, last) in zip(refs[:packs], spans):
        row = (1 - place) * half if swapped else place * half

        def step(i, carry, packed_ref=packed_ref, swapped=swapped, row=row, base=done - first):
            slot = lax.rem(base + i, slots)

            @pl.when(base + i >= slots)
            def _():
                for k in range(3):
                    copy(k, slot, row, i).wait()

            at = pl.ds(pl.multiple_of(place * own_width + i * width, LANES), width)
            normed, incoming = rows_ref[:toks, at], rows_ref[toks:, at]
            if swapped:
                normed = jnp.concatenate([normed[each:], normed[:each]], axis=0)
                incoming = jnp.concatenate([incoming[each:], incoming[:each]], axis=0)
            for k, right in enumerate((normed, normed, incoming)):
                left = packed_ref[:, k * toks : (k + 1) * toks]
                value = jnp.dot(left, right, preferred_element_type=jnp.float32)
                buf[slot, k] = value.astype(jnp.bfloat16)
                copy(k, slot, row, i).start()
            return carry

        lax.fori_loop(first, last, step, 0)
        done += last - first
    for slot in range(min(slots, done)):
        for k in range(3):
            copy(k, slot, place * half, 0).wait()


def weight_pass(packs, rows, ffw, spans, before=(), after=()):
    half, toks, model = packs[0].shape[0], rows.shape[0] // 2, rows.shape[1]
    own_width = model // 2
    blocks = sum(last - first for _, first, last in spans)
    out = jax.ShapeDtypeStruct((ffw, own_width), jnp.bfloat16)
    return pl.pallas_call(
        functools.partial(weight_kernel, toks, spans, len(packs)),
        out_shape=(out,) * 3 + (jax.ShapeDtypeStruct((8, LANES), jnp.float32),),
        in_specs=[VMEM_SPEC] * (len(packs) + 1) + [ANY_SPEC] * (len(before) + len(after)),
        out_specs=(ANY_SPEC,) * 3 + (VMEM_SPEC,),
        scratch_shapes=[
            pltpu.VMEM((3, 3, half, BLOCK), jnp.bfloat16),
            pltpu.SemaphoreType.DMA((3, 3)),
        ],
        input_output_aliases={len(packs) + 1 + i: i for i in range(len(before))},
        compiler_params=pltpu.CompilerParams(vmem_limit_bytes=16 * MIB),
        cost_estimate=pl.CostEstimate(
            flops=6 * toks * half * BLOCK * blocks,
            bytes_accessed=6 * half * BLOCK * blocks,
            transcendentals=0,
        ),
        name="weight_pass",
    )(*packs, rows, *before, *after)


def add_arrived(kept_ref, gain_ref, arrived, extra, held, gain_out_ref):
    gain = gain_ref[...] + (extra[0:1] + extra[1:2])
    held[...] = kept_ref[...] + arrived
    gain_out_ref[...] = gain
    return gain


def fold_kernel(
    kept_ref, gain_ref, arrived_ref, _, keep_ref, gain_out_ref, send_ref, send_gain_ref, held
):
    count = kept_ref.shape[0]
    arrived = arrived_ref[...].astype(jnp.float32)
    gain = add_arrived(kept_ref, gain_ref, arrived[:count], arrived[count:], held, gain_out_ref)
    keep_ref[...] = held[: count // 2, :]
    send_ref[...] = held[count // 2 :, :].astype(jnp.bfloat16)
    send_gain_ref[:1, :] = high_part(gain)
    send_gain_ref[1:, :] = low_part(gain)


def spread_kernel(rows, kept_ref, gain_ref, arrived_ref, extra_ref, _, own_ref, gain_out_ref, *refs):
    outs, held = refs[:-1], refs[-1]
    arrived, extra = arrived_ref[...].astype(jnp.float32), extra_ref[...].astype(jnp.float32)
    gain = add_arrived(kept_ref, gain_ref, arrived, extra, held, gain_out_ref)
    own_ref[...] = held[:rows, :]
    for k, out in enumerate(outs):
        out[:rows, :] = held[rows * (k + 1) : rows * (k + 2), :].astype(jnp.bfloat16)
        out[rows : rows + 1, :] = high_part(gain)
        out[rows + 1 :, :] = low_part(gain)


def add_rows(kernel, kept, gain, arrived, written, kept_rows, sent_rows, name):
    count, model = kept.shape
    return pl.pallas_call(
        kernel,
        out_shape=(
            jax.ShapeDtypeStruct((kept_rows, model), jnp.float32),
            jax.ShapeDtypeStruct((1, model), jnp.float32),
        )
        + tuple(jax.ShapeDtypeStruct((n, model), jnp.bfloat16) for n in sent_rows),
        in_specs=[VMEM_SPEC] * (2 + len(arrived)) + [ANY_SPEC],
        out_specs=(VMEM_SPEC,) * (2 + len(sent_rows)),
        scratch_shapes=[pltpu.VMEM((count, model), jnp.float32)],
        compiler_params=pltpu.CompilerParams(vmem_limit_bytes=8 * MIB),
        name=name,
    )(kept, gain, *arrived, written)


def finish_kernel(rows, tokens_ref, incoming_ref, norm_gain_ref, own_ref, gain_ref, *refs):
    pieces, input_ref, gain_out_ref = refs[:-2], refs[-2], refs[-1]
    grad_normed, gain = own_ref[...], gain_ref[...]
    for piece in pieces:
        value = piece[...].astype(jnp.float32)
        grad_normed = grad_normed + value[:rows]
        gain = gain + (value[rows : rows + 1] + value[rows + 1 : rows + 2])
    gain_out_ref[...] = gain
    values = tokens_ref[...].astype(jnp.float32)
    inverse = lax.rsqrt(jnp.mean(values * values, axis=-1, keepdims=True) + EPSILON)
    scaled = values * inverse
    grad_scaled = grad_normed * norm_gain_ref[...]
    projected = jnp.mean(grad_scaled * scaled, axis=-1, keepdims=True)
    result = incoming_ref[...].astype(jnp.float32) + inverse * (grad_scaled - scaled * projected)
    input_ref[...] = result.astype(jnp.bfloat16)


def finish(rows, tokens, incoming, norm_gain, own, gain, pieces):
    model = tokens.shape[1]
    return pl.pallas_call(
        functools.partial(finish_kernel, rows),
        out_shape=(
            jax.ShapeDtypeStruct((rows, model), jnp.bfloat16),
            jax.ShapeDtypeStruct((1, model), jnp.float32),
        ),
        in_specs=[VMEM_SPEC] * (5 + len(pieces)),
        out_specs=(VMEM_SPEC,) * 2,
        compiler_params=pltpu.CompilerParams(vmem_limit_bytes=8 * MIB),
        name="finish",
    )(tokens, incoming, norm_gain, own, gain, *pieces)


def small_body(tokens, norm_gain, gate_weight, up_weight, down_weight, cotangent):
    rows, model = tokens.shape[1] * tokens.shape[2], tokens.shape[3]
    ffw = down_weight.shape[0]
    tp_count = lax.axis_size("tp")
    own_tokens, own_incoming = tokens.reshape(rows, model), cotangent.reshape(rows, model)
    gain_hbm = norm_gain.reshape(1, model)

    weights = (gate_weight.T, up_weight.T, down_weight)
    chunks = model // CHUNK
    piece = jnp.concatenate([own_tokens, own_incoming], axis=0)
    near = exchange(piece, "tp", 1)
    along = [exchange(piece, "tp", bits) for bits in ALONG_Z]
    fetched, gain_row, done = fetch_weights(weights, gain_hbm, 0, chunks // 2, CHUNK, (piece,))
    along = relay(along, done)
    across = [exchange(arrived, "tp", 1) for arrived in along]
    more, _, done = fetch_weights(
        weights, gain_hbm, chunks // 2, chunks - chunks // 2, CHUNK, (along[0],)
    )
    fetched = [fetched, more]
    own = sort_rows(rows, [piece, *along, near, *across], done)
    peer = exchange(own, "dp", 1)
    packed, kept, send, gain, all_rows = hidden_pass(own, peer, gain_row, fetched)
    arrived = exchange(send, "dp", 1)
    peer_packed = exchange(packed, "dp", 1)
    blocks = model // 2 // BLOCK
    cut = blocks // 2
    *grads, written = weight_pass([packed], all_rows, ffw, [(False, 0, cut)])
    kept, gain, send, send_gain = add_rows(
        fold_kernel, kept, gain, [arrived], written, kept.shape[0] // 2, (kept.shape[0] // 2, 2), "fold"
    )
    arrived = [exchange(send, "tp", 1), exchange(send_gain, "tp", 1)]
    *grads, written = weight_pass(
        [packed, peer_packed], all_rows, ffw, [(False, cut, blocks), (True, 0, 2)], grads, (send,)
    )
    kept, gain, *sends = add_rows(
        functools.partial(spread_kernel, rows), kept, gain, arrived, written, rows, (rows + 2,) * 3,
        "spread",
    )
    arrived = [exchange(send, "tp", bits) for send, bits in zip(sends, ALONG_Z)]
    gate_t, up_t, down_grad, _ = weight_pass(
        [peer_packed], all_rows, ffw, [(True, 2, blocks)], grads, (sends[0],)
    )
    input_rows, gain_grad = finish(
        rows, own_tokens, own_incoming, gain_row, kept, gain, arrived
    )
    return (
        input_rows.reshape(tokens.shape),
        gain_grad.reshape(model),
        gate_t.T,
        up_t.T,
        down_grad,
    )


def body(tokens, norm_gain, gate_weight, up_weight, down_weight, cotangent):
    tp_count, dp_count = lax.axis_size("tp"), lax.axis_size("dp")
    ffw, model = down_weight.shape
    toks = tokens.shape[1] * tokens.shape[2] * tp_count * dp_count
    small = (
        dp_count == 2
        and tp_count == 8
        and toks == 32
        and model % 1024 == 0
        and ffw % 32 == 0
        and 3 * ffw * model <= 40 * MIB
    )
    chosen = small_body if small else general_body
    return chosen(tokens, norm_gain, gate_weight, up_weight, down_weight, cotangent)


def solution(mesh):
    placed = (
        P(("groups", "dp"), None, "tp", None),
        P(),
        P(None, "tp"),
        P(None, "tp"),
        P("tp", None),
        P(("groups", "dp"), None, "tp", None),
    )
    return jax.shard_map(
        body,
        mesh=mesh,
        in_specs=placed,
        out_specs=(
            P(("groups", "dp"), None, "tp", None),
            P("groups"),
            P(("groups", "dp"), "tp"),
            P(("groups", "dp"), "tp"),
            P("tp", ("groups", "dp")),
        ),
        check_vma=False,
    )
```

```python
import functools

import jax
import jax.numpy as jnp
from jax import lax
from jax.experimental import pallas as pl
from jax.experimental.pallas import tpu as pltpu
from jax.sharding import PartitionSpec as P

EPSILON = 1e-06
LANES = 128
MIB = 1 << 20
CHUNK = 512
ALONG_Z = (2, 4, 6)


def contract(left, right, left_dim, right_dim):
    return lax.dot_general(
        left, right, (((left_dim,), (right_dim,)), ((), ())), preferred_element_type=jnp.float32
    )


def norm_tokens(values_in, norm_gain):
    values = values_in.astype(jnp.float32)
    inverse = lax.rsqrt(jnp.mean(values * values, axis=-1, keepdims=True) + EPSILON)
    scaled = values * inverse
    return (scaled, inverse, (scaled * norm_gain).astype(jnp.bfloat16))


def local_pass(normed_all, grads_all, gate_weight, up_weight, down_weight):
    gate_value = jnp.dot(normed_all, gate_weight, preferred_element_type=jnp.float32)
    up_value = jnp.dot(normed_all, up_weight, preferred_element_type=jnp.float32)
    sigmoid_gate = jax.nn.sigmoid(gate_value)
    active = gate_value * sigmoid_gate
    hidden = (active * up_value).astype(jnp.bfloat16)
    grad_hidden = contract(grads_all, down_weight, 1, 1)
    grad_gate = (
        grad_hidden * up_value * sigmoid_gate * (1.0 + gate_value * (1.0 - sigmoid_gate))
    ).astype(jnp.bfloat16)
    grad_up = (grad_hidden * active).astype(jnp.bfloat16)
    partial_value = contract(grad_gate, gate_weight, 1, 1) + contract(grad_up, up_weight, 1, 1)
    gate_term = contract(normed_all, grad_gate, 0, 0)
    up_term = contract(normed_all, grad_up, 0, 0)
    down_term = contract(hidden, grads_all, 0, 0)
    return (partial_value, gate_term, up_term, down_term)


def general_body(tokens, norm_gain, gate_weight, up_weight, down_weight, cotangent):
    micro_count, own_tokens, model_width = (tokens.shape[1], tokens.shape[2], tokens.shape[3])
    tp_count = lax.axis_size("tp")
    scaled, inverse, normed = norm_tokens(tokens[0], norm_gain)
    normed_all, grads_all = (
        lax.all_gather(normed, "tp", axis=1, tiled=True),
        lax.all_gather(cotangent[0], "tp", axis=1, tiled=True),
    )
    partial_value, gate_term, up_term, down_term = local_pass(
        normed_all.reshape(-1, model_width),
        grads_all.reshape(-1, model_width),
        gate_weight,
        up_weight,
        down_weight,
    )
    pieces = lax.all_to_all(
        partial_value.reshape(micro_count, tp_count, own_tokens, model_width),
        "tp",
        split_axis=1,
        concat_axis=1,
        tiled=True,
    )
    grad_normed = jnp.sum(pieces, axis=1)
    grad_scaled = grad_normed * norm_gain
    projected = jnp.mean(grad_scaled * scaled, axis=-1, keepdims=True)
    input_rows = cotangent[0].astype(jnp.float32) + inverse * (grad_scaled - scaled * projected)
    gain_term = jnp.sum((grad_normed * scaled).reshape(-1, model_width), axis=0)
    gain_grad = lax.psum(gain_term, ("tp", "dp"))
    gate_grad, up_grad, down_grad = (
        lax.psum_scatter(gate_term.astype(jnp.bfloat16), "dp", scatter_dimension=0, tiled=True),
        lax.psum_scatter(up_term.astype(jnp.bfloat16), "dp", scatter_dimension=0, tiled=True),
        lax.psum_scatter(down_term.astype(jnp.bfloat16), "dp", scatter_dimension=1, tiled=True),
    )
    return (input_rows.astype(jnp.bfloat16)[None], gain_grad, gate_grad, up_grad, down_grad)


VMEM_SPEC = pl.BlockSpec(memory_space=pltpu.VMEM)
ANY_SPEC = pl.BlockSpec(memory_space=pl.ANY)


def exchange(value, axis, bits):
    count = lax.axis_size(axis)
    return lax.ppermute(value, axis, [(i, i ^ bits) for i in range(count)])


def high_part(value):
    return value.astype(jnp.bfloat16)


def low_part(value):
    return (value - value.astype(jnp.bfloat16).astype(jnp.float32)).astype(jnp.bfloat16)


def relay_kernel(*refs):
    count = len(refs) // 2
    for source, target in zip(refs[:count], refs[count + 1 :]):
        target[...] = source[...]


def relay(pieces, fetched):
    return pl.pallas_call(
        relay_kernel,
        out_shape=tuple(jax.ShapeDtypeStruct(piece.shape, piece.dtype) for piece in pieces),
        in_specs=[VMEM_SPEC] * len(pieces) + [ANY_SPEC],
        out_specs=(VMEM_SPEC,) * len(pieces),
        compiler_params=pltpu.CompilerParams(vmem_limit_bytes=4 * MIB),
        name="relay",
    )(*pieces, fetched)


def sort_kernel(rows, *refs):
    pieces, out_ref, held = refs[:-3], refs[-2], refs[-1]
    count = len(pieces)
    for k, piece in enumerate(pieces):
        value = piece[...].astype(jnp.float32)
        held[rows * k : rows * (k + 1), :] = value[:rows]
        held[rows * (count + k) : rows * (count + k + 1), :] = value[rows:]
    out_ref[...] = held[...].astype(jnp.bfloat16)


def sort_rows(rows, pieces, fetched):
    shape = (2 * rows * len(pieces), pieces[0].shape[1])
    return pl.pallas_call(
        functools.partial(sort_kernel, rows),
        out_shape=jax.ShapeDtypeStruct(shape, jnp.bfloat16),
        in_specs=[VMEM_SPEC] * len(pieces) + [ANY_SPEC],
        out_specs=VMEM_SPEC,
        scratch_shapes=[pltpu.VMEM(shape, jnp.float32)],
        compiler_params=pltpu.CompilerParams(vmem_limit_bytes=8 * MIB),
        name="sort_rows",
    )(*pieces, fetched)


def chunk_copies(sources, top, chunk, pair_ref, down_ref, sems):
    rows = down_ref.shape[0]
    start = top + chunk * rows
    at = pl.ds(start if isinstance(start, int) else pl.multiple_of(start, 16), rows)
    targets = (pair_ref.at[pl.ds(0, rows)], pair_ref.at[pl.ds(rows, rows)], down_ref)
    return [
        pltpu.make_async_copy(source.at[at], target, sems.at[w])
        for w, (source, target) in enumerate(zip(sources, targets))
    ]


def fetch_kernel(chunk, *refs):
    sources, gain_hbm = refs[:3], refs[3]
    pair_ref, down_ref, gain_ref, done_ref, sems, gain_sem = refs[-6:]
    top = lax.axis_index("dp") * (sources[2].shape[0] // 2)
    copies = [pltpu.make_async_copy(gain_hbm, gain_ref, gain_sem)]
    copies += chunk_copies(sources, top, chunk, pair_ref, down_ref, sems)
    for copy in copies:
        copy.start()
    done_ref[...] = jnp.zeros_like(done_ref)
    for copy in copies:
        copy.wait()


def in_hbm(arrays):
    return [pltpu.with_memory_space_constraint(x, pltpu.HBM) for x in arrays]


def fetch_weights(weights, gain, chunk, rows, after=()):
    model = weights[0].shape[1]
    pair, down, gain, done = pl.pallas_call(
        functools.partial(fetch_kernel, chunk),
        out_shape=(
            pltpu.VMEM((2 * rows, model), jnp.bfloat16),
            pltpu.VMEM((rows, model), jnp.bfloat16),
            pltpu.VMEM(gain.shape, gain.dtype),
            pltpu.VMEM((8, LANES), jnp.float32),
        ),
        in_specs=[ANY_SPEC] * (4 + len(after)),
        out_specs=(VMEM_SPEC,) * 4,
        scratch_shapes=[pltpu.SemaphoreType.DMA((3,)), pltpu.SemaphoreType.DMA(())],
        compiler_params=pltpu.CompilerParams(vmem_limit_bytes=4 * MIB),
        cost_estimate=pl.CostEstimate(
            flops=0, bytes_accessed=6 * rows * model, transcendentals=0
        ),
        name="fetch_weights",
    )(*in_hbm((*weights, gain)), *after)
    return (pair, down), gain, done


def hidden_kernel(ready, own_ref, peer_ref, gain_ref, *refs):
    sources, fetched, refs = refs[:3], refs[3 : 3 + 2 * ready], refs[3 + 2 * ready :]
    packed_ref, mine_ref, theirs_ref, gain_part_ref, rows_ref = refs[:5]
    pair_buf, down_buf, total, inverse_buf, sems = refs[5:]
    rest, rows, model = down_buf.shape
    toks = total.shape[0]
    each = toks // 2
    top = lax.axis_index("dp") * (sources[2].shape[0] // 2)

    def copies(c):
        return chunk_copies(sources, top, ready + c, pair_buf.at[c], down_buf.at[c], sems.at[c])

    for c in range(rest):
        for copy in copies(c):
            copy.start()

    def pieces(first):
        return [slice(at, at + CHUNK) for at in range(first, model, CHUNK)]

    squares = jnp.zeros((toks, 1), jnp.float32)
    for at in pieces(0):
        value = jnp.concatenate([own_ref[:each, at], peer_ref[:each, at]], axis=0)
        value = value.astype(jnp.float32)
        squares = squares + jnp.sum(value * value, axis=-1, keepdims=True)
    inverse = lax.rsqrt(squares / model + EPSILON)
    inverse_buf[...] = jnp.broadcast_to(inverse, inverse_buf.shape)
    for at in pieces(0):
        value = jnp.concatenate([own_ref[:each, at], peer_ref[:each, at]], axis=0)
        normed = (value.astype(jnp.float32) * inverse * gain_ref[:, at]).astype(jnp.bfloat16)
        rows_ref[:toks, at] = normed
        rows_ref[toks:, at] = jnp.concatenate([own_ref[each:, at], peer_ref[each:, at]], axis=0)
    total[...] = jnp.zeros_like(total)

    def chunk_pass(pair_ref, down_ref, at):
        both = contract(pair_ref[...], rows_ref[:toks, :], 1, 1)
        grad = contract(down_ref[...], rows_ref[toks:, :], 1, 1)
        gate, up = both[:rows], both[rows:]
        sigmoid = jax.nn.sigmoid(gate)
        active = gate * sigmoid
        grad_gate = grad * up * sigmoid * (1.0 + gate * (1.0 - sigmoid))
        grad_up = grad * active
        parts = [grad_gate, grad_up, active * up, jnp.zeros_like(active)]
        packed_ref[at, :] = jnp.concatenate(parts, axis=1).astype(jnp.bfloat16)
        left = jnp.concatenate([grad_gate, grad_up], axis=0).astype(jnp.bfloat16)
        total[...] += contract(left, pair_ref[...], 0, 0)

    for c in range(ready):
        chunk_pass(fetched[2 * c], fetched[2 * c + 1], pl.ds(c * rows, rows))

    def step(c, carry):
        for copy in copies(c):
            copy.wait()
        at = pl.ds(pl.multiple_of((ready + c) * rows, 16), rows)
        chunk_pass(pair_buf.at[c], down_buf.at[c], at)
        return carry

    lax.fori_loop(0, rest, step, 0)

    for at in pieces(0):
        value = jnp.concatenate([own_ref[:each, at], peer_ref[:each, at]], axis=0)
        part = total[:, at]
        gain = jnp.sum(part * (value.astype(jnp.float32) * inverse_buf[:, :1]), axis=0, keepdims=True)
        gain_part_ref[:, at] = gain
        mine_ref[:, at] = part[:each]
        theirs_ref[:each, at] = part[each:].astype(jnp.bfloat16)
        theirs_ref[each : each + 1, at] = high_part(gain)
        theirs_ref[each + 1 : each + 2, at] = low_part(gain)


def hidden_pass(own, peer, gain, weights, fetched):
    toks, model = own.shape
    each, half, rows = toks // 2, weights[2].shape[0] // 2, fetched[0][1].shape[0]
    rest = half // rows - len(fetched)
    ready = [pltpu.with_memory_space_constraint(x, pltpu.VMEM) for part in fetched for x in part]
    return pl.pallas_call(
        functools.partial(hidden_kernel, len(fetched)),
        out_shape=(
            jax.ShapeDtypeStruct((half, LANES), jnp.bfloat16),
            jax.ShapeDtypeStruct((each, model), jnp.float32),
            jax.ShapeDtypeStruct((each + 2, model), jnp.bfloat16),
            jax.ShapeDtypeStruct((1, model), jnp.float32),
            jax.ShapeDtypeStruct((2 * toks, model), jnp.bfloat16),
        ),
        in_specs=[VMEM_SPEC] * 3 + [ANY_SPEC] * 3 + [VMEM_SPEC] * len(ready),
        out_specs=(VMEM_SPEC,) * 5,
        scratch_shapes=[
            pltpu.VMEM((rest, 2 * rows, model), jnp.bfloat16),
            pltpu.VMEM((rest, rows, model), jnp.bfloat16),
            pltpu.VMEM((toks, model), jnp.float32),
            pltpu.VMEM((toks, LANES), jnp.float32),
            pltpu.SemaphoreType.DMA((rest, 3)),
        ],
        compiler_params=pltpu.CompilerParams(vmem_limit_bytes=32 * MIB),
        cost_estimate=pl.CostEstimate(
            flops=10 * toks * half * model, bytes_accessed=6 * half * model, transcendentals=half * toks
        ),
        name="hidden_pass",
    )(own, peer, gain, *in_hbm(weights), *ready)


def weight_kernel(toks, spans, packs, *refs):
    rows_ref, refs = refs[packs], refs[:packs] + refs[packs + 1 :]
    outs, written_ref, buf, sems = refs[-6:-3], refs[-3], refs[-2], refs[-1]
    slots, _, rows, own_width = buf.shape
    half, each = outs[0].shape[0] // 2, toks // 2
    place = lax.axis_index("dp")
    written_ref[...] = jnp.zeros_like(written_ref)
    own = pl.ds(pl.multiple_of(place * own_width, LANES), own_width)

    def copy(k, slot, row):
        target = outs[k].at[pl.ds(pl.multiple_of(row, 16), rows)]
        return pltpu.make_async_copy(buf.at[slot, k], target, sems.at[slot, k])

    done = 0
    for packed_ref, (swapped, first, last) in zip(refs[:packs], spans):
        top = (1 - place) * half if swapped else place * half

        def step(i, carry, packed_ref=packed_ref, swapped=swapped, top=top, base=done - first):
            slot = lax.rem(base + i, slots)

            @pl.when(base + i >= slots)
            def _():
                for k in range(3):
                    copy(k, slot, top + i * rows).wait()

            normed, incoming = rows_ref[:toks, own], rows_ref[toks:, own]
            if swapped:
                normed = jnp.concatenate([normed[each:], normed[:each]], axis=0)
                incoming = jnp.concatenate([incoming[each:], incoming[:each]], axis=0)
            at = pl.ds(pl.multiple_of(i * rows, 16), rows)
            for k, right in enumerate((normed, normed, incoming)):
                left = packed_ref[at, :][:, k * toks : (k + 1) * toks]
                value = jnp.dot(left, right, preferred_element_type=jnp.float32)
                buf[slot, k] = value.astype(jnp.bfloat16)
                copy(k, slot, top + i * rows).start()
            return carry

        lax.fori_loop(first, last, step, 0)
        done += last - first
    for slot in range(min(slots, done)):
        for k in range(3):
            copy(k, slot, place * half).wait()


def weight_pass(packs, rows, ffw, step_rows, spans, before=(), after=()):
    toks, model = rows.shape[0] // 2, rows.shape[1]
    own_width = model // 2
    blocks = sum(last - first for _, first, last in spans)
    out = jax.ShapeDtypeStruct((ffw, own_width), jnp.bfloat16)
    return pl.pallas_call(
        functools.partial(weight_kernel, toks, spans, len(packs)),
        out_shape=(out,) * 3 + (jax.ShapeDtypeStruct((8, LANES), jnp.float32),),
        in_specs=[VMEM_SPEC] * (len(packs) + 1) + [ANY_SPEC] * (len(before) + len(after)),
        out_specs=(ANY_SPEC,) * 3 + (VMEM_SPEC,),
        scratch_shapes=[
            pltpu.VMEM((3, 3, step_rows, own_width), jnp.bfloat16),
            pltpu.SemaphoreType.DMA((3, 3)),
        ],
        input_output_aliases={len(packs) + 1 + i: i for i in range(len(before))},
        compiler_params=pltpu.CompilerParams(vmem_limit_bytes=16 * MIB),
        cost_estimate=pl.CostEstimate(
            flops=6 * toks * step_rows * own_width * blocks,
            bytes_accessed=6 * step_rows * own_width * blocks,
            transcendentals=0,
        ),
        name="weight_pass",
    )(*packs, rows, *before, *after)


def add_arrived(kept_ref, gain_ref, arrived, extra, held, gain_out_ref):
    gain = gain_ref[...] + (extra[0:1] + extra[1:2])
    held[...] = kept_ref[...] + arrived
    gain_out_ref[...] = gain
    return gain


def fold_kernel(
    kept_ref, gain_ref, arrived_ref, _, keep_ref, gain_out_ref, send_ref, send_gain_ref, held
):
    count = kept_ref.shape[0]
    arrived = arrived_ref[...].astype(jnp.float32)
    gain = add_arrived(kept_ref, gain_ref, arrived[:count], arrived[count:], held, gain_out_ref)
    keep_ref[...] = held[: count // 2, :]
    send_ref[...] = held[count // 2 :, :].astype(jnp.bfloat16)
    send_gain_ref[:1, :] = high_part(gain)
    send_gain_ref[1:, :] = low_part(gain)


def spread_kernel(rows, kept_ref, gain_ref, arrived_ref, extra_ref, _, own_ref, gain_out_ref, *refs):
    outs, held = refs[:-1], refs[-1]
    arrived, extra = arrived_ref[...].astype(jnp.float32), extra_ref[...].astype(jnp.float32)
    gain = add_arrived(kept_ref, gain_ref, arrived, extra, held, gain_out_ref)
    own_ref[...] = held[:rows, :]
    for k, out in enumerate(outs):
        out[:rows, :] = held[rows * (k + 1) : rows * (k + 2), :].astype(jnp.bfloat16)
        out[rows : rows + 1, :] = high_part(gain)
        out[rows + 1 :, :] = low_part(gain)


def add_rows(kernel, kept, gain, arrived, written, kept_rows, sent_rows, name):
    count, model = kept.shape
    return pl.pallas_call(
        kernel,
        out_shape=(
            jax.ShapeDtypeStruct((kept_rows, model), jnp.float32),
            jax.ShapeDtypeStruct((1, model), jnp.float32),
        )
        + tuple(jax.ShapeDtypeStruct((n, model), jnp.bfloat16) for n in sent_rows),
        in_specs=[VMEM_SPEC] * (2 + len(arrived)) + [ANY_SPEC],
        out_specs=(VMEM_SPEC,) * (2 + len(sent_rows)),
        scratch_shapes=[pltpu.VMEM((count, model), jnp.float32)],
        compiler_params=pltpu.CompilerParams(vmem_limit_bytes=8 * MIB),
        name=name,
    )(kept, gain, *arrived, written)


def finish_kernel(rows, tokens_ref, incoming_ref, norm_gain_ref, own_ref, gain_ref, *refs):
    pieces, input_ref, gain_out_ref = refs[:-2], refs[-2], refs[-1]
    grad_normed, gain = own_ref[...], gain_ref[...]
    for piece in pieces:
        value = piece[...].astype(jnp.float32)
        grad_normed = grad_normed + value[:rows]
        gain = gain + (value[rows : rows + 1] + value[rows + 1 : rows + 2])
    gain_out_ref[...] = gain
    values = tokens_ref[...].astype(jnp.float32)
    inverse = lax.rsqrt(jnp.mean(values * values, axis=-1, keepdims=True) + EPSILON)
    scaled = values * inverse
    grad_scaled = grad_normed * norm_gain_ref[...]
    projected = jnp.mean(grad_scaled * scaled, axis=-1, keepdims=True)
    result = incoming_ref[...].astype(jnp.float32) + inverse * (grad_scaled - scaled * projected)
    input_ref[...] = result.astype(jnp.bfloat16)


def finish(rows, tokens, incoming, norm_gain, own, gain, pieces):
    model = tokens.shape[1]
    return pl.pallas_call(
        functools.partial(finish_kernel, rows),
        out_shape=(
            jax.ShapeDtypeStruct((rows, model), jnp.bfloat16),
            jax.ShapeDtypeStruct((1, model), jnp.float32),
        ),
        in_specs=[VMEM_SPEC] * (5 + len(pieces)),
        out_specs=(VMEM_SPEC,) * 2,
        compiler_params=pltpu.CompilerParams(vmem_limit_bytes=8 * MIB),
        name="finish",
    )(tokens, incoming, norm_gain, own, gain, *pieces)


def small_body(tokens, norm_gain, gate_weight, up_weight, down_weight, cotangent):
    rows, model = tokens.shape[1] * tokens.shape[2], tokens.shape[3]
    ffw = down_weight.shape[0]
    tp_count = lax.axis_size("tp")
    own_tokens, own_incoming = tokens.reshape(rows, model), cotangent.reshape(rows, model)
    gain_hbm = norm_gain.reshape(1, model)

    weights = (gate_weight.T, up_weight.T, down_weight)
    step_rows = 160
    blocks = ffw // 2 // step_rows
    piece = jnp.concatenate([own_tokens, own_incoming], axis=0)
    near = exchange(piece, "tp", 1)
    along = [exchange(piece, "tp", bits) for bits in ALONG_Z]
    fetched, gain_row, done = fetch_weights(weights, gain_hbm, 0, step_rows, (piece,))
    along = relay(along, done)
    across = [exchange(arrived, "tp", 1) for arrived in along]
    more, _, done = fetch_weights(weights, gain_hbm, 1, step_rows, (along[0],))
    own = sort_rows(rows, [piece, *along, near, *across], done)
    peer = exchange(own, "dp", 1)
    packed, kept, send, gain, all_rows = hidden_pass(own, peer, gain_row, weights, [fetched, more])
    arrived = exchange(send, "dp", 1)
    peer_packed = exchange(packed, "dp", 1)
    cut, turn = blocks // 2, blocks // 3
    *grads, written = weight_pass([packed], all_rows, ffw, step_rows, [(False, 0, cut)])
    kept, gain, send, send_gain = add_rows(
        fold_kernel, kept, gain, [arrived], written, kept.shape[0] // 2, (kept.shape[0] // 2, 2), "fold"
    )
    arrived = [exchange(send, "tp", 1), exchange(send_gain, "tp", 1)]
    *grads, written = weight_pass(
        [packed, peer_packed], all_rows, ffw, step_rows,
        [(False, cut, blocks), (True, 0, turn)], grads, (send,),
    )
    kept, gain, *sends = add_rows(
        functools.partial(spread_kernel, rows), kept, gain, arrived, written, rows, (rows + 2,) * 3,
        "spread",
    )
    arrived = [exchange(send, "tp", bits) for send, bits in zip(sends, ALONG_Z)]
    gate_t, up_t, down_grad, _ = weight_pass(
        [peer_packed], all_rows, ffw, step_rows, [(True, turn, blocks)], grads, (sends[0],)
    )
    input_rows, gain_grad = finish(
        rows, own_tokens, own_incoming, gain_row, kept, gain, arrived
    )
    return (
        input_rows.reshape(tokens.shape),
        gain_grad.reshape(model),
        gate_t.T,
        up_t.T,
        down_grad,
    )


def body(tokens, norm_gain, gate_weight, up_weight, down_weight, cotangent):
    tp_count, dp_count = lax.axis_size("tp"), lax.axis_size("dp")
    ffw, model = down_weight.shape
    toks = tokens.shape[1] * tokens.shape[2] * tp_count * dp_count
    small = (
        dp_count == 2
        and tp_count == 8
        and toks == 32
        and model % 1024 == 0
        and ffw % 320 == 0
        and 3 * ffw * model <= 40 * MIB
    )
    chosen = small_body if small else general_body
    return chosen(tokens, norm_gain, gate_weight, up_weight, down_weight, cotangent)


def solution(mesh):
    placed = (
        P(("groups", "dp"), None, "tp", None),
        P(),
        P(None, "tp"),
        P(None, "tp"),
        P("tp", None),
        P(("groups", "dp"), None, "tp", None),
    )
    return jax.shard_map(
        body,
        mesh=mesh,
        in_specs=placed,
        out_specs=(
            P(("groups", "dp"), None, "tp", None),
            P("groups"),
            P(("groups", "dp"), "tp"),
            P(("groups", "dp"), "tp"),
            P("tp", ("groups", "dp")),
        ),
        check_vma=False,
    )
```

```python
import functools

import jax
import jax.numpy as jnp
from jax import lax
from jax.experimental import pallas as pl
from jax.experimental.pallas import tpu as pltpu
from jax.sharding import PartitionSpec as P

EPSILON = 1e-06
LANES = 128
MIB = 1 << 20
CHUNK = 512
ALONG_Z = (2, 4, 6)


def contract(left, right, left_dim, right_dim):
    return lax.dot_general(
        left, right, (((left_dim,), (right_dim,)), ((), ())), preferred_element_type=jnp.float32
    )


def norm_tokens(values_in, norm_gain):
    values = values_in.astype(jnp.float32)
    inverse = lax.rsqrt(jnp.mean(values * values, axis=-1, keepdims=True) + EPSILON)
    scaled = values * inverse
    return (scaled, inverse, (scaled * norm_gain).astype(jnp.bfloat16))


def local_pass(normed_all, grads_all, gate_weight, up_weight, down_weight):
    gate_value = jnp.dot(normed_all, gate_weight, preferred_element_type=jnp.float32)
    up_value = jnp.dot(normed_all, up_weight, preferred_element_type=jnp.float32)
    sigmoid_gate = jax.nn.sigmoid(gate_value)
    active = gate_value * sigmoid_gate
    hidden = (active * up_value).astype(jnp.bfloat16)
    grad_hidden = contract(grads_all, down_weight, 1, 1)
    grad_gate = (
        grad_hidden * up_value * sigmoid_gate * (1.0 + gate_value * (1.0 - sigmoid_gate))
    ).astype(jnp.bfloat16)
    grad_up = (grad_hidden * active).astype(jnp.bfloat16)
    partial_value = contract(grad_gate, gate_weight, 1, 1) + contract(grad_up, up_weight, 1, 1)
    gate_term = contract(normed_all, grad_gate, 0, 0)
    up_term = contract(normed_all, grad_up, 0, 0)
    down_term = contract(hidden, grads_all, 0, 0)
    return (partial_value, gate_term, up_term, down_term)


def general_body(tokens, norm_gain, gate_weight, up_weight, down_weight, cotangent):
    micro_count, own_tokens, model_width = (tokens.shape[1], tokens.shape[2], tokens.shape[3])
    tp_count = lax.axis_size("tp")
    scaled, inverse, normed = norm_tokens(tokens[0], norm_gain)
    normed_all, grads_all = (
        lax.all_gather(normed, "tp", axis=1, tiled=True),
        lax.all_gather(cotangent[0], "tp", axis=1, tiled=True),
    )
    partial_value, gate_term, up_term, down_term = local_pass(
        normed_all.reshape(-1, model_width),
        grads_all.reshape(-1, model_width),
        gate_weight,
        up_weight,
        down_weight,
    )
    pieces = lax.all_to_all(
        partial_value.reshape(micro_count, tp_count, own_tokens, model_width),
        "tp",
        split_axis=1,
        concat_axis=1,
        tiled=True,
    )
    grad_normed = jnp.sum(pieces, axis=1)
    grad_scaled = grad_normed * norm_gain
    projected = jnp.mean(grad_scaled * scaled, axis=-1, keepdims=True)
    input_rows = cotangent[0].astype(jnp.float32) + inverse * (grad_scaled - scaled * projected)
    gain_term = jnp.sum((grad_normed * scaled).reshape(-1, model_width), axis=0)
    gain_grad = lax.psum(gain_term, ("tp", "dp"))
    gate_grad, up_grad, down_grad = (
        lax.psum_scatter(gate_term.astype(jnp.bfloat16), "dp", scatter_dimension=0, tiled=True),
        lax.psum_scatter(up_term.astype(jnp.bfloat16), "dp", scatter_dimension=0, tiled=True),
        lax.psum_scatter(down_term.astype(jnp.bfloat16), "dp", scatter_dimension=1, tiled=True),
    )
    return (input_rows.astype(jnp.bfloat16)[None], gain_grad, gate_grad, up_grad, down_grad)


VMEM_SPEC = pl.BlockSpec(memory_space=pltpu.VMEM)
ANY_SPEC = pl.BlockSpec(memory_space=pl.ANY)


def exchange(value, axis, bits):
    count = lax.axis_size(axis)
    return lax.ppermute(value, axis, [(i, i ^ bits) for i in range(count)])


def high_part(value):
    return value.astype(jnp.bfloat16)


def low_part(value):
    return (value - value.astype(jnp.bfloat16).astype(jnp.float32)).astype(jnp.bfloat16)


def relay_kernel(*refs):
    count = len(refs) // 2
    for source, target in zip(refs[:count], refs[count + 1 :]):
        target[...] = source[...]


def relay(pieces, fetched):
    return pl.pallas_call(
        relay_kernel,
        out_shape=tuple(jax.ShapeDtypeStruct(piece.shape, piece.dtype) for piece in pieces),
        in_specs=[VMEM_SPEC] * len(pieces) + [ANY_SPEC],
        out_specs=(VMEM_SPEC,) * len(pieces),
        compiler_params=pltpu.CompilerParams(vmem_limit_bytes=4 * MIB),
        name="relay",
    )(*pieces, fetched)


def sort_kernel(rows, *refs):
    pieces, out_ref, held = refs[:-3], refs[-2], refs[-1]
    count = len(pieces)
    for k, piece in enumerate(pieces):
        value = piece[...].astype(jnp.float32)
        held[rows * k : rows * (k + 1), :] = value[:rows]
        held[rows * (count + k) : rows * (count + k + 1), :] = value[rows:]
    out_ref[...] = held[...].astype(jnp.bfloat16)


def sort_rows(rows, pieces, fetched):
    shape = (2 * rows * len(pieces), pieces[0].shape[1])
    return pl.pallas_call(
        functools.partial(sort_kernel, rows),
        out_shape=jax.ShapeDtypeStruct(shape, jnp.bfloat16),
        in_specs=[VMEM_SPEC] * len(pieces) + [ANY_SPEC],
        out_specs=VMEM_SPEC,
        scratch_shapes=[pltpu.VMEM(shape, jnp.float32)],
        compiler_params=pltpu.CompilerParams(vmem_limit_bytes=8 * MIB),
        name="sort_rows",
    )(*pieces, fetched)


def chunk_copies(sources, top, chunk, pair_ref, down_ref, sems):
    rows = down_ref.shape[0]
    start = top + chunk * rows
    at = pl.ds(start if isinstance(start, int) else pl.multiple_of(start, 16), rows)
    targets = (pair_ref.at[pl.ds(0, rows)], pair_ref.at[pl.ds(rows, rows)], down_ref)
    return [
        pltpu.make_async_copy(source.at[at], target, sems.at[w])
        for w, (source, target) in enumerate(zip(sources, targets))
    ]


def fetch_kernel(chunk, *refs):
    sources, gain_hbm = refs[:3], refs[3]
    pair_ref, down_ref, gain_ref, done_ref, sems, gain_sem = refs[-6:]
    top = lax.axis_index("dp") * (sources[2].shape[0] // 2)
    copies = [pltpu.make_async_copy(gain_hbm, gain_ref, gain_sem)]
    copies += chunk_copies(sources, top, chunk, pair_ref, down_ref, sems)
    for copy in copies:
        copy.start()
    done_ref[...] = jnp.zeros_like(done_ref)
    for copy in copies:
        copy.wait()


def in_hbm(arrays):
    return [pltpu.with_memory_space_constraint(x, pltpu.HBM) for x in arrays]


def fetch_weights(weights, gain, chunk, rows, after=()):
    model = weights[0].shape[1]
    pair, down, gain, done = pl.pallas_call(
        functools.partial(fetch_kernel, chunk),
        out_shape=(
            pltpu.VMEM((2 * rows, model), jnp.bfloat16),
            pltpu.VMEM((rows, model), jnp.bfloat16),
            pltpu.VMEM(gain.shape, gain.dtype),
            pltpu.VMEM((8, LANES), jnp.float32),
        ),
        in_specs=[ANY_SPEC] * (4 + len(after)),
        out_specs=(VMEM_SPEC,) * 4,
        scratch_shapes=[pltpu.SemaphoreType.DMA((3,)), pltpu.SemaphoreType.DMA(())],
        compiler_params=pltpu.CompilerParams(vmem_limit_bytes=4 * MIB),
        cost_estimate=pl.CostEstimate(
            flops=0, bytes_accessed=6 * rows * model, transcendentals=0
        ),
        name="fetch_weights",
    )(*in_hbm((*weights, gain)), *after)
    return (pair, down), gain, done


def hidden_kernel(ready, own_ref, peer_ref, gain_ref, *refs):
    sources, fetched, refs = refs[:3], refs[3 : 3 + 2 * ready], refs[3 + 2 * ready :]
    packed_ref, mine_ref, theirs_ref, gain_part_ref, rows_ref = refs[:5]
    pair_buf, down_buf, total, inverse_buf, sems = refs[5:]
    rest, rows, model = down_buf.shape
    toks = total.shape[0]
    each = toks // 2
    top = lax.axis_index("dp") * (sources[2].shape[0] // 2)

    def copies(c):
        return chunk_copies(sources, top, ready + c, pair_buf.at[c], down_buf.at[c], sems.at[c])

    for c in range(rest):
        for copy in copies(c):
            copy.start()

    def pieces(first):
        return [slice(at, at + CHUNK) for at in range(first, model, CHUNK)]

    squares = jnp.zeros((toks, 1), jnp.float32)
    for at in pieces(0):
        value = jnp.concatenate([own_ref[:each, at], peer_ref[:each, at]], axis=0)
        value = value.astype(jnp.float32)
        squares = squares + jnp.sum(value * value, axis=-1, keepdims=True)
    inverse = lax.rsqrt(squares / model + EPSILON)
    inverse_buf[...] = jnp.broadcast_to(inverse, inverse_buf.shape)
    for at in pieces(0):
        value = jnp.concatenate([own_ref[:each, at], peer_ref[:each, at]], axis=0)
        normed = (value.astype(jnp.float32) * inverse * gain_ref[:, at]).astype(jnp.bfloat16)
        rows_ref[:toks, at] = normed
        rows_ref[toks:, at] = jnp.concatenate([own_ref[each:, at], peer_ref[each:, at]], axis=0)
    total[...] = jnp.zeros_like(total)

    def chunk_pass(pair_ref, down_ref, at):
        gate_ref, up_ref = pair_ref.at[pl.ds(0, rows)], pair_ref.at[pl.ds(rows, rows)]
        gate = contract(rows_ref[:toks, :], gate_ref[...], 1, 1)
        up = contract(rows_ref[:toks, :], up_ref[...], 1, 1)
        grad = contract(rows_ref[toks:, :], down_ref[...], 1, 1)
        sigmoid = jax.nn.sigmoid(gate)
        active = gate * sigmoid
        grad_gate = grad * up * sigmoid * (1.0 + gate * (1.0 - sigmoid))
        grad_up = grad * active
        parts = [grad_gate, grad_up, active * up, jnp.zeros_like(active)]
        packed_ref[at, :] = jnp.concatenate(parts, axis=0).T.astype(jnp.bfloat16)
        part = contract(grad_gate.astype(jnp.bfloat16), gate_ref[...], 1, 0)
        total[...] += part + contract(grad_up.astype(jnp.bfloat16), up_ref[...], 1, 0)

    for c in range(ready):
        chunk_pass(fetched[2 * c], fetched[2 * c + 1], pl.ds(c * rows, rows))

    def step(c, carry):
        for copy in copies(c):
            copy.wait()
        at = pl.ds(pl.multiple_of((ready + c) * rows, 16), rows)
        chunk_pass(pair_buf.at[c], down_buf.at[c], at)
        return carry

    lax.fori_loop(0, rest, step, 0)

    for at in pieces(0):
        value = jnp.concatenate([own_ref[:each, at], peer_ref[:each, at]], axis=0)
        part = total[:, at]
        gain = jnp.sum(part * (value.astype(jnp.float32) * inverse_buf[:, :1]), axis=0, keepdims=True)
        gain_part_ref[:, at] = gain
        mine_ref[:, at] = part[:each]
        theirs_ref[:each, at] = part[each:].astype(jnp.bfloat16)
        theirs_ref[each : each + 1, at] = high_part(gain)
        theirs_ref[each + 1 : each + 2, at] = low_part(gain)


def hidden_pass(own, peer, gain, weights, fetched):
    toks, model = own.shape
    each, half, rows = toks // 2, weights[2].shape[0] // 2, fetched[0][1].shape[0]
    rest = half // rows - len(fetched)
    ready = [pltpu.with_memory_space_constraint(x, pltpu.VMEM) for part in fetched for x in part]
    return pl.pallas_call(
        functools.partial(hidden_kernel, len(fetched)),
        out_shape=(
            jax.ShapeDtypeStruct((half, LANES), jnp.bfloat16),
            jax.ShapeDtypeStruct((each, model), jnp.float32),
            jax.ShapeDtypeStruct((each + 2, model), jnp.bfloat16),
            jax.ShapeDtypeStruct((1, model), jnp.float32),
            jax.ShapeDtypeStruct((2 * toks, model), jnp.bfloat16),
        ),
        in_specs=[VMEM_SPEC] * 3 + [ANY_SPEC] * 3 + [VMEM_SPEC] * len(ready),
        out_specs=(VMEM_SPEC,) * 5,
        scratch_shapes=[
            pltpu.VMEM((rest, 2 * rows, model), jnp.bfloat16),
            pltpu.VMEM((rest, rows, model), jnp.bfloat16),
            pltpu.VMEM((toks, model), jnp.float32),
            pltpu.VMEM((toks, LANES), jnp.float32),
            pltpu.SemaphoreType.DMA((rest, 3)),
        ],
        compiler_params=pltpu.CompilerParams(vmem_limit_bytes=32 * MIB),
        cost_estimate=pl.CostEstimate(
            flops=10 * toks * half * model, bytes_accessed=6 * half * model, transcendentals=half * toks
        ),
        name="hidden_pass",
    )(own, peer, gain, *in_hbm(weights), *ready)


def weight_kernel(toks, spans, packs, *refs):
    rows_ref, refs = refs[packs], refs[:packs] + refs[packs + 1 :]
    outs, written_ref, buf, sems = refs[-6:-3], refs[-3], refs[-2], refs[-1]
    slots, _, rows, own_width = buf.shape
    half, each = outs[0].shape[0] // 2, toks // 2
    place = lax.axis_index("dp")
    written_ref[...] = jnp.zeros_like(written_ref)
    own = pl.ds(pl.multiple_of(place * own_width, LANES), own_width)

    def copy(k, slot, row):
        target = outs[k].at[pl.ds(pl.multiple_of(row, 16), rows)]
        return pltpu.make_async_copy(buf.at[slot, k], target, sems.at[slot, k])

    done = 0
    for packed_ref, (swapped, first, last) in zip(refs[:packs], spans):
        top = (1 - place) * half if swapped else place * half

        def step(i, carry, packed_ref=packed_ref, swapped=swapped, top=top, base=done - first):
            slot = lax.rem(base + i, slots)

            @pl.when(base + i >= slots)
            def _():
                for k in range(3):
                    copy(k, slot, top + i * rows).wait()

            normed, incoming = rows_ref[:toks, own], rows_ref[toks:, own]
            if swapped:
                normed = jnp.concatenate([normed[each:], normed[:each]], axis=0)
                incoming = jnp.concatenate([incoming[each:], incoming[:each]], axis=0)
            at = pl.ds(pl.multiple_of(i * rows, 16), rows)
            for k, right in enumerate((normed, normed, incoming)):
                left = packed_ref[at, :][:, k * toks : (k + 1) * toks]
                value = jnp.dot(left, right, preferred_element_type=jnp.float32)
                buf[slot, k] = value.astype(jnp.bfloat16)
                copy(k, slot, top + i * rows).start()
            return carry

        lax.fori_loop(first, last, step, 0)
        done += last - first
    for slot in range(min(slots, done)):
        for k in range(3):
            copy(k, slot, place * half).wait()


def weight_pass(packs, rows, ffw, step_rows, spans, before=(), after=()):
    toks, model = rows.shape[0] // 2, rows.shape[1]
    own_width = model // 2
    blocks = sum(last - first for _, first, last in spans)
    out = jax.ShapeDtypeStruct((ffw, own_width), jnp.bfloat16)
    return pl.pallas_call(
        functools.partial(weight_kernel, toks, spans, len(packs)),
        out_shape=(out,) * 3 + (jax.ShapeDtypeStruct((8, LANES), jnp.float32),),
        in_specs=[VMEM_SPEC] * (len(packs) + 1) + [ANY_SPEC] * (len(before) + len(after)),
        out_specs=(ANY_SPEC,) * 3 + (VMEM_SPEC,),
        scratch_shapes=[
            pltpu.VMEM((3, 3, step_rows, own_width), jnp.bfloat16),
            pltpu.SemaphoreType.DMA((3, 3)),
        ],
        input_output_aliases={len(packs) + 1 + i: i for i in range(len(before))},
        compiler_params=pltpu.CompilerParams(vmem_limit_bytes=16 * MIB),
        cost_estimate=pl.CostEstimate(
            flops=6 * toks * step_rows * own_width * blocks,
            bytes_accessed=6 * step_rows * own_width * blocks,
            transcendentals=0,
        ),
        name="weight_pass",
    )(*packs, rows, *before, *after)


def add_arrived(kept_ref, gain_ref, arrived, extra, held, gain_out_ref):
    gain = gain_ref[...] + (extra[0:1] + extra[1:2])
    held[...] = kept_ref[...] + arrived
    gain_out_ref[...] = gain
    return gain


def fold_kernel(
    kept_ref, gain_ref, arrived_ref, _, keep_ref, gain_out_ref, send_ref, send_gain_ref, held
):
    count = kept_ref.shape[0]
    arrived = arrived_ref[...].astype(jnp.float32)
    gain = add_arrived(kept_ref, gain_ref, arrived[:count], arrived[count:], held, gain_out_ref)
    keep_ref[...] = held[: count // 2, :]
    send_ref[...] = held[count // 2 :, :].astype(jnp.bfloat16)
    send_gain_ref[:1, :] = high_part(gain)
    send_gain_ref[1:, :] = low_part(gain)


def spread_kernel(rows, kept_ref, gain_ref, arrived_ref, extra_ref, _, own_ref, gain_out_ref, *refs):
    outs, held = refs[:-1], refs[-1]
    arrived, extra = arrived_ref[...].astype(jnp.float32), extra_ref[...].astype(jnp.float32)
    gain = add_arrived(kept_ref, gain_ref, arrived, extra, held, gain_out_ref)
    own_ref[...] = held[:rows, :]
    for k, out in enumerate(outs):
        out[:rows, :] = held[rows * (k + 1) : rows * (k + 2), :].astype(jnp.bfloat16)
        out[rows : rows + 1, :] = high_part(gain)
        out[rows + 1 :, :] = low_part(gain)


def add_rows(kernel, kept, gain, arrived, written, kept_rows, sent_rows, name):
    count, model = kept.shape
    return pl.pallas_call(
        kernel,
        out_shape=(
            jax.ShapeDtypeStruct((kept_rows, model), jnp.float32),
            jax.ShapeDtypeStruct((1, model), jnp.float32),
        )
        + tuple(jax.ShapeDtypeStruct((n, model), jnp.bfloat16) for n in sent_rows),
        in_specs=[VMEM_SPEC] * (2 + len(arrived)) + [ANY_SPEC],
        out_specs=(VMEM_SPEC,) * (2 + len(sent_rows)),
        scratch_shapes=[pltpu.VMEM((count, model), jnp.float32)],
        compiler_params=pltpu.CompilerParams(vmem_limit_bytes=8 * MIB),
        name=name,
    )(kept, gain, *arrived, written)


def finish_kernel(rows, tokens_ref, incoming_ref, norm_gain_ref, own_ref, gain_ref, *refs):
    pieces, input_ref, gain_out_ref = refs[:-2], refs[-2], refs[-1]
    grad_normed, gain = own_ref[...], gain_ref[...]
    for piece in pieces:
        value = piece[...].astype(jnp.float32)
        grad_normed = grad_normed + value[:rows]
        gain = gain + (value[rows : rows + 1] + value[rows + 1 : rows + 2])
    gain_out_ref[...] = gain
    values = tokens_ref[...].astype(jnp.float32)
    inverse = lax.rsqrt(jnp.mean(values * values, axis=-1, keepdims=True) + EPSILON)
    scaled = values * inverse
    grad_scaled = grad_normed * norm_gain_ref[...]
    projected = jnp.mean(grad_scaled * scaled, axis=-1, keepdims=True)
    result = incoming_ref[...].astype(jnp.float32) + inverse * (grad_scaled - scaled * projected)
    input_ref[...] = result.astype(jnp.bfloat16)


def finish(rows, tokens, incoming, norm_gain, own, gain, pieces):
    model = tokens.shape[1]
    return pl.pallas_call(
        functools.partial(finish_kernel, rows),
        out_shape=(
            jax.ShapeDtypeStruct((rows, model), jnp.bfloat16),
            jax.ShapeDtypeStruct((1, model), jnp.float32),
        ),
        in_specs=[VMEM_SPEC] * (5 + len(pieces)),
        out_specs=(VMEM_SPEC,) * 2,
        compiler_params=pltpu.CompilerParams(vmem_limit_bytes=8 * MIB),
        name="finish",
    )(tokens, incoming, norm_gain, own, gain, *pieces)


def small_body(tokens, norm_gain, gate_weight, up_weight, down_weight, cotangent):
    rows, model = tokens.shape[1] * tokens.shape[2], tokens.shape[3]
    ffw = down_weight.shape[0]
    tp_count = lax.axis_size("tp")
    own_tokens, own_incoming = tokens.reshape(rows, model), cotangent.reshape(rows, model)
    gain_hbm = norm_gain.reshape(1, model)

    weights = (gate_weight.T, up_weight.T, down_weight)
    step_rows = 160
    blocks = ffw // 2 // step_rows
    piece = jnp.concatenate([own_tokens, own_incoming], axis=0)
    near = exchange(piece, "tp", 1)
    along = [exchange(piece, "tp", bits) for bits in ALONG_Z]
    fetched, gain_row, done = fetch_weights(weights, gain_hbm, 0, step_rows, (piece,))
    along = relay(along, done)
    across = [exchange(arrived, "tp", 1) for arrived in along]
    more, _, done = fetch_weights(weights, gain_hbm, 1, step_rows, (along[0],))
    own = sort_rows(rows, [piece, *along, near, *across], done)
    peer = exchange(own, "dp", 1)
    packed, kept, send, gain, all_rows = hidden_pass(own, peer, gain_row, weights, [fetched, more])
    arrived = exchange(send, "dp", 1)
    peer_packed = exchange(packed, "dp", 1)
    cut, turn = blocks // 2, blocks // 3
    *grads, written = weight_pass([packed], all_rows, ffw, step_rows, [(False, 0, cut)])
    kept, gain, send, send_gain = add_rows(
        fold_kernel, kept, gain, [arrived], written, kept.shape[0] // 2, (kept.shape[0] // 2, 2), "fold"
    )
    arrived = [exchange(send, "tp", 1), exchange(send_gain, "tp", 1)]
    *grads, written = weight_pass(
        [packed, peer_packed], all_rows, ffw, step_rows,
        [(False, cut, blocks), (True, 0, turn)], grads, (send,),
    )
    kept, gain, *sends = add_rows(
        functools.partial(spread_kernel, rows), kept, gain, arrived, written, rows, (rows + 2,) * 3,
        "spread",
    )
    arrived = [exchange(send, "tp", bits) for send, bits in zip(sends, ALONG_Z)]
    gate_t, up_t, down_grad, _ = weight_pass(
        [peer_packed], all_rows, ffw, step_rows, [(True, turn, blocks)], grads, (sends[0],)
    )
    input_rows, gain_grad = finish(
        rows, own_tokens, own_incoming, gain_row, kept, gain, arrived
    )
    return (
        input_rows.reshape(tokens.shape),
        gain_grad.reshape(model),
        gate_t.T,
        up_t.T,
        down_grad,
    )


def body(tokens, norm_gain, gate_weight, up_weight, down_weight, cotangent):
    tp_count, dp_count = lax.axis_size("tp"), lax.axis_size("dp")
    ffw, model = down_weight.shape
    toks = tokens.shape[1] * tokens.shape[2] * tp_count * dp_count
    small = (
        dp_count == 2
        and tp_count == 8
        and toks == 32
        and model % 1024 == 0
        and ffw % 320 == 0
        and 3 * ffw * model <= 40 * MIB
    )
    chosen = small_body if small else general_body
    return chosen(tokens, norm_gain, gate_weight, up_weight, down_weight, cotangent)


def solution(mesh):
    placed = (
        P(("groups", "dp"), None, "tp", None),
        P(),
        P(None, "tp"),
        P(None, "tp"),
        P("tp", None),
        P(("groups", "dp"), None, "tp", None),
    )
    return jax.shard_map(
        body,
        mesh=mesh,
        in_specs=placed,
        out_specs=(
            P(("groups", "dp"), None, "tp", None),
            P("groups"),
            P(("groups", "dp"), "tp"),
            P(("groups", "dp"), "tp"),
            P("tp", ("groups", "dp")),
        ),
        check_vma=False,
    )
```

```python
import functools

import jax
import jax.numpy as jnp
from jax import lax
from jax.experimental import pallas as pl
from jax.experimental.pallas import tpu as pltpu
from jax.sharding import PartitionSpec as P

EPSILON = 1e-06
LANES = 128
MIB = 1 << 20
CHUNK = 1024
ALONG_Z = (2, 4, 6)


def contract(left, right, left_dim, right_dim):
    return lax.dot_general(
        left, right, (((left_dim,), (right_dim,)), ((), ())), preferred_element_type=jnp.float32
    )


def norm_tokens(values_in, norm_gain):
    values = values_in.astype(jnp.float32)
    inverse = lax.rsqrt(jnp.mean(values * values, axis=-1, keepdims=True) + EPSILON)
    scaled = values * inverse
    return (scaled, inverse, (scaled * norm_gain).astype(jnp.bfloat16))


def local_pass(normed_all, grads_all, gate_weight, up_weight, down_weight):
    gate_value = jnp.dot(normed_all, gate_weight, preferred_element_type=jnp.float32)
    up_value = jnp.dot(normed_all, up_weight, preferred_element_type=jnp.float32)
    sigmoid_gate = jax.nn.sigmoid(gate_value)
    active = gate_value * sigmoid_gate
    hidden = (active * up_value).astype(jnp.bfloat16)
    grad_hidden = contract(grads_all, down_weight, 1, 1)
    grad_gate = (
        grad_hidden * up_value * sigmoid_gate * (1.0 + gate_value * (1.0 - sigmoid_gate))
    ).astype(jnp.bfloat16)
    grad_up = (grad_hidden * active).astype(jnp.bfloat16)
    partial_value = contract(grad_gate, gate_weight, 1, 1) + contract(grad_up, up_weight, 1, 1)
    gate_term = contract(normed_all, grad_gate, 0, 0)
    up_term = contract(normed_all, grad_up, 0, 0)
    down_term = contract(hidden, grads_all, 0, 0)
    return (partial_value, gate_term, up_term, down_term)


def general_body(tokens, norm_gain, gate_weight, up_weight, down_weight, cotangent):
    micro_count, own_tokens, model_width = (tokens.shape[1], tokens.shape[2], tokens.shape[3])
    tp_count = lax.axis_size("tp")
    scaled, inverse, normed = norm_tokens(tokens[0], norm_gain)
    normed_all, grads_all = (
        lax.all_gather(normed, "tp", axis=1, tiled=True),
        lax.all_gather(cotangent[0], "tp", axis=1, tiled=True),
    )
    partial_value, gate_term, up_term, down_term = local_pass(
        normed_all.reshape(-1, model_width),
        grads_all.reshape(-1, model_width),
        gate_weight,
        up_weight,
        down_weight,
    )
    pieces = lax.all_to_all(
        partial_value.reshape(micro_count, tp_count, own_tokens, model_width),
        "tp",
        split_axis=1,
        concat_axis=1,
        tiled=True,
    )
    grad_normed = jnp.sum(pieces, axis=1)
    grad_scaled = grad_normed * norm_gain
    projected = jnp.mean(grad_scaled * scaled, axis=-1, keepdims=True)
    input_rows = cotangent[0].astype(jnp.float32) + inverse * (grad_scaled - scaled * projected)
    gain_term = jnp.sum((grad_normed * scaled).reshape(-1, model_width), axis=0)
    gain_grad = lax.psum(gain_term, ("tp", "dp"))
    gate_grad, up_grad, down_grad = (
        lax.psum_scatter(gate_term.astype(jnp.bfloat16), "dp", scatter_dimension=0, tiled=True),
        lax.psum_scatter(up_term.astype(jnp.bfloat16), "dp", scatter_dimension=0, tiled=True),
        lax.psum_scatter(down_term.astype(jnp.bfloat16), "dp", scatter_dimension=1, tiled=True),
    )
    return (input_rows.astype(jnp.bfloat16)[None], gain_grad, gate_grad, up_grad, down_grad)


VMEM_SPEC = pl.BlockSpec(memory_space=pltpu.VMEM)
ANY_SPEC = pl.BlockSpec(memory_space=pl.ANY)


def exchange(value, axis, bits):
    count = lax.axis_size(axis)
    return lax.ppermute(value, axis, [(i, i ^ bits) for i in range(count)])


def high_part(value):
    return value.astype(jnp.bfloat16)


def low_part(value):
    return (value - value.astype(jnp.bfloat16).astype(jnp.float32)).astype(jnp.bfloat16)


def relay_kernel(*refs):
    count = len(refs) // 2
    for source, target in zip(refs[:count], refs[count + 1 :]):
        target[...] = source[...]


def relay(pieces, fetched):
    return pl.pallas_call(
        relay_kernel,
        out_shape=tuple(jax.ShapeDtypeStruct(piece.shape, piece.dtype) for piece in pieces),
        in_specs=[VMEM_SPEC] * len(pieces) + [ANY_SPEC],
        out_specs=(VMEM_SPEC,) * len(pieces),
        compiler_params=pltpu.CompilerParams(vmem_limit_bytes=4 * MIB),
        name="relay",
    )(*pieces, fetched)


def sort_kernel(rows, *refs):
    pieces, out_ref, held = refs[:-3], refs[-2], refs[-1]
    count = len(pieces)
    for k, piece in enumerate(pieces):
        value = piece[...].astype(jnp.float32)
        held[rows * k : rows * (k + 1), :] = value[:rows]
        held[rows * (count + k) : rows * (count + k + 1), :] = value[rows:]
    out_ref[...] = held[...].astype(jnp.bfloat16)


def sort_rows(rows, pieces, fetched):
    shape = (2 * rows * len(pieces), pieces[0].shape[1])
    return pl.pallas_call(
        functools.partial(sort_kernel, rows),
        out_shape=jax.ShapeDtypeStruct(shape, jnp.bfloat16),
        in_specs=[VMEM_SPEC] * len(pieces) + [ANY_SPEC],
        out_specs=VMEM_SPEC,
        scratch_shapes=[pltpu.VMEM(shape, jnp.float32)],
        compiler_params=pltpu.CompilerParams(vmem_limit_bytes=8 * MIB),
        name="sort_rows",
    )(*pieces, fetched)


def padded(count):
    return -(-count // LANES) * LANES


def chunk_copies(sources, chunk, pair_ref, down_ref, sems):
    wide, width = down_ref.shape
    half = sources[2].shape[0] // 2
    top = pl.multiple_of(lax.axis_index("dp") * half, 16)
    start = chunk * width
    at = pl.ds(start if isinstance(start, int) else pl.multiple_of(start, LANES), width)
    targets = (pair_ref.at[pl.ds(0, half)], pair_ref.at[pl.ds(wide, half)], down_ref.at[pl.ds(0, half)])
    return [
        pltpu.make_async_copy(source.at[pl.ds(top, half), at], target, sems.at[w])
        for w, (source, target) in enumerate(zip(sources, targets))
    ]


def clear_between(pair_ref, down_ref, half):
    wide, width = down_ref.shape
    if wide > half:
        zeros = jnp.zeros((wide - half, width), jnp.bfloat16)
        pair_ref[half:wide, :] = zeros
        pair_ref[wide + half :, :] = zeros
        down_ref[half:, :] = zeros


def fetch_kernel(chunk, *refs):
    sources, gain_hbm = refs[:3], refs[3]
    pair_ref, down_ref, gain_ref, done_ref, sems, gain_sem = refs[-6:]
    copies = [pltpu.make_async_copy(gain_hbm, gain_ref, gain_sem)]
    copies += chunk_copies(sources, chunk, pair_ref, down_ref, sems)
    for copy in copies:
        copy.start()
    done_ref[...] = jnp.zeros_like(done_ref)
    clear_between(pair_ref, down_ref, sources[2].shape[0] // 2)
    for copy in copies:
        copy.wait()


def in_hbm(arrays):
    return [pltpu.with_memory_space_constraint(x, pltpu.HBM) for x in arrays]


def fetch_weights(weights, gain, chunk, after=()):
    half = weights[2].shape[0] // 2
    pair, down, gain, done = pl.pallas_call(
        functools.partial(fetch_kernel, chunk),
        out_shape=(
            pltpu.VMEM((2 * padded(half), CHUNK), jnp.bfloat16),
            pltpu.VMEM((padded(half), CHUNK), jnp.bfloat16),
            pltpu.VMEM(gain.shape, gain.dtype),
            pltpu.VMEM((8, LANES), jnp.float32),
        ),
        in_specs=[ANY_SPEC] * (4 + len(after)),
        out_specs=(VMEM_SPEC,) * 4,
        scratch_shapes=[pltpu.SemaphoreType.DMA((3,)), pltpu.SemaphoreType.DMA(())],
        compiler_params=pltpu.CompilerParams(vmem_limit_bytes=4 * MIB),
        cost_estimate=pl.CostEstimate(
            flops=0, bytes_accessed=6 * half * CHUNK, transcendentals=0
        ),
        name="fetch_weights",
    )(*in_hbm((*weights, gain)), *after)
    return (pair, down), gain, done


def hidden_kernel(ready, own_ref, peer_ref, gain_ref, *refs):
    sources, fetched, refs = refs[:3], refs[3 : 3 + 2 * ready], refs[3 + 2 * ready :]
    packed_ref, mine_ref, theirs_ref, gain_part_ref, rows_ref = refs[:5]
    pair_buf, down_buf, acc, acc_grad, left, inverse_buf, sems = refs[5:]
    rest, wide, width = down_buf.shape
    toks, half = acc.shape[0], packed_ref.shape[0]
    each, model = toks // 2, rows_ref.shape[1]

    def copies(c):
        return chunk_copies(sources, ready + c, pair_buf.at[c], down_buf.at[c], sems.at[c])

    for c in range(rest):
        for copy in copies(c):
            copy.start()
    for c in range(rest):
        clear_between(pair_buf.at[c], down_buf.at[c], half)

    squares = jnp.zeros((toks, 1), jnp.float32)
    pieces = [slice(at, at + 512) for at in range(0, model, 512)]
    for at in pieces:
        value = jnp.concatenate([own_ref[:each, at], peer_ref[:each, at]], axis=0)
        value = value.astype(jnp.float32)
        squares = squares + jnp.sum(value * value, axis=-1, keepdims=True)
    inverse = lax.rsqrt(squares / model + EPSILON)
    inverse_buf[...] = jnp.broadcast_to(inverse, inverse_buf.shape)
    for at in pieces:
        value = jnp.concatenate([own_ref[:each, at], peer_ref[:each, at]], axis=0)
        normed = (value.astype(jnp.float32) * inverse * gain_ref[:, at]).astype(jnp.bfloat16)
        rows_ref[:toks, at] = normed
        rows_ref[toks:, at] = jnp.concatenate([own_ref[each:, at], peer_ref[each:, at]], axis=0)
    acc[...] = jnp.zeros_like(acc)
    acc_grad[...] = jnp.zeros_like(acc_grad)

    def forward(pair_ref, down_ref, at):
        acc[...] += contract(rows_ref[:toks, at], pair_ref[...], 1, 1)
        acc_grad[...] += contract(rows_ref[toks:, at], down_ref[...], 1, 1)

    def backward(pair_ref, at):
        part = jnp.dot(left[...], pair_ref[...], preferred_element_type=jnp.float32)
        value = jnp.concatenate([own_ref[:each, at], peer_ref[:each, at]], axis=0)
        scaled = value.astype(jnp.float32) * inverse_buf[:, :1]
        gain = jnp.sum(part * scaled, axis=0, keepdims=True)
        gain_part_ref[:, at] = gain
        mine_ref[:, at] = part[:each]
        theirs_ref[:each, at] = part[each:].astype(jnp.bfloat16)
        theirs_ref[each : each + 1, at] = high_part(gain)
        theirs_ref[each + 1 : each + 2, at] = low_part(gain)

    def place(c):
        return pl.ds(pl.multiple_of((ready + c) * width, LANES), width)

    for c in range(ready):
        forward(fetched[2 * c], fetched[2 * c + 1], pl.ds(c * width, width))

    def forward_step(c, carry):
        for copy in copies(c):
            copy.wait()
        forward(pair_buf.at[c], down_buf.at[c], place(c))
        return carry

    lax.fori_loop(0, rest, forward_step, 0)

    for first in range(0, wide, LANES):
        at = slice(first, first + LANES)
        up_at = slice(wide + first, wide + first + LANES)
        gate, up, grad = acc[:, at], acc[:, up_at], acc_grad[:, at]
        sigmoid = jax.nn.sigmoid(gate)
        active = gate * sigmoid
        grad_gate = grad * up * sigmoid * (1.0 + gate * (1.0 - sigmoid))
        grad_up = grad * active
        left[:, at] = grad_gate.astype(jnp.bfloat16)
        left[:, up_at] = grad_up.astype(jnp.bfloat16)
        parts = [grad_gate, grad_up, active * up, jnp.zeros_like(active)]
        columns = jnp.concatenate(parts, axis=0).T.astype(jnp.bfloat16)
        last = min(first + LANES, half)
        packed_ref[first:last, :] = columns[: last - first]

    for c in range(ready):
        backward(fetched[2 * c], pl.ds(c * width, width))

    def backward_step(c, carry):
        backward(pair_buf.at[c], place(c))
        return carry

    lax.fori_loop(0, rest, backward_step, 0)


def hidden_pass(own, peer, gain, weights, fetched):
    toks, model = own.shape
    each, half = toks // 2, weights[2].shape[0] // 2
    wide, rest = padded(half), model // CHUNK - len(fetched)
    ready = [pltpu.with_memory_space_constraint(x, pltpu.VMEM) for part in fetched for x in part]
    return pl.pallas_call(
        functools.partial(hidden_kernel, len(fetched)),
        out_shape=(
            jax.ShapeDtypeStruct((half, LANES), jnp.bfloat16),
            jax.ShapeDtypeStruct((each, model), jnp.float32),
            jax.ShapeDtypeStruct((each + 2, model), jnp.bfloat16),
            jax.ShapeDtypeStruct((1, model), jnp.float32),
            jax.ShapeDtypeStruct((2 * toks, model), jnp.bfloat16),
        ),
        in_specs=[VMEM_SPEC] * 3 + [ANY_SPEC] * 3 + [VMEM_SPEC] * len(ready),
        out_specs=(VMEM_SPEC,) * 5,
        scratch_shapes=[
            pltpu.VMEM((rest, 2 * wide, CHUNK), jnp.bfloat16),
            pltpu.VMEM((rest, wide, CHUNK), jnp.bfloat16),
            pltpu.VMEM((toks, 2 * wide), jnp.float32),
            pltpu.VMEM((toks, wide), jnp.float32),
            pltpu.VMEM((toks, 2 * wide), jnp.bfloat16),
            pltpu.VMEM((toks, LANES), jnp.float32),
            pltpu.SemaphoreType.DMA((rest, 3)),
        ],
        compiler_params=pltpu.CompilerParams(vmem_limit_bytes=32 * MIB),
        cost_estimate=pl.CostEstimate(
            flops=10 * toks * half * model, bytes_accessed=6 * half * model, transcendentals=half * toks
        ),
        name="hidden_pass",
    )(own, peer, gain, *in_hbm(weights), *ready)


def weight_kernel(toks, spans, packs, *refs):
    rows_ref, refs = refs[packs], refs[:packs] + refs[packs + 1 :]
    outs, written_ref, buf, right_buf, sems = refs[-7:-4], *refs[-4:]
    slots, _, rows, own_width = buf.shape
    half, each = outs[0].shape[0] // 2, toks // 2
    place = lax.axis_index("dp")
    written_ref[...] = jnp.zeros_like(written_ref)
    own = pl.ds(pl.multiple_of(place * own_width, LANES), own_width)

    def copy(k, slot, row):
        target = outs[k].at[pl.ds(pl.multiple_of(row, 16), rows)]
        return pltpu.make_async_copy(buf.at[slot, k], target, sems.at[slot, k])

    done = 0
    for packed_ref, (swapped, first, last) in zip(refs[:packs], spans):
        top = (1 - place) * half if swapped else place * half
        if swapped:
            for at in (0, toks):
                mine, theirs = rows_ref[at : at + each, own], rows_ref[at + each : at + toks, own]
                right_buf[at : at + toks, :] = jnp.concatenate([theirs, mine], axis=0)
        else:
            right_buf[...] = rows_ref[:, own]

        def step(i, carry, packed_ref=packed_ref, top=top, base=done - first):
            slot = lax.rem(base + i, slots)

            @pl.when(base + i >= slots)
            def _():
                for k in range(3):
                    copy(k, slot, top + i * rows).wait()

            normed, incoming = right_buf[:toks, :], right_buf[toks:, :]
            at = pl.ds(pl.multiple_of(i * rows, 16), rows)
            for k, right in enumerate((normed, normed, incoming)):
                left = packed_ref[at, :][:, k * toks : (k + 1) * toks]
                value = jnp.dot(left, right, preferred_element_type=jnp.float32)
                buf[slot, k] = value.astype(jnp.bfloat16)
                copy(k, slot, top + i * rows).start()
            return carry

        lax.fori_loop(first, last, step, 0)
        done += last - first
    for slot in range(min(slots, done)):
        for k in range(3):
            copy(k, slot, place * half).wait()


def weight_pass(packs, rows, ffw, step_rows, spans, before=(), after=()):
    toks, model = rows.shape[0] // 2, rows.shape[1]
    own_width = model // 2
    blocks = sum(last - first for _, first, last in spans)
    out = jax.ShapeDtypeStruct((ffw, own_width), jnp.bfloat16)
    return pl.pallas_call(
        functools.partial(weight_kernel, toks, spans, len(packs)),
        out_shape=(out,) * 3 + (jax.ShapeDtypeStruct((8, LANES), jnp.float32),),
        in_specs=[VMEM_SPEC] * (len(packs) + 1) + [ANY_SPEC] * (len(before) + len(after)),
        out_specs=(ANY_SPEC,) * 3 + (VMEM_SPEC,),
        scratch_shapes=[
            pltpu.VMEM((3, 3, step_rows, own_width), jnp.bfloat16),
            pltpu.VMEM((2 * toks, own_width), jnp.bfloat16),
            pltpu.SemaphoreType.DMA((3, 3)),
        ],
        input_output_aliases={len(packs) + 1 + i: i for i in range(len(before))},
        compiler_params=pltpu.CompilerParams(vmem_limit_bytes=16 * MIB),
        cost_estimate=pl.CostEstimate(
            flops=6 * toks * step_rows * own_width * blocks,
            bytes_accessed=6 * step_rows * own_width * blocks,
            transcendentals=0,
        ),
        name="weight_pass",
    )(*packs, rows, *before, *after)


def add_arrived(kept_ref, gain_ref, arrived, extra, held, gain_out_ref):
    gain = gain_ref[...] + (extra[0:1] + extra[1:2])
    held[...] = kept_ref[...] + arrived
    gain_out_ref[...] = gain
    return gain


def fold_kernel(
    kept_ref, gain_ref, arrived_ref, _, keep_ref, gain_out_ref, send_ref, send_gain_ref, held
):
    count = kept_ref.shape[0]
    arrived = arrived_ref[...].astype(jnp.float32)
    gain = add_arrived(kept_ref, gain_ref, arrived[:count], arrived[count:], held, gain_out_ref)
    keep_ref[...] = held[: count // 2, :]
    send_ref[...] = held[count // 2 :, :].astype(jnp.bfloat16)
    send_gain_ref[:1, :] = high_part(gain)
    send_gain_ref[1:, :] = low_part(gain)


def spread_kernel(rows, kept_ref, gain_ref, arrived_ref, extra_ref, _, own_ref, gain_out_ref, *refs):
    outs, held = refs[:-1], refs[-1]
    arrived, extra = arrived_ref[...].astype(jnp.float32), extra_ref[...].astype(jnp.float32)
    gain = add_arrived(kept_ref, gain_ref, arrived, extra, held, gain_out_ref)
    own_ref[...] = held[:rows, :]
    for k, out in enumerate(outs):
        out[:rows, :] = held[rows * (k + 1) : rows * (k + 2), :].astype(jnp.bfloat16)
        out[rows : rows + 1, :] = high_part(gain)
        out[rows + 1 :, :] = low_part(gain)


def add_rows(kernel, kept, gain, arrived, written, kept_rows, sent_rows, name):
    count, model = kept.shape
    return pl.pallas_call(
        kernel,
        out_shape=(
            jax.ShapeDtypeStruct((kept_rows, model), jnp.float32),
            jax.ShapeDtypeStruct((1, model), jnp.float32),
        )
        + tuple(jax.ShapeDtypeStruct((n, model), jnp.bfloat16) for n in sent_rows),
        in_specs=[VMEM_SPEC] * (2 + len(arrived)) + [ANY_SPEC],
        out_specs=(VMEM_SPEC,) * (2 + len(sent_rows)),
        scratch_shapes=[pltpu.VMEM((count, model), jnp.float32)],
        compiler_params=pltpu.CompilerParams(vmem_limit_bytes=8 * MIB),
        name=name,
    )(kept, gain, *arrived, written)


def finish_kernel(rows, tokens_ref, incoming_ref, norm_gain_ref, own_ref, gain_ref, *refs):
    pieces, input_ref, gain_out_ref = refs[:-2], refs[-2], refs[-1]
    grad_normed, gain = own_ref[...], gain_ref[...]
    for piece in pieces:
        value = piece[...].astype(jnp.float32)
        grad_normed = grad_normed + value[:rows]
        gain = gain + (value[rows : rows + 1] + value[rows + 1 : rows + 2])
    gain_out_ref[...] = gain
    values = tokens_ref[...].astype(jnp.float32)
    inverse = lax.rsqrt(jnp.mean(values * values, axis=-1, keepdims=True) + EPSILON)
    scaled = values * inverse
    grad_scaled = grad_normed * norm_gain_ref[...]
    projected = jnp.mean(grad_scaled * scaled, axis=-1, keepdims=True)
    result = incoming_ref[...].astype(jnp.float32) + inverse * (grad_scaled - scaled * projected)
    input_ref[...] = result.astype(jnp.bfloat16)


def finish(rows, tokens, incoming, norm_gain, own, gain, pieces):
    model = tokens.shape[1]
    return pl.pallas_call(
        functools.partial(finish_kernel, rows),
        out_shape=(
            jax.ShapeDtypeStruct((rows, model), jnp.bfloat16),
            jax.ShapeDtypeStruct((1, model), jnp.float32),
        ),
        in_specs=[VMEM_SPEC] * (5 + len(pieces)),
        out_specs=(VMEM_SPEC,) * 2,
        compiler_params=pltpu.CompilerParams(vmem_limit_bytes=8 * MIB),
        name="finish",
    )(tokens, incoming, norm_gain, own, gain, *pieces)


def small_body(tokens, norm_gain, gate_weight, up_weight, down_weight, cotangent):
    rows, model = tokens.shape[1] * tokens.shape[2], tokens.shape[3]
    ffw = down_weight.shape[0]
    tp_count = lax.axis_size("tp")
    own_tokens, own_incoming = tokens.reshape(rows, model), cotangent.reshape(rows, model)
    gain_hbm = norm_gain.reshape(1, model)

    weights = (gate_weight.T, up_weight.T, down_weight)
    step_rows = 160
    blocks = ffw // 2 // step_rows
    piece = jnp.concatenate([own_tokens, own_incoming], axis=0)
    near = exchange(piece, "tp", 1)
    along = [exchange(piece, "tp", bits) for bits in ALONG_Z]
    fetched, gain_row, done = fetch_weights(weights, gain_hbm, 0, (piece,))
    along = relay(along, done)
    across = [exchange(arrived, "tp", 1) for arrived in along]
    more, _, done = fetch_weights(weights, gain_hbm, 1, (along[0],))
    own = sort_rows(rows, [piece, *along, near, *across], done)
    peer = exchange(own, "dp", 1)
    packed, kept, send, gain, all_rows = hidden_pass(own, peer, gain_row, weights, [fetched, more])
    arrived = exchange(send, "dp", 1)
    peer_packed = exchange(packed, "dp", 1)
    cut, turn = blocks // 2, blocks // 3
    *grads, written = weight_pass([packed], all_rows, ffw, step_rows, [(False, 0, cut)])
    kept, gain, send, send_gain = add_rows(
        fold_kernel, kept, gain, [arrived], written, kept.shape[0] // 2, (kept.shape[0] // 2, 2), "fold"
    )
    arrived = [exchange(send, "tp", 1), exchange(send_gain, "tp", 1)]
    *grads, written = weight_pass(
        [packed, peer_packed], all_rows, ffw, step_rows,
        [(False, cut, blocks), (True, 0, turn)], grads, (send,),
    )
    kept, gain, *sends = add_rows(
        functools.partial(spread_kernel, rows), kept, gain, arrived, written, rows, (rows + 2,) * 3,
        "spread",
    )
    arrived = [exchange(send, "tp", bits) for send, bits in zip(sends, ALONG_Z)]
    gate_t, up_t, down_grad, _ = weight_pass(
        [peer_packed], all_rows, ffw, step_rows, [(True, turn, blocks)], grads, (sends[0],)
    )
    input_rows, gain_grad = finish(
        rows, own_tokens, own_incoming, gain_row, kept, gain, arrived
    )
    return (
        input_rows.reshape(tokens.shape),
        gain_grad.reshape(model),
        gate_t.T,
        up_t.T,
        down_grad,
    )


def body(tokens, norm_gain, gate_weight, up_weight, down_weight, cotangent):
    tp_count, dp_count = lax.axis_size("tp"), lax.axis_size("dp")
    ffw, model = down_weight.shape
    toks = tokens.shape[1] * tokens.shape[2] * tp_count * dp_count
    small = (
        dp_count == 2
        and tp_count == 8
        and toks == 32
        and model % 1024 == 0
        and ffw % 320 == 0
        and 3 * ffw * model <= 40 * MIB
    )
    chosen = small_body if small else general_body
    return chosen(tokens, norm_gain, gate_weight, up_weight, down_weight, cotangent)


def solution(mesh):
    placed = (
        P(("groups", "dp"), None, "tp", None),
        P(),
        P(None, "tp"),
        P(None, "tp"),
        P("tp", None),
        P(("groups", "dp"), None, "tp", None),
    )
    return jax.shard_map(
        body,
        mesh=mesh,
        in_specs=placed,
        out_specs=(
            P(("groups", "dp"), None, "tp", None),
            P("groups"),
            P(("groups", "dp"), "tp"),
            P(("groups", "dp"), "tp"),
            P("tp", ("groups", "dp")),
        ),
        check_vma=False,
    )
```

```python
import functools

import jax
import jax.numpy as jnp
from jax import lax
from jax.experimental import pallas as pl
from jax.experimental.pallas import tpu as pltpu
from jax.sharding import PartitionSpec as P

EPSILON = 1e-06
LANES = 128
MIB = 1 << 20
CHUNK = 1024
ALONG_Z = (2, 4, 6)


def contract(left, right, left_dim, right_dim):
    return lax.dot_general(
        left, right, (((left_dim,), (right_dim,)), ((), ())), preferred_element_type=jnp.float32
    )


def norm_tokens(values_in, norm_gain):
    values = values_in.astype(jnp.float32)
    inverse = lax.rsqrt(jnp.mean(values * values, axis=-1, keepdims=True) + EPSILON)
    scaled = values * inverse
    return (scaled, inverse, (scaled * norm_gain).astype(jnp.bfloat16))


def local_pass(normed_all, grads_all, gate_weight, up_weight, down_weight):
    gate_value = jnp.dot(normed_all, gate_weight, preferred_element_type=jnp.float32)
    up_value = jnp.dot(normed_all, up_weight, preferred_element_type=jnp.float32)
    sigmoid_gate = jax.nn.sigmoid(gate_value)
    active = gate_value * sigmoid_gate
    hidden = (active * up_value).astype(jnp.bfloat16)
    grad_hidden = contract(grads_all, down_weight, 1, 1)
    grad_gate = (
        grad_hidden * up_value * sigmoid_gate * (1.0 + gate_value * (1.0 - sigmoid_gate))
    ).astype(jnp.bfloat16)
    grad_up = (grad_hidden * active).astype(jnp.bfloat16)
    partial_value = contract(grad_gate, gate_weight, 1, 1) + contract(grad_up, up_weight, 1, 1)
    gate_term = contract(normed_all, grad_gate, 0, 0)
    up_term = contract(normed_all, grad_up, 0, 0)
    down_term = contract(hidden, grads_all, 0, 0)
    return (partial_value, gate_term, up_term, down_term)


def general_body(tokens, norm_gain, gate_weight, up_weight, down_weight, cotangent):
    micro_count, own_tokens, model_width = (tokens.shape[1], tokens.shape[2], tokens.shape[3])
    tp_count = lax.axis_size("tp")
    scaled, inverse, normed = norm_tokens(tokens[0], norm_gain)
    normed_all, grads_all = (
        lax.all_gather(normed, "tp", axis=1, tiled=True),
        lax.all_gather(cotangent[0], "tp", axis=1, tiled=True),
    )
    partial_value, gate_term, up_term, down_term = local_pass(
        normed_all.reshape(-1, model_width),
        grads_all.reshape(-1, model_width),
        gate_weight,
        up_weight,
        down_weight,
    )
    pieces = lax.all_to_all(
        partial_value.reshape(micro_count, tp_count, own_tokens, model_width),
        "tp",
        split_axis=1,
        concat_axis=1,
        tiled=True,
    )
    grad_normed = jnp.sum(pieces, axis=1)
    grad_scaled = grad_normed * norm_gain
    projected = jnp.mean(grad_scaled * scaled, axis=-1, keepdims=True)
    input_rows = cotangent[0].astype(jnp.float32) + inverse * (grad_scaled - scaled * projected)
    gain_term = jnp.sum((grad_normed * scaled).reshape(-1, model_width), axis=0)
    gain_grad = lax.psum(gain_term, ("tp", "dp"))
    gate_grad, up_grad, down_grad = (
        lax.psum_scatter(gate_term.astype(jnp.bfloat16), "dp", scatter_dimension=0, tiled=True),
        lax.psum_scatter(up_term.astype(jnp.bfloat16), "dp", scatter_dimension=0, tiled=True),
        lax.psum_scatter(down_term.astype(jnp.bfloat16), "dp", scatter_dimension=1, tiled=True),
    )
    return (input_rows.astype(jnp.bfloat16)[None], gain_grad, gate_grad, up_grad, down_grad)


VMEM_SPEC = pl.BlockSpec(memory_space=pltpu.VMEM)
ANY_SPEC = pl.BlockSpec(memory_space=pl.ANY)


def exchange(value, axis, bits):
    count = lax.axis_size(axis)
    return lax.ppermute(value, axis, [(i, i ^ bits) for i in range(count)])


def high_part(value):
    return value.astype(jnp.bfloat16)


def low_part(value):
    return (value - value.astype(jnp.bfloat16).astype(jnp.float32)).astype(jnp.bfloat16)


def relay_kernel(*refs):
    count = len(refs) // 2
    for source, target in zip(refs[:count], refs[count + 1 :]):
        target[...] = source[...]


def relay(pieces, fetched):
    return pl.pallas_call(
        relay_kernel,
        out_shape=tuple(jax.ShapeDtypeStruct(piece.shape, piece.dtype) for piece in pieces),
        in_specs=[VMEM_SPEC] * len(pieces) + [ANY_SPEC],
        out_specs=(VMEM_SPEC,) * len(pieces),
        compiler_params=pltpu.CompilerParams(vmem_limit_bytes=4 * MIB),
        name="relay",
    )(*pieces, fetched)


def sort_kernel(rows, *refs):
    pieces, out_ref, held = refs[:-3], refs[-2], refs[-1]
    count = len(pieces)
    for k, piece in enumerate(pieces):
        value = piece[...].astype(jnp.float32)
        held[rows * k : rows * (k + 1), :] = value[:rows]
        held[rows * (count + k) : rows * (count + k + 1), :] = value[rows:]
    out_ref[...] = held[...].astype(jnp.bfloat16)


def sort_rows(rows, pieces, fetched):
    shape = (2 * rows * len(pieces), pieces[0].shape[1])
    return pl.pallas_call(
        functools.partial(sort_kernel, rows),
        out_shape=jax.ShapeDtypeStruct(shape, jnp.bfloat16),
        in_specs=[VMEM_SPEC] * len(pieces) + [ANY_SPEC],
        out_specs=VMEM_SPEC,
        scratch_shapes=[pltpu.VMEM(shape, jnp.float32)],
        compiler_params=pltpu.CompilerParams(vmem_limit_bytes=8 * MIB),
        name="sort_rows",
    )(*pieces, fetched)


def padded(count):
    return -(-count // LANES) * LANES


def chunk_copies(sources, chunk, pair_ref, down_ref, sems):
    wide, width = down_ref.shape
    half = sources[2].shape[0] // 2
    top = pl.multiple_of(lax.axis_index("dp") * half, 16)
    start = chunk * width
    at = pl.ds(start if isinstance(start, int) else pl.multiple_of(start, LANES), width)
    targets = (pair_ref.at[pl.ds(0, half)], pair_ref.at[pl.ds(wide, half)], down_ref.at[pl.ds(0, half)])
    return [
        pltpu.make_async_copy(source.at[pl.ds(top, half), at], target, sems.at[w])
        for w, (source, target) in enumerate(zip(sources, targets))
    ]


def clear_between(pair_ref, down_ref, half):
    wide, width = down_ref.shape
    if wide > half:
        zeros = jnp.zeros((wide - half, width), jnp.bfloat16)
        pair_ref[half:wide, :] = zeros
        pair_ref[wide + half :, :] = zeros


def fetch_kernel(chunk, *refs):
    sources, gain_hbm = refs[:3], refs[3]
    pair_ref, down_ref, gain_ref, done_ref, sems, gain_sem = refs[-6:]
    copies = [pltpu.make_async_copy(gain_hbm, gain_ref, gain_sem)]
    copies += chunk_copies(sources, chunk, pair_ref, down_ref, sems)
    for copy in copies:
        copy.start()
    done_ref[...] = jnp.zeros_like(done_ref)
    clear_between(pair_ref, down_ref, sources[2].shape[0] // 2)
    for copy in copies:
        copy.wait()


def in_hbm(arrays):
    return [pltpu.with_memory_space_constraint(x, pltpu.HBM) for x in arrays]


def fetch_weights(weights, gain, chunk, after=()):
    half = weights[2].shape[0] // 2
    pair, down, gain, done = pl.pallas_call(
        functools.partial(fetch_kernel, chunk),
        out_shape=(
            pltpu.VMEM((2 * padded(half), CHUNK), jnp.bfloat16),
            pltpu.VMEM((padded(half), CHUNK), jnp.bfloat16),
            pltpu.VMEM(gain.shape, gain.dtype),
            pltpu.VMEM((8, LANES), jnp.float32),
        ),
        in_specs=[ANY_SPEC] * (4 + len(after)),
        out_specs=(VMEM_SPEC,) * 4,
        scratch_shapes=[pltpu.SemaphoreType.DMA((3,)), pltpu.SemaphoreType.DMA(())],
        compiler_params=pltpu.CompilerParams(vmem_limit_bytes=4 * MIB),
        cost_estimate=pl.CostEstimate(
            flops=0, bytes_accessed=6 * half * CHUNK, transcendentals=0
        ),
        name="fetch_weights",
    )(*in_hbm((*weights, gain)), *after)
    return (pair, down), gain, done


def hidden_kernel(ready, own_ref, peer_ref, gain_ref, *refs):
    sources, fetched, refs = refs[:3], refs[3 : 3 + 2 * ready], refs[3 + 2 * ready :]
    packed_ref, mine_ref, theirs_ref, gain_part_ref, rows_ref = refs[:5]
    pair_buf, down_buf, acc, acc_grad, left, inverse_buf, sems = refs[5:]
    rest, wide, width = down_buf.shape
    toks, half = acc.shape[1], packed_ref.shape[0]
    each, model = toks // 2, rows_ref.shape[1]

    def copies(c):
        return chunk_copies(sources, ready + c, pair_buf.at[c], down_buf.at[c], sems.at[c])

    for c in range(rest):
        for copy in copies(c):
            copy.start()
    for c in range(rest):
        clear_between(pair_buf.at[c], down_buf.at[c], half)

    squares = jnp.zeros((toks, 1), jnp.float32)
    pieces = [slice(at, at + 512) for at in range(0, model, 512)]
    for at in pieces:
        value = jnp.concatenate([own_ref[:each, at], peer_ref[:each, at]], axis=0)
        value = value.astype(jnp.float32)
        squares = squares + jnp.sum(value * value, axis=-1, keepdims=True)
    inverse = lax.rsqrt(squares / model + EPSILON)
    inverse_buf[...] = jnp.broadcast_to(inverse, inverse_buf.shape)
    for at in pieces:
        value = jnp.concatenate([own_ref[:each, at], peer_ref[:each, at]], axis=0)
        normed = (value.astype(jnp.float32) * inverse * gain_ref[:, at]).astype(jnp.bfloat16)
        rows_ref[:toks, at] = normed
        rows_ref[toks:, at] = jnp.concatenate([own_ref[each:, at], peer_ref[each:, at]], axis=0)
    acc[...] = jnp.zeros_like(acc)
    acc_grad[...] = jnp.zeros_like(acc_grad)

    def forward(pair_ref, down_ref, at):
        right = rows_ref[:toks, at]
        acc[:half, :] += contract(pair_ref[:half, :], right, 1, 1)
        acc[wide : wide + half, :] += contract(pair_ref[wide : wide + half, :], right, 1, 1)
        acc_grad[:half, :] += contract(down_ref[:half, :], rows_ref[toks:, at], 1, 1)

    def backward(pair_ref, at):
        part = jnp.dot(left[...], pair_ref[...], preferred_element_type=jnp.float32)
        value = jnp.concatenate([own_ref[:each, at], peer_ref[:each, at]], axis=0)
        scaled = value.astype(jnp.float32) * inverse_buf[:, :1]
        gain = jnp.sum(part * scaled, axis=0, keepdims=True)
        gain_part_ref[:, at] = gain
        mine_ref[:, at] = part[:each]
        theirs_ref[:each, at] = part[each:].astype(jnp.bfloat16)
        theirs_ref[each : each + 1, at] = high_part(gain)
        theirs_ref[each + 1 : each + 2, at] = low_part(gain)

    def place(c):
        return pl.ds(pl.multiple_of((ready + c) * width, LANES), width)

    for c in range(ready):
        forward(fetched[2 * c], fetched[2 * c + 1], pl.ds(c * width, width))

    def forward_step(c, carry):
        for copy in copies(c):
            copy.wait()
        forward(pair_buf.at[c], down_buf.at[c], place(c))
        return carry

    lax.fori_loop(0, rest, forward_step, 0)

    for first in range(0, wide, LANES):
        at = slice(first, first + LANES)
        up_at = slice(wide + first, wide + first + LANES)
        gate, up, grad = acc[at, :].T, acc[up_at, :].T, acc_grad[at, :].T
        sigmoid = jax.nn.sigmoid(gate)
        active = gate * sigmoid
        grad_gate = grad * up * sigmoid * (1.0 + gate * (1.0 - sigmoid))
        grad_up = grad * active
        left[:, at] = grad_gate.astype(jnp.bfloat16)
        left[:, up_at] = grad_up.astype(jnp.bfloat16)
        parts = [grad_gate, grad_up, active * up, jnp.zeros_like(active)]
        columns = jnp.concatenate(parts, axis=0).T.astype(jnp.bfloat16)
        last = min(first + LANES, half)
        packed_ref[first:last, :] = columns[: last - first]

    for c in range(ready):
        backward(fetched[2 * c], pl.ds(c * width, width))

    def backward_step(c, carry):
        backward(pair_buf.at[c], place(c))
        return carry

    lax.fori_loop(0, rest, backward_step, 0)


def hidden_pass(own, peer, gain, weights, fetched):
    toks, model = own.shape
    each, half = toks // 2, weights[2].shape[0] // 2
    wide, rest = padded(half), model // CHUNK - len(fetched)
    ready = [pltpu.with_memory_space_constraint(x, pltpu.VMEM) for part in fetched for x in part]
    return pl.pallas_call(
        functools.partial(hidden_kernel, len(fetched)),
        out_shape=(
            jax.ShapeDtypeStruct((half, LANES), jnp.bfloat16),
            jax.ShapeDtypeStruct((each, model), jnp.float32),
            jax.ShapeDtypeStruct((each + 2, model), jnp.bfloat16),
            jax.ShapeDtypeStruct((1, model), jnp.float32),
            jax.ShapeDtypeStruct((2 * toks, model), jnp.bfloat16),
        ),
        in_specs=[VMEM_SPEC] * 3 + [ANY_SPEC] * 3 + [VMEM_SPEC] * len(ready),
        out_specs=(VMEM_SPEC,) * 5,
        scratch_shapes=[
            pltpu.VMEM((rest, 2 * wide, CHUNK), jnp.bfloat16),
            pltpu.VMEM((rest, wide, CHUNK), jnp.bfloat16),
            pltpu.VMEM((2 * wide, toks), jnp.float32),
            pltpu.VMEM((wide, toks), jnp.float32),
            pltpu.VMEM((toks, 2 * wide), jnp.bfloat16),
            pltpu.VMEM((toks, LANES), jnp.float32),
            pltpu.SemaphoreType.DMA((rest, 3)),
        ],
        compiler_params=pltpu.CompilerParams(vmem_limit_bytes=32 * MIB),
        cost_estimate=pl.CostEstimate(
            flops=10 * toks * half * model, bytes_accessed=6 * half * model, transcendentals=half * toks
        ),
        name="hidden_pass",
    )(own, peer, gain, *in_hbm(weights), *ready)


def weight_kernel(toks, spans, packs, *refs):
    rows_ref, refs = refs[packs], refs[:packs] + refs[packs + 1 :]
    outs, written_ref, buf, right_buf, sems = refs[-7:-4], *refs[-4:]
    slots, _, rows, own_width = buf.shape
    half, each = outs[0].shape[0] // 2, toks // 2
    place = lax.axis_index("dp")
    written_ref[...] = jnp.zeros_like(written_ref)
    own = pl.ds(pl.multiple_of(place * own_width, LANES), own_width)

    def copy(k, slot, row):
        target = outs[k].at[pl.ds(pl.multiple_of(row, 16), rows)]
        return pltpu.make_async_copy(buf.at[slot, k], target, sems.at[slot, k])

    done = 0
    for packed_ref, (swapped, first, last) in zip(refs[:packs], spans):
        top = (1 - place) * half if swapped else place * half
        if swapped:
            for at in (0, toks):
                mine, theirs = rows_ref[at : at + each, own], rows_ref[at + each : at + toks, own]
                right_buf[at : at + toks, :] = jnp.concatenate([theirs, mine], axis=0)
        else:
            right_buf[...] = rows_ref[:, own]

        def step(i, carry, packed_ref=packed_ref, top=top, base=done - first):
            slot = lax.rem(base + i, slots)

            @pl.when(base + i >= slots)
            def _():
                for k in range(3):
                    copy(k, slot, top + i * rows).wait()

            normed, incoming = right_buf[:toks, :], right_buf[toks:, :]
            at = pl.ds(pl.multiple_of(i * rows, 16), rows)
            for k, right in enumerate((normed, normed, incoming)):
                left = packed_ref[at, :][:, k * toks : (k + 1) * toks]
                value = jnp.dot(left, right, preferred_element_type=jnp.float32)
                buf[slot, k] = value.astype(jnp.bfloat16)
                copy(k, slot, top + i * rows).start()
            return carry

        lax.fori_loop(first, last, step, 0)
        done += last - first
    for slot in range(min(slots, done)):
        for k in range(3):
            copy(k, slot, place * half).wait()


def weight_pass(packs, rows, ffw, step_rows, spans, before=(), after=()):
    toks, model = rows.shape[0] // 2, rows.shape[1]
    own_width = model // 2
    blocks = sum(last - first for _, first, last in spans)
    out = jax.ShapeDtypeStruct((ffw, own_width), jnp.bfloat16)
    return pl.pallas_call(
        functools.partial(weight_kernel, toks, spans, len(packs)),
        out_shape=(out,) * 3 + (jax.ShapeDtypeStruct((8, LANES), jnp.float32),),
        in_specs=[VMEM_SPEC] * (len(packs) + 1) + [ANY_SPEC] * (len(before) + len(after)),
        out_specs=(ANY_SPEC,) * 3 + (VMEM_SPEC,),
        scratch_shapes=[
            pltpu.VMEM((3, 3, step_rows, own_width), jnp.bfloat16),
            pltpu.VMEM((2 * toks, own_width), jnp.bfloat16),
            pltpu.SemaphoreType.DMA((3, 3)),
        ],
        input_output_aliases={len(packs) + 1 + i: i for i in range(len(before))},
        compiler_params=pltpu.CompilerParams(vmem_limit_bytes=16 * MIB),
        cost_estimate=pl.CostEstimate(
            flops=6 * toks * step_rows * own_width * blocks,
            bytes_accessed=6 * step_rows * own_width * blocks,
            transcendentals=0,
        ),
        name="weight_pass",
    )(*packs, rows, *before, *after)


def add_arrived(kept_ref, gain_ref, arrived, extra, held, gain_out_ref):
    gain = gain_ref[...] + (extra[0:1] + extra[1:2])
    held[...] = kept_ref[...] + arrived
    gain_out_ref[...] = gain
    return gain


def fold_kernel(
    kept_ref, gain_ref, arrived_ref, _, keep_ref, gain_out_ref, send_ref, send_gain_ref, held
):
    count = kept_ref.shape[0]
    arrived = arrived_ref[...].astype(jnp.float32)
    gain = add_arrived(kept_ref, gain_ref, arrived[:count], arrived[count:], held, gain_out_ref)
    keep_ref[...] = held[: count // 2, :]
    send_ref[...] = held[count // 2 :, :].astype(jnp.bfloat16)
    send_gain_ref[:1, :] = high_part(gain)
    send_gain_ref[1:, :] = low_part(gain)


def spread_kernel(rows, kept_ref, gain_ref, arrived_ref, extra_ref, _, own_ref, gain_out_ref, *refs):
    outs, held = refs[:-1], refs[-1]
    arrived, extra = arrived_ref[...].astype(jnp.float32), extra_ref[...].astype(jnp.float32)
    gain = add_arrived(kept_ref, gain_ref, arrived, extra, held, gain_out_ref)
    own_ref[...] = held[:rows, :]
    for k, out in enumerate(outs):
        out[:rows, :] = held[rows * (k + 1) : rows * (k + 2), :].astype(jnp.bfloat16)
        out[rows : rows + 1, :] = high_part(gain)
        out[rows + 1 :, :] = low_part(gain)


def add_rows(kernel, kept, gain, arrived, written, kept_rows, sent_rows, name):
    count, model = kept.shape
    return pl.pallas_call(
        kernel,
        out_shape=(
            jax.ShapeDtypeStruct((kept_rows, model), jnp.float32),
            jax.ShapeDtypeStruct((1, model), jnp.float32),
        )
        + tuple(jax.ShapeDtypeStruct((n, model), jnp.bfloat16) for n in sent_rows),
        in_specs=[VMEM_SPEC] * (2 + len(arrived)) + [ANY_SPEC],
        out_specs=(VMEM_SPEC,) * (2 + len(sent_rows)),
        scratch_shapes=[pltpu.VMEM((count, model), jnp.float32)],
        compiler_params=pltpu.CompilerParams(vmem_limit_bytes=8 * MIB),
        name=name,
    )(kept, gain, *arrived, written)


def finish_kernel(rows, tokens_ref, incoming_ref, norm_gain_ref, own_ref, gain_ref, *refs):
    pieces, input_ref, gain_out_ref = refs[:-2], refs[-2], refs[-1]
    grad_normed, gain = own_ref[...], gain_ref[...]
    for piece in pieces:
        value = piece[...].astype(jnp.float32)
        grad_normed = grad_normed + value[:rows]
        gain = gain + (value[rows : rows + 1] + value[rows + 1 : rows + 2])
    gain_out_ref[...] = gain
    values = tokens_ref[...].astype(jnp.float32)
    inverse = lax.rsqrt(jnp.mean(values * values, axis=-1, keepdims=True) + EPSILON)
    scaled = values * inverse
    grad_scaled = grad_normed * norm_gain_ref[...]
    projected = jnp.mean(grad_scaled * scaled, axis=-1, keepdims=True)
    result = incoming_ref[...].astype(jnp.float32) + inverse * (grad_scaled - scaled * projected)
    input_ref[...] = result.astype(jnp.bfloat16)


def finish(rows, tokens, incoming, norm_gain, own, gain, pieces):
    model = tokens.shape[1]
    return pl.pallas_call(
        functools.partial(finish_kernel, rows),
        out_shape=(
            jax.ShapeDtypeStruct((rows, model), jnp.bfloat16),
            jax.ShapeDtypeStruct((1, model), jnp.float32),
        ),
        in_specs=[VMEM_SPEC] * (5 + len(pieces)),
        out_specs=(VMEM_SPEC,) * 2,
        compiler_params=pltpu.CompilerParams(vmem_limit_bytes=8 * MIB),
        name="finish",
    )(tokens, incoming, norm_gain, own, gain, *pieces)


def small_body(tokens, norm_gain, gate_weight, up_weight, down_weight, cotangent):
    rows, model = tokens.shape[1] * tokens.shape[2], tokens.shape[3]
    ffw = down_weight.shape[0]
    tp_count = lax.axis_size("tp")
    own_tokens, own_incoming = tokens.reshape(rows, model), cotangent.reshape(rows, model)
    gain_hbm = norm_gain.reshape(1, model)

    weights = (gate_weight.T, up_weight.T, down_weight)
    step_rows = 160
    blocks = ffw // 2 // step_rows
    piece = jnp.concatenate([own_tokens, own_incoming], axis=0)
    near = exchange(piece, "tp", 1)
    along = [exchange(piece, "tp", bits) for bits in ALONG_Z]
    fetched, gain_row, done = fetch_weights(weights, gain_hbm, 0, (piece,))
    along = relay(along, done)
    across = [exchange(arrived, "tp", 1) for arrived in along]
    more, _, done = fetch_weights(weights, gain_hbm, 1, (along[0],))
    own = sort_rows(rows, [piece, *along, near, *across], done)
    peer = exchange(own, "dp", 1)
    packed, kept, send, gain, all_rows = hidden_pass(own, peer, gain_row, weights, [fetched, more])
    arrived = exchange(send, "dp", 1)
    peer_packed = exchange(packed, "dp", 1)
    cut, turn = blocks // 2, blocks // 3
    *grads, written = weight_pass([packed], all_rows, ffw, step_rows, [(False, 0, cut)])
    kept, gain, send, send_gain = add_rows(
        fold_kernel, kept, gain, [arrived], written, kept.shape[0] // 2, (kept.shape[0] // 2, 2), "fold"
    )
    arrived = [exchange(send, "tp", 1), exchange(send_gain, "tp", 1)]
    *grads, written = weight_pass(
        [packed, peer_packed], all_rows, ffw, step_rows,
        [(False, cut, blocks), (True, 0, turn)], grads, (send,),
    )
    kept, gain, *sends = add_rows(
        functools.partial(spread_kernel, rows), kept, gain, arrived, written, rows, (rows + 2,) * 3,
        "spread",
    )
    arrived = [exchange(send, "tp", bits) for send, bits in zip(sends, ALONG_Z)]
    gate_t, up_t, down_grad, _ = weight_pass(
        [peer_packed], all_rows, ffw, step_rows, [(True, turn, blocks)], grads, (sends[0],)
    )
    input_rows, gain_grad = finish(
        rows, own_tokens, own_incoming, gain_row, kept, gain, arrived
    )
    return (
        input_rows.reshape(tokens.shape),
        gain_grad.reshape(model),
        gate_t.T,
        up_t.T,
        down_grad,
    )


def body(tokens, norm_gain, gate_weight, up_weight, down_weight, cotangent):
    tp_count, dp_count = lax.axis_size("tp"), lax.axis_size("dp")
    ffw, model = down_weight.shape
    toks = tokens.shape[1] * tokens.shape[2] * tp_count * dp_count
    small = (
        dp_count == 2
        and tp_count == 8
        and toks == 32
        and model % 1024 == 0
        and ffw % 320 == 0
        and 3 * ffw * model <= 40 * MIB
    )
    chosen = small_body if small else general_body
    return chosen(tokens, norm_gain, gate_weight, up_weight, down_weight, cotangent)


def solution(mesh):
    placed = (
        P(("groups", "dp"), None, "tp", None),
        P(),
        P(None, "tp"),
        P(None, "tp"),
        P("tp", None),
        P(("groups", "dp"), None, "tp", None),
    )
    return jax.shard_map(
        body,
        mesh=mesh,
        in_specs=placed,
        out_specs=(
            P(("groups", "dp"), None, "tp", None),
            P("groups"),
            P(("groups", "dp"), "tp"),
            P(("groups", "dp"), "tp"),
            P("tp", ("groups", "dp")),
        ),
        check_vma=False,
    )
```

```python
import functools

import jax
import jax.numpy as jnp
from jax import lax
from jax.experimental import pallas as pl
from jax.experimental.pallas import tpu as pltpu
from jax.sharding import PartitionSpec as P

EPSILON = 1e-06
LANES = 128
MIB = 1 << 20
CHUNK = 512
ALONG_Z = (2, 4, 6)


def contract(left, right, left_dim, right_dim):
    return lax.dot_general(
        left, right, (((left_dim,), (right_dim,)), ((), ())), preferred_element_type=jnp.float32
    )


def norm_tokens(values_in, norm_gain):
    values = values_in.astype(jnp.float32)
    inverse = lax.rsqrt(jnp.mean(values * values, axis=-1, keepdims=True) + EPSILON)
    scaled = values * inverse
    return (scaled, inverse, (scaled * norm_gain).astype(jnp.bfloat16))


def local_pass(normed_all, grads_all, gate_weight, up_weight, down_weight):
    gate_value = jnp.dot(normed_all, gate_weight, preferred_element_type=jnp.float32)
    up_value = jnp.dot(normed_all, up_weight, preferred_element_type=jnp.float32)
    sigmoid_gate = jax.nn.sigmoid(gate_value)
    active = gate_value * sigmoid_gate
    hidden = (active * up_value).astype(jnp.bfloat16)
    grad_hidden = contract(grads_all, down_weight, 1, 1)
    grad_gate = (
        grad_hidden * up_value * sigmoid_gate * (1.0 + gate_value * (1.0 - sigmoid_gate))
    ).astype(jnp.bfloat16)
    grad_up = (grad_hidden * active).astype(jnp.bfloat16)
    partial_value = contract(grad_gate, gate_weight, 1, 1) + contract(grad_up, up_weight, 1, 1)
    gate_term = contract(normed_all, grad_gate, 0, 0)
    up_term = contract(normed_all, grad_up, 0, 0)
    down_term = contract(hidden, grads_all, 0, 0)
    return (partial_value, gate_term, up_term, down_term)


def general_body(tokens, norm_gain, gate_weight, up_weight, down_weight, cotangent):
    micro_count, own_tokens, model_width = (tokens.shape[1], tokens.shape[2], tokens.shape[3])
    tp_count = lax.axis_size("tp")
    scaled, inverse, normed = norm_tokens(tokens[0], norm_gain)
    normed_all, grads_all = (
        lax.all_gather(normed, "tp", axis=1, tiled=True),
        lax.all_gather(cotangent[0], "tp", axis=1, tiled=True),
    )
    partial_value, gate_term, up_term, down_term = local_pass(
        normed_all.reshape(-1, model_width),
        grads_all.reshape(-1, model_width),
        gate_weight,
        up_weight,
        down_weight,
    )
    pieces = lax.all_to_all(
        partial_value.reshape(micro_count, tp_count, own_tokens, model_width),
        "tp",
        split_axis=1,
        concat_axis=1,
        tiled=True,
    )
    grad_normed = jnp.sum(pieces, axis=1)
    grad_scaled = grad_normed * norm_gain
    projected = jnp.mean(grad_scaled * scaled, axis=-1, keepdims=True)
    input_rows = cotangent[0].astype(jnp.float32) + inverse * (grad_scaled - scaled * projected)
    gain_term = jnp.sum((grad_normed * scaled).reshape(-1, model_width), axis=0)
    gain_grad = lax.psum(gain_term, ("tp", "dp"))
    gate_grad, up_grad, down_grad = (
        lax.psum_scatter(gate_term.astype(jnp.bfloat16), "dp", scatter_dimension=0, tiled=True),
        lax.psum_scatter(up_term.astype(jnp.bfloat16), "dp", scatter_dimension=0, tiled=True),
        lax.psum_scatter(down_term.astype(jnp.bfloat16), "dp", scatter_dimension=1, tiled=True),
    )
    return (input_rows.astype(jnp.bfloat16)[None], gain_grad, gate_grad, up_grad, down_grad)


VMEM_SPEC = pl.BlockSpec(memory_space=pltpu.VMEM)
ANY_SPEC = pl.BlockSpec(memory_space=pl.ANY)


def exchange(value, axis, bits):
    count = lax.axis_size(axis)
    return lax.ppermute(value, axis, [(i, i ^ bits) for i in range(count)])


def high_part(value):
    return value.astype(jnp.bfloat16)


def low_part(value):
    return (value - value.astype(jnp.bfloat16).astype(jnp.float32)).astype(jnp.bfloat16)


def relay_kernel(*refs):
    count = len(refs) // 2
    for source, target in zip(refs[:count], refs[count + 1 :]):
        target[...] = source[...]


def relay(pieces, fetched):
    return pl.pallas_call(
        relay_kernel,
        out_shape=tuple(jax.ShapeDtypeStruct(piece.shape, piece.dtype) for piece in pieces),
        in_specs=[VMEM_SPEC] * len(pieces) + [ANY_SPEC],
        out_specs=(VMEM_SPEC,) * len(pieces),
        compiler_params=pltpu.CompilerParams(vmem_limit_bytes=4 * MIB),
        name="relay",
    )(*pieces, fetched)


def sort_kernel(rows, *refs):
    pieces, out_ref, held = refs[:-3], refs[-2], refs[-1]
    count = len(pieces)
    for k, piece in enumerate(pieces):
        value = piece[...].astype(jnp.float32)
        held[rows * k : rows * (k + 1), :] = value[:rows]
        held[rows * (count + k) : rows * (count + k + 1), :] = value[rows:]
    out_ref[...] = held[...].astype(jnp.bfloat16)


def sort_rows(rows, pieces, fetched):
    shape = (2 * rows * len(pieces), pieces[0].shape[1])
    return pl.pallas_call(
        functools.partial(sort_kernel, rows),
        out_shape=jax.ShapeDtypeStruct(shape, jnp.bfloat16),
        in_specs=[VMEM_SPEC] * len(pieces) + [ANY_SPEC],
        out_specs=VMEM_SPEC,
        scratch_shapes=[pltpu.VMEM(shape, jnp.float32)],
        compiler_params=pltpu.CompilerParams(vmem_limit_bytes=8 * MIB),
        name="sort_rows",
    )(*pieces, fetched)


def padded(count):
    return -(-count // LANES) * LANES


def chunk_copies(sources, chunk, pair_ref, down_ref, sems):
    wide, width = down_ref.shape
    half = sources[2].shape[0] // 2
    top = pl.multiple_of(lax.axis_index("dp") * half, 16)
    start = chunk * width
    at = pl.ds(start if isinstance(start, int) else pl.multiple_of(start, LANES), width)
    targets = (pair_ref.at[pl.ds(0, half)], pair_ref.at[pl.ds(wide, half)], down_ref.at[pl.ds(0, half)])
    return [
        pltpu.make_async_copy(source.at[pl.ds(top, half), at], target, sems.at[w])
        for w, (source, target) in enumerate(zip(sources, targets))
    ]


def clear_between(pair_ref, down_ref, half):
    wide, width = down_ref.shape
    if wide > half:
        zeros = jnp.zeros((wide - half, width), jnp.bfloat16)
        pair_ref[half:wide, :] = zeros
        pair_ref[wide + half :, :] = zeros


def fetch_kernel(first, count, *refs):
    sources, gain_hbm = refs[:3], refs[3]
    gain_ref, done_ref, sems, gain_sem = refs[-4:]
    targets = refs[-4 - 2 * count : -4]
    copies = [pltpu.make_async_copy(gain_hbm, gain_ref, gain_sem)]
    for c in range(count):
        copies += chunk_copies(sources, first + c, *targets[2 * c : 2 * c + 2], sems.at[c])
    for copy in copies:
        copy.start()
    done_ref[...] = jnp.zeros_like(done_ref)
    for c in range(count):
        clear_between(*targets[2 * c : 2 * c + 2], sources[2].shape[0] // 2)
    for copy in copies:
        copy.wait()


def in_hbm(arrays):
    return [pltpu.with_memory_space_constraint(x, pltpu.HBM) for x in arrays]


def fetch_weights(weights, gain, first, count, after=()):
    half = weights[2].shape[0] // 2
    *chunks, gain, done = pl.pallas_call(
        functools.partial(fetch_kernel, first, count),
        out_shape=(
            pltpu.VMEM((2 * padded(half), CHUNK), jnp.bfloat16),
            pltpu.VMEM((padded(half), CHUNK), jnp.bfloat16),
        )
        * count
        + (
            pltpu.VMEM(gain.shape, gain.dtype),
            pltpu.VMEM((8, LANES), jnp.float32),
        ),
        in_specs=[ANY_SPEC] * (4 + len(after)),
        out_specs=(VMEM_SPEC,) * (2 * count + 2),
        scratch_shapes=[pltpu.SemaphoreType.DMA((count, 3)), pltpu.SemaphoreType.DMA(())],
        compiler_params=pltpu.CompilerParams(vmem_limit_bytes=4 * MIB),
        cost_estimate=pl.CostEstimate(
            flops=0, bytes_accessed=6 * half * CHUNK * count, transcendentals=0
        ),
        name="fetch_weights",
    )(*in_hbm((*weights, gain)), *after)
    return list(zip(chunks[::2], chunks[1::2])), gain, done


def hidden_kernel(ready, own_ref, peer_ref, gain_ref, *refs):
    sources, fetched, refs = refs[:3], refs[3 : 3 + 2 * ready], refs[3 + 2 * ready :]
    packed_ref, mine_ref, theirs_ref, gain_part_ref, rows_ref = refs[:5]
    pair_buf, down_buf, acc, acc_grad, left, inverse_buf, sems = refs[5:]
    rest, wide, width = down_buf.shape
    toks, half = acc.shape[1], packed_ref.shape[0]
    each, model = toks // 2, rows_ref.shape[1]

    def copies(c):
        return chunk_copies(sources, ready + c, pair_buf.at[c], down_buf.at[c], sems.at[c])

    for c in range(rest):
        for copy in copies(c):
            copy.start()
    for c in range(rest):
        clear_between(pair_buf.at[c], down_buf.at[c], half)

    squares = jnp.zeros((toks, 1), jnp.float32)
    pieces = [slice(at, at + 512) for at in range(0, model, 512)]
    for at in pieces:
        value = jnp.concatenate([own_ref[:each, at], peer_ref[:each, at]], axis=0)
        value = value.astype(jnp.float32)
        squares = squares + jnp.sum(value * value, axis=-1, keepdims=True)
    inverse = lax.rsqrt(squares / model + EPSILON)
    inverse_buf[...] = jnp.broadcast_to(inverse, inverse_buf.shape)
    for at in pieces:
        value = jnp.concatenate([own_ref[:each, at], peer_ref[:each, at]], axis=0)
        normed = (value.astype(jnp.float32) * inverse * gain_ref[:, at]).astype(jnp.bfloat16)
        rows_ref[:toks, at] = normed
        rows_ref[toks:, at] = jnp.concatenate([own_ref[each:, at], peer_ref[each:, at]], axis=0)
    acc[...] = jnp.zeros_like(acc)
    acc_grad[...] = jnp.zeros_like(acc_grad)

    def forward(pair_ref, down_ref, at):
        right = rows_ref[:toks, at]
        acc[:half, :] += contract(pair_ref[:half, :], right, 1, 1)
        acc[wide : wide + half, :] += contract(pair_ref[wide : wide + half, :], right, 1, 1)
        acc_grad[:half, :] += contract(down_ref[:half, :], rows_ref[toks:, at], 1, 1)

    def backward(pair_ref, at):
        part = jnp.dot(left[...], pair_ref[...], preferred_element_type=jnp.float32)
        value = jnp.concatenate([own_ref[:each, at], peer_ref[:each, at]], axis=0)
        scaled = value.astype(jnp.float32) * inverse_buf[:, :1]
        gain = jnp.sum(part * scaled, axis=0, keepdims=True)
        gain_part_ref[:, at] = gain
        mine_ref[:, at] = part[:each]
        theirs_ref[:each, at] = part[each:].astype(jnp.bfloat16)
        theirs_ref[each : each + 1, at] = high_part(gain)
        theirs_ref[each + 1 : each + 2, at] = low_part(gain)

    def place(c):
        return pl.ds(pl.multiple_of((ready + c) * width, LANES), width)

    for c in range(ready):
        forward(fetched[2 * c], fetched[2 * c + 1], pl.ds(c * width, width))

    def forward_step(c, carry):
        for copy in copies(c):
            copy.wait()
        forward(pair_buf.at[c], down_buf.at[c], place(c))
        return carry

    lax.fori_loop(0, rest, forward_step, 0)

    for first in range(0, wide, LANES):
        at = slice(first, first + LANES)
        up_at = slice(wide + first, wide + first + LANES)
        gate, up, grad = acc[at, :].T, acc[up_at, :].T, acc_grad[at, :].T
        sigmoid = jax.nn.sigmoid(gate)
        active = gate * sigmoid
        grad_gate = grad * up * sigmoid * (1.0 + gate * (1.0 - sigmoid))
        grad_up = grad * active
        left[:, at] = grad_gate.astype(jnp.bfloat16)
        left[:, up_at] = grad_up.astype(jnp.bfloat16)
        parts = [grad_gate, grad_up, active * up, jnp.zeros_like(active)]
        columns = jnp.concatenate(parts, axis=0).T.astype(jnp.bfloat16)
        last = min(first + LANES, half)
        packed_ref[first:last, :] = columns[: last - first]

    for c in range(ready):
        backward(fetched[2 * c], pl.ds(c * width, width))

    def backward_step(c, carry):
        backward(pair_buf.at[c], place(c))
        return carry

    lax.fori_loop(0, rest, backward_step, 0)


def hidden_pass(own, peer, gain, weights, fetched):
    toks, model = own.shape
    each, half = toks // 2, weights[2].shape[0] // 2
    wide, rest = padded(half), model // CHUNK - len(fetched)
    ready = [pltpu.with_memory_space_constraint(x, pltpu.VMEM) for part in fetched for x in part]
    return pl.pallas_call(
        functools.partial(hidden_kernel, len(fetched)),
        out_shape=(
            jax.ShapeDtypeStruct((half, LANES), jnp.bfloat16),
            jax.ShapeDtypeStruct((each, model), jnp.float32),
            jax.ShapeDtypeStruct((each + 2, model), jnp.bfloat16),
            jax.ShapeDtypeStruct((1, model), jnp.float32),
            jax.ShapeDtypeStruct((2 * toks, model), jnp.bfloat16),
        ),
        in_specs=[VMEM_SPEC] * 3 + [ANY_SPEC] * 3 + [VMEM_SPEC] * len(ready),
        out_specs=(VMEM_SPEC,) * 5,
        scratch_shapes=[
            pltpu.VMEM((rest, 2 * wide, CHUNK), jnp.bfloat16),
            pltpu.VMEM((rest, wide, CHUNK), jnp.bfloat16),
            pltpu.VMEM((2 * wide, toks), jnp.float32),
            pltpu.VMEM((wide, toks), jnp.float32),
            pltpu.VMEM((toks, 2 * wide), jnp.bfloat16),
            pltpu.VMEM((toks, LANES), jnp.float32),
            pltpu.SemaphoreType.DMA((rest, 3)),
        ],
        compiler_params=pltpu.CompilerParams(vmem_limit_bytes=32 * MIB),
        cost_estimate=pl.CostEstimate(
            flops=10 * toks * half * model, bytes_accessed=6 * half * model, transcendentals=half * toks
        ),
        name="hidden_pass",
    )(own, peer, gain, *in_hbm(weights), *ready)


def weight_kernel(toks, spans, packs, *refs):
    rows_ref, refs = refs[packs], refs[:packs] + refs[packs + 1 :]
    outs, written_ref, buf, right_buf, sems = refs[-7:-4], *refs[-4:]
    slots, _, rows, own_width = buf.shape
    half, each = outs[0].shape[0] // 2, toks // 2
    place = lax.axis_index("dp")
    written_ref[...] = jnp.zeros_like(written_ref)
    own = pl.ds(pl.multiple_of(place * own_width, LANES), own_width)

    def copy(k, slot, row):
        target = outs[k].at[pl.ds(pl.multiple_of(row, 16), rows)]
        return pltpu.make_async_copy(buf.at[slot, k], target, sems.at[slot, k])

    done = 0
    for packed_ref, (swapped, first, last) in zip(refs[:packs], spans):
        top = (1 - place) * half if swapped else place * half
        if swapped:
            for at in (0, toks):
                mine, theirs = rows_ref[at : at + each, own], rows_ref[at + each : at + toks, own]
                right_buf[at : at + toks, :] = jnp.concatenate([theirs, mine], axis=0)
        else:
            right_buf[...] = rows_ref[:, own]

        def step(i, carry, packed_ref=packed_ref, top=top, base=done - first):
            slot = lax.rem(base + i, slots)

            @pl.when(base + i >= slots)
            def _():
                for k in range(3):
                    copy(k, slot, top + i * rows).wait()

            normed, incoming = right_buf[:toks, :], right_buf[toks:, :]
            at = pl.ds(pl.multiple_of(i * rows, 16), rows)
            for k, right in enumerate((normed, normed, incoming)):
                left = packed_ref[at, :][:, k * toks : (k + 1) * toks]
                value = jnp.dot(left, right, preferred_element_type=jnp.float32)
                buf[slot, k] = value.astype(jnp.bfloat16)
                copy(k, slot, top + i * rows).start()
            return carry

        lax.fori_loop(first, last, step, 0)
        done += last - first
    for slot in range(min(slots, done)):
        for k in range(3):
            copy(k, slot, place * half).wait()


def weight_pass(packs, rows, ffw, step_rows, spans, before=(), after=()):
    toks, model = rows.shape[0] // 2, rows.shape[1]
    own_width = model // 2
    blocks = sum(last - first for _, first, last in spans)
    out = jax.ShapeDtypeStruct((ffw, own_width), jnp.bfloat16)
    return pl.pallas_call(
        functools.partial(weight_kernel, toks, spans, len(packs)),
        out_shape=(out,) * 3 + (jax.ShapeDtypeStruct((8, LANES), jnp.float32),),
        in_specs=[VMEM_SPEC] * (len(packs) + 1) + [ANY_SPEC] * (len(before) + len(after)),
        out_specs=(ANY_SPEC,) * 3 + (VMEM_SPEC,),
        scratch_shapes=[
            pltpu.VMEM((3, 3, step_rows, own_width), jnp.bfloat16),
            pltpu.VMEM((2 * toks, own_width), jnp.bfloat16),
            pltpu.SemaphoreType.DMA((3, 3)),
        ],
        input_output_aliases={len(packs) + 1 + i: i for i in range(len(before))},
        compiler_params=pltpu.CompilerParams(vmem_limit_bytes=16 * MIB),
        cost_estimate=pl.CostEstimate(
            flops=6 * toks * step_rows * own_width * blocks,
            bytes_accessed=6 * step_rows * own_width * blocks,
            transcendentals=0,
        ),
        name="weight_pass",
    )(*packs, rows, *before, *after)


def add_arrived(kept_ref, gain_ref, arrived, extra, held, gain_out_ref):
    gain = gain_ref[...] + (extra[0:1] + extra[1:2])
    held[...] = kept_ref[...] + arrived
    gain_out_ref[...] = gain
    return gain


def fold_kernel(
    kept_ref, gain_ref, arrived_ref, _, keep_ref, gain_out_ref, send_ref, send_gain_ref, held
):
    count = kept_ref.shape[0]
    arrived = arrived_ref[...].astype(jnp.float32)
    gain = add_arrived(kept_ref, gain_ref, arrived[:count], arrived[count:], held, gain_out_ref)
    keep_ref[...] = held[: count // 2, :]
    send_ref[...] = held[count // 2 :, :].astype(jnp.bfloat16)
    send_gain_ref[:1, :] = high_part(gain)
    send_gain_ref[1:, :] = low_part(gain)


def spread_kernel(rows, kept_ref, gain_ref, arrived_ref, extra_ref, _, own_ref, gain_out_ref, *refs):
    outs, held = refs[:-1], refs[-1]
    arrived, extra = arrived_ref[...].astype(jnp.float32), extra_ref[...].astype(jnp.float32)
    gain = add_arrived(kept_ref, gain_ref, arrived, extra, held, gain_out_ref)
    own_ref[...] = held[:rows, :]
    for k, out in enumerate(outs):
        out[:rows, :] = held[rows * (k + 1) : rows * (k + 2), :].astype(jnp.bfloat16)
        out[rows : rows + 1, :] = high_part(gain)
        out[rows + 1 :, :] = low_part(gain)


def add_rows(kernel, kept, gain, arrived, written, kept_rows, sent_rows, name):
    count, model = kept.shape
    return pl.pallas_call(
        kernel,
        out_shape=(
            jax.ShapeDtypeStruct((kept_rows, model), jnp.float32),
            jax.ShapeDtypeStruct((1, model), jnp.float32),
        )
        + tuple(jax.ShapeDtypeStruct((n, model), jnp.bfloat16) for n in sent_rows),
        in_specs=[VMEM_SPEC] * (2 + len(arrived)) + [ANY_SPEC],
        out_specs=(VMEM_SPEC,) * (2 + len(sent_rows)),
        scratch_shapes=[pltpu.VMEM((count, model), jnp.float32)],
        compiler_params=pltpu.CompilerParams(vmem_limit_bytes=8 * MIB),
        name=name,
    )(kept, gain, *arrived, written)


def finish_kernel(rows, tokens_ref, incoming_ref, norm_gain_ref, own_ref, gain_ref, *refs):
    pieces, input_ref, gain_out_ref = refs[:-2], refs[-2], refs[-1]
    grad_normed, gain = own_ref[...], gain_ref[...]
    for piece in pieces:
        value = piece[...].astype(jnp.float32)
        grad_normed = grad_normed + value[:rows]
        gain = gain + (value[rows : rows + 1] + value[rows + 1 : rows + 2])
    gain_out_ref[...] = gain
    values = tokens_ref[...].astype(jnp.float32)
    inverse = lax.rsqrt(jnp.mean(values * values, axis=-1, keepdims=True) + EPSILON)
    scaled = values * inverse
    grad_scaled = grad_normed * norm_gain_ref[...]
    projected = jnp.mean(grad_scaled * scaled, axis=-1, keepdims=True)
    result = incoming_ref[...].astype(jnp.float32) + inverse * (grad_scaled - scaled * projected)
    input_ref[...] = result.astype(jnp.bfloat16)


def finish(rows, tokens, incoming, norm_gain, own, gain, pieces):
    model = tokens.shape[1]
    return pl.pallas_call(
        functools.partial(finish_kernel, rows),
        out_shape=(
            jax.ShapeDtypeStruct((rows, model), jnp.bfloat16),
            jax.ShapeDtypeStruct((1, model), jnp.float32),
        ),
        in_specs=[VMEM_SPEC] * (5 + len(pieces)),
        out_specs=(VMEM_SPEC,) * 2,
        compiler_params=pltpu.CompilerParams(vmem_limit_bytes=8 * MIB),
        name="finish",
    )(tokens, incoming, norm_gain, own, gain, *pieces)


def small_body(tokens, norm_gain, gate_weight, up_weight, down_weight, cotangent):
    rows, model = tokens.shape[1] * tokens.shape[2], tokens.shape[3]
    ffw = down_weight.shape[0]
    tp_count = lax.axis_size("tp")
    own_tokens, own_incoming = tokens.reshape(rows, model), cotangent.reshape(rows, model)
    gain_hbm = norm_gain.reshape(1, model)

    weights = (gate_weight.T, up_weight.T, down_weight)
    step_rows = 160
    blocks = ffw // 2 // step_rows
    piece = jnp.concatenate([own_tokens, own_incoming], axis=0)
    near = exchange(piece, "tp", 1)
    along = [exchange(piece, "tp", bits) for bits in ALONG_Z]
    fetched, gain_row, done = fetch_weights(weights, gain_hbm, 0, 2, (piece,))
    along = relay(along, done)
    across = [exchange(arrived, "tp", 1) for arrived in along]
    more, _, done = fetch_weights(weights, gain_hbm, 2, 1, (along[0],))
    own = sort_rows(rows, [piece, *along, near, *across], done)
    peer = exchange(own, "dp", 1)
    packed, kept, send, gain, all_rows = hidden_pass(own, peer, gain_row, weights, fetched + more)
    arrived = exchange(send, "dp", 1)
    peer_packed = exchange(packed, "dp", 1)
    cut, turn = blocks // 2, blocks // 3
    *grads, written = weight_pass([packed], all_rows, ffw, step_rows, [(False, 0, cut)])
    kept, gain, send, send_gain = add_rows(
        fold_kernel, kept, gain, [arrived], written, kept.shape[0] // 2, (kept.shape[0] // 2, 2), "fold"
    )
    arrived = [exchange(send, "tp", 1), exchange(send_gain, "tp", 1)]
    *grads, written = weight_pass(
        [packed, peer_packed], all_rows, ffw, step_rows,
        [(False, cut, blocks), (True, 0, turn)], grads, (send,),
    )
    kept, gain, *sends = add_rows(
        functools.partial(spread_kernel, rows), kept, gain, arrived, written, rows, (rows + 2,) * 3,
        "spread",
    )
    arrived = [exchange(send, "tp", bits) for send, bits in zip(sends, ALONG_Z)]
    gate_t, up_t, down_grad, _ = weight_pass(
        [peer_packed], all_rows, ffw, step_rows, [(True, turn, blocks)], grads, (sends[0],)
    )
    input_rows, gain_grad = finish(
        rows, own_tokens, own_incoming, gain_row, kept, gain, arrived
    )
    return (
        input_rows.reshape(tokens.shape),
        gain_grad.reshape(model),
        gate_t.T,
        up_t.T,
        down_grad,
    )


def body(tokens, norm_gain, gate_weight, up_weight, down_weight, cotangent):
    tp_count, dp_count = lax.axis_size("tp"), lax.axis_size("dp")
    ffw, model = down_weight.shape
    toks = tokens.shape[1] * tokens.shape[2] * tp_count * dp_count
    small = (
        dp_count == 2
        and tp_count == 8
        and toks == 32
        and model % 1024 == 0
        and ffw % 320 == 0
        and 3 * ffw * model <= 40 * MIB
    )
    chosen = small_body if small else general_body
    return chosen(tokens, norm_gain, gate_weight, up_weight, down_weight, cotangent)


def solution(mesh):
    placed = (
        P(("groups", "dp"), None, "tp", None),
        P(),
        P(None, "tp"),
        P(None, "tp"),
        P("tp", None),
        P(("groups", "dp"), None, "tp", None),
    )
    return jax.shard_map(
        body,
        mesh=mesh,
        in_specs=placed,
        out_specs=(
            P(("groups", "dp"), None, "tp", None),
            P("groups"),
            P(("groups", "dp"), "tp"),
            P(("groups", "dp"), "tp"),
            P("tp", ("groups", "dp")),
        ),
        check_vma=False,
    )
```

```python
import functools

import jax
import jax.numpy as jnp
from jax import lax
from jax.experimental import pallas as pl
from jax.experimental.pallas import tpu as pltpu
from jax.sharding import PartitionSpec as P

EPSILON = 1e-06
LANES = 128
MIB = 1 << 20
CHUNK = 512
ALONG_Z = (2, 4, 6)


def contract(left, right, left_dim, right_dim):
    return lax.dot_general(
        left, right, (((left_dim,), (right_dim,)), ((), ())), preferred_element_type=jnp.float32
    )


def norm_tokens(values_in, norm_gain):
    values = values_in.astype(jnp.float32)
    inverse = lax.rsqrt(jnp.mean(values * values, axis=-1, keepdims=True) + EPSILON)
    scaled = values * inverse
    return (scaled, inverse, (scaled * norm_gain).astype(jnp.bfloat16))


def local_pass(normed_all, grads_all, gate_weight, up_weight, down_weight):
    gate_value = jnp.dot(normed_all, gate_weight, preferred_element_type=jnp.float32)
    up_value = jnp.dot(normed_all, up_weight, preferred_element_type=jnp.float32)
    sigmoid_gate = jax.nn.sigmoid(gate_value)
    active = gate_value * sigmoid_gate
    hidden = (active * up_value).astype(jnp.bfloat16)
    grad_hidden = contract(grads_all, down_weight, 1, 1)
    grad_gate = (
        grad_hidden * up_value * sigmoid_gate * (1.0 + gate_value * (1.0 - sigmoid_gate))
    ).astype(jnp.bfloat16)
    grad_up = (grad_hidden * active).astype(jnp.bfloat16)
    partial_value = contract(grad_gate, gate_weight, 1, 1) + contract(grad_up, up_weight, 1, 1)
    gate_term = contract(normed_all, grad_gate, 0, 0)
    up_term = contract(normed_all, grad_up, 0, 0)
    down_term = contract(hidden, grads_all, 0, 0)
    return (partial_value, gate_term, up_term, down_term)


def general_body(tokens, norm_gain, gate_weight, up_weight, down_weight, cotangent):
    micro_count, own_tokens, model_width = (tokens.shape[1], tokens.shape[2], tokens.shape[3])
    tp_count = lax.axis_size("tp")
    scaled, inverse, normed = norm_tokens(tokens[0], norm_gain)
    normed_all, grads_all = (
        lax.all_gather(normed, "tp", axis=1, tiled=True),
        lax.all_gather(cotangent[0], "tp", axis=1, tiled=True),
    )
    partial_value, gate_term, up_term, down_term = local_pass(
        normed_all.reshape(-1, model_width),
        grads_all.reshape(-1, model_width),
        gate_weight,
        up_weight,
        down_weight,
    )
    pieces = lax.all_to_all(
        partial_value.reshape(micro_count, tp_count, own_tokens, model_width),
        "tp",
        split_axis=1,
        concat_axis=1,
        tiled=True,
    )
    grad_normed = jnp.sum(pieces, axis=1)
    grad_scaled = grad_normed * norm_gain
    projected = jnp.mean(grad_scaled * scaled, axis=-1, keepdims=True)
    input_rows = cotangent[0].astype(jnp.float32) + inverse * (grad_scaled - scaled * projected)
    gain_term = jnp.sum((grad_normed * scaled).reshape(-1, model_width), axis=0)
    gain_grad = lax.psum(gain_term, ("tp", "dp"))
    gate_grad, up_grad, down_grad = (
        lax.psum_scatter(gate_term.astype(jnp.bfloat16), "dp", scatter_dimension=0, tiled=True),
        lax.psum_scatter(up_term.astype(jnp.bfloat16), "dp", scatter_dimension=0, tiled=True),
        lax.psum_scatter(down_term.astype(jnp.bfloat16), "dp", scatter_dimension=1, tiled=True),
    )
    return (input_rows.astype(jnp.bfloat16)[None], gain_grad, gate_grad, up_grad, down_grad)


VMEM_SPEC = pl.BlockSpec(memory_space=pltpu.VMEM)
ANY_SPEC = pl.BlockSpec(memory_space=pl.ANY)


def exchange(value, axis, bits):
    count = lax.axis_size(axis)
    return lax.ppermute(value, axis, [(i, i ^ bits) for i in range(count)])


def high_part(value):
    return value.astype(jnp.bfloat16)


def low_part(value):
    return (value - value.astype(jnp.bfloat16).astype(jnp.float32)).astype(jnp.bfloat16)


def relay_kernel(*refs):
    count = len(refs) // 2
    for source, target in zip(refs[:count], refs[count + 1 :]):
        target[...] = source[...]


def relay(pieces, fetched):
    return pl.pallas_call(
        relay_kernel,
        out_shape=tuple(jax.ShapeDtypeStruct(piece.shape, piece.dtype) for piece in pieces),
        in_specs=[VMEM_SPEC] * len(pieces) + [ANY_SPEC],
        out_specs=(VMEM_SPEC,) * len(pieces),
        compiler_params=pltpu.CompilerParams(vmem_limit_bytes=4 * MIB),
        name="relay",
    )(*pieces, fetched)


def sort_kernel(rows, *refs):
    pieces, out_ref, held = refs[:-3], refs[-2], refs[-1]
    count = len(pieces)
    for k, piece in enumerate(pieces):
        value = piece[...].astype(jnp.float32)
        held[rows * k : rows * (k + 1), :] = value[:rows]
        held[rows * (count + k) : rows * (count + k + 1), :] = value[rows:]
    out_ref[...] = held[...].astype(jnp.bfloat16)


def sort_rows(rows, pieces, fetched):
    shape = (2 * rows * len(pieces), pieces[0].shape[1])
    return pl.pallas_call(
        functools.partial(sort_kernel, rows),
        out_shape=jax.ShapeDtypeStruct(shape, jnp.bfloat16),
        in_specs=[VMEM_SPEC] * len(pieces) + [ANY_SPEC],
        out_specs=VMEM_SPEC,
        scratch_shapes=[pltpu.VMEM(shape, jnp.float32)],
        compiler_params=pltpu.CompilerParams(vmem_limit_bytes=8 * MIB),
        name="sort_rows",
    )(*pieces, fetched)


def padded(count):
    return -(-count // LANES) * LANES


def chunk_copies(sources, chunk, pair_ref, down_ref, sems):
    wide, width = down_ref.shape
    half = sources[2].shape[0] // 2
    top = pl.multiple_of(lax.axis_index("dp") * half, 16)
    start = chunk * width
    at = pl.ds(start if isinstance(start, int) else pl.multiple_of(start, LANES), width)
    targets = (pair_ref.at[pl.ds(0, half)], pair_ref.at[pl.ds(wide, half)], down_ref.at[pl.ds(0, half)])
    return [
        pltpu.make_async_copy(source.at[pl.ds(top, half), at], target, sems.at[w])
        for w, (source, target) in enumerate(zip(sources, targets))
    ]


def clear_between(pair_ref, down_ref, half):
    wide, width = down_ref.shape
    if wide > half:
        zeros = jnp.zeros((wide - half, width), jnp.bfloat16)
        pair_ref[half:wide, :] = zeros
        pair_ref[wide + half :, :] = zeros


def fetch_kernel(first, count, *refs):
    sources, gain_hbm = refs[:3], refs[3]
    gain_ref, done_ref, sems, gain_sem = refs[-4:]
    targets = refs[-4 - 2 * count : -4]
    copies = [pltpu.make_async_copy(gain_hbm, gain_ref, gain_sem)]
    for c in range(count):
        copies += chunk_copies(sources, first + c, *targets[2 * c : 2 * c + 2], sems.at[c])
    for copy in copies:
        copy.start()
    done_ref[...] = jnp.zeros_like(done_ref)
    for c in range(count):
        clear_between(*targets[2 * c : 2 * c + 2], sources[2].shape[0] // 2)
    for copy in copies:
        copy.wait()


def in_hbm(arrays):
    return [pltpu.with_memory_space_constraint(x, pltpu.HBM) for x in arrays]


def fetch_weights(weights, gain, first, count, after=()):
    half = weights[2].shape[0] // 2
    *chunks, gain, done = pl.pallas_call(
        functools.partial(fetch_kernel, first, count),
        out_shape=(
            pltpu.VMEM((2 * padded(half), CHUNK), jnp.bfloat16),
            pltpu.VMEM((padded(half), CHUNK), jnp.bfloat16),
        )
        * count
        + (
            pltpu.VMEM(gain.shape, gain.dtype),
            pltpu.VMEM((8, LANES), jnp.float32),
        ),
        in_specs=[ANY_SPEC] * (4 + len(after)),
        out_specs=(VMEM_SPEC,) * (2 * count + 2),
        scratch_shapes=[pltpu.SemaphoreType.DMA((count, 3)), pltpu.SemaphoreType.DMA(())],
        compiler_params=pltpu.CompilerParams(vmem_limit_bytes=4 * MIB),
        cost_estimate=pl.CostEstimate(
            flops=0, bytes_accessed=6 * half * CHUNK * count, transcendentals=0
        ),
        name="fetch_weights",
    )(*in_hbm((*weights, gain)), *after)
    return list(zip(chunks[::2], chunks[1::2])), gain, done


def hidden_kernel(ready, own_ref, peer_ref, gain_ref, *refs):
    sources, fetched, refs = refs[:3], refs[3 : 3 + 2 * ready], refs[3 + 2 * ready :]
    packed_ref, mine_ref, theirs_ref, gain_part_ref, rows_ref = refs[:5]
    pair_buf, down_buf, acc, acc_grad, left, inverse_buf, sems = refs[5:]
    rest, wide, width = down_buf.shape
    toks, half = acc.shape[1], packed_ref.shape[0]
    each, model = toks // 2, rows_ref.shape[1]

    def copies(c):
        return chunk_copies(sources, ready + c, pair_buf.at[c], down_buf.at[c], sems.at[c])

    for c in range(rest):
        for copy in copies(c):
            copy.start()
    for c in range(rest):
        clear_between(pair_buf.at[c], down_buf.at[c], half)

    squares = jnp.zeros((toks, 1), jnp.float32)
    pieces = [slice(at, at + 512) for at in range(0, model, 512)]
    for at in pieces:
        value = jnp.concatenate([own_ref[:each, at], peer_ref[:each, at]], axis=0)
        value = value.astype(jnp.float32)
        squares = squares + jnp.sum(value * value, axis=-1, keepdims=True)
    inverse = lax.rsqrt(squares / model + EPSILON)
    inverse_buf[...] = jnp.broadcast_to(inverse, inverse_buf.shape)
    for at in pieces:
        value = jnp.concatenate([own_ref[:each, at], peer_ref[:each, at]], axis=0)
        normed = (value.astype(jnp.float32) * inverse * gain_ref[:, at]).astype(jnp.bfloat16)
        rows_ref[:toks, at] = normed
        rows_ref[toks:, at] = jnp.concatenate([own_ref[each:, at], peer_ref[each:, at]], axis=0)
    acc[...] = jnp.zeros_like(acc)
    acc_grad[...] = jnp.zeros_like(acc_grad)

    def forward(pair_ref, down_ref, at):
        right = rows_ref[:toks, at]
        acc[:half, :] += contract(pair_ref[:half, :], right, 1, 1)
        acc[wide : wide + half, :] += contract(pair_ref[wide : wide + half, :], right, 1, 1)
        acc_grad[:half, :] += contract(down_ref[:half, :], rows_ref[toks:, at], 1, 1)

    def backward(pair_ref, at):
        part = jnp.dot(left[...], pair_ref[...], preferred_element_type=jnp.float32)
        value = jnp.concatenate([own_ref[:each, at], peer_ref[:each, at]], axis=0)
        scaled = value.astype(jnp.float32) * inverse_buf[:, :1]
        gain = jnp.sum(part * scaled, axis=0, keepdims=True)
        gain_part_ref[:, at] = gain
        mine_ref[:, at] = part[:each]
        theirs_ref[:each, at] = part[each:].astype(jnp.bfloat16)
        theirs_ref[each : each + 1, at] = high_part(gain)
        theirs_ref[each + 1 : each + 2, at] = low_part(gain)

    def place(c):
        return pl.ds(pl.multiple_of((ready + c) * width, LANES), width)

    for c in range(ready):
        forward(fetched[2 * c], fetched[2 * c + 1], pl.ds(c * width, width))

    def forward_step(c, carry):
        for copy in copies(c):
            copy.wait()
        forward(pair_buf.at[c], down_buf.at[c], place(c))
        return carry

    lax.fori_loop(0, rest, forward_step, 0)

    for first in range(0, wide, LANES):
        at = slice(first, first + LANES)
        up_at = slice(wide + first, wide + first + LANES)
        gate, up, grad = acc[at, :].T, acc[up_at, :].T, acc_grad[at, :].T
        sigmoid = jax.nn.sigmoid(gate)
        active = gate * sigmoid
        grad_gate = grad * up * sigmoid * (1.0 + gate * (1.0 - sigmoid))
        grad_up = grad * active
        left[:, at] = grad_gate.astype(jnp.bfloat16)
        left[:, up_at] = grad_up.astype(jnp.bfloat16)
        parts = [grad_gate, grad_up, active * up, jnp.zeros_like(active)]
        columns = jnp.concatenate(parts, axis=0).T.astype(jnp.bfloat16)
        last = min(first + LANES, half)
        packed_ref[first:last, :] = columns[: last - first]

    for c in range(ready):
        backward(fetched[2 * c], pl.ds(c * width, width))

    def backward_step(c, carry):
        backward(pair_buf.at[c], place(c))
        return carry

    lax.fori_loop(0, rest, backward_step, 0)


def hidden_pass(own, peer, gain, weights, fetched):
    toks, model = own.shape
    each, half = toks // 2, weights[2].shape[0] // 2
    wide, rest = padded(half), model // CHUNK - len(fetched)
    ready = [pltpu.with_memory_space_constraint(x, pltpu.VMEM) for part in fetched for x in part]
    return pl.pallas_call(
        functools.partial(hidden_kernel, len(fetched)),
        out_shape=(
            jax.ShapeDtypeStruct((half, LANES), jnp.bfloat16),
            jax.ShapeDtypeStruct((each, model), jnp.float32),
            jax.ShapeDtypeStruct((each + 2, model), jnp.bfloat16),
            jax.ShapeDtypeStruct((1, model), jnp.float32),
            jax.ShapeDtypeStruct((2 * toks, model), jnp.bfloat16),
        ),
        in_specs=[VMEM_SPEC] * 3 + [ANY_SPEC] * 3 + [VMEM_SPEC] * len(ready),
        out_specs=(VMEM_SPEC,) * 5,
        scratch_shapes=[
            pltpu.VMEM((rest, 2 * wide, CHUNK), jnp.bfloat16),
            pltpu.VMEM((rest, wide, CHUNK), jnp.bfloat16),
            pltpu.VMEM((2 * wide, toks), jnp.float32),
            pltpu.VMEM((wide, toks), jnp.float32),
            pltpu.VMEM((toks, 2 * wide), jnp.bfloat16),
            pltpu.VMEM((toks, LANES), jnp.float32),
            pltpu.SemaphoreType.DMA((rest, 3)),
        ],
        compiler_params=pltpu.CompilerParams(vmem_limit_bytes=32 * MIB),
        cost_estimate=pl.CostEstimate(
            flops=10 * toks * half * model, bytes_accessed=6 * half * model, transcendentals=half * toks
        ),
        name="hidden_pass",
    )(own, peer, gain, *in_hbm(weights), *ready)


def weight_kernel(toks, spans, packs, *refs):
    rows_ref, refs = refs[packs], refs[:packs] + refs[packs + 1 :]
    outs, written_ref, buf, right_buf, sems = refs[-7:-4], *refs[-4:]
    slots, _, rows, own_width = buf.shape
    half, each = outs[0].shape[0] // 2, toks // 2
    place = lax.axis_index("dp")
    written_ref[...] = jnp.zeros_like(written_ref)
    own = pl.ds(pl.multiple_of(place * own_width, LANES), own_width)

    def copy(k, slot, row):
        target = outs[k].at[pl.ds(pl.multiple_of(row, 16), rows)]
        return pltpu.make_async_copy(buf.at[slot, k], target, sems.at[slot, k])

    done = 0
    for packed_ref, (swapped, first, last) in zip(refs[:packs], spans):
        top = (1 - place) * half if swapped else place * half
        if swapped:
            for at in (0, toks):
                mine, theirs = rows_ref[at : at + each, own], rows_ref[at + each : at + toks, own]
                right_buf[at : at + toks, :] = jnp.concatenate([theirs, mine], axis=0)
        else:
            right_buf[...] = rows_ref[:, own]

        def step(i, carry, packed_ref=packed_ref, top=top, base=done - first):
            slot = lax.rem(base + i, slots)

            @pl.when(base + i >= slots)
            def _():
                for k in range(3):
                    copy(k, slot, top + i * rows).wait()

            normed, incoming = right_buf[:toks, :], right_buf[toks:, :]
            at = pl.ds(pl.multiple_of(i * rows, 16), rows)
            for k, right in enumerate((normed, normed, incoming)):
                left = packed_ref[at, :][:, k * toks : (k + 1) * toks]
                value = jnp.dot(left, right, preferred_element_type=jnp.float32)
                buf[slot, k] = value.astype(jnp.bfloat16)
                copy(k, slot, top + i * rows).start()
            return carry

        lax.fori_loop(first, last, step, 0)
        done += last - first
    for slot in range(min(slots, done)):
        for k in range(3):
            copy(k, slot, place * half).wait()


def weight_pass(packs, rows, ffw, step_rows, spans, before=(), after=()):
    toks, model = rows.shape[0] // 2, rows.shape[1]
    own_width = model // 2
    blocks = sum(last - first for _, first, last in spans)
    out = jax.ShapeDtypeStruct((ffw, own_width), jnp.bfloat16)
    return pl.pallas_call(
        functools.partial(weight_kernel, toks, spans, len(packs)),
        out_shape=(out,) * 3 + (jax.ShapeDtypeStruct((8, LANES), jnp.float32),),
        in_specs=[VMEM_SPEC] * (len(packs) + 1) + [ANY_SPEC] * (len(before) + len(after)),
        out_specs=(ANY_SPEC,) * 3 + (VMEM_SPEC,),
        scratch_shapes=[
            pltpu.VMEM((3, 3, step_rows, own_width), jnp.bfloat16),
            pltpu.VMEM((2 * toks, own_width), jnp.bfloat16),
            pltpu.SemaphoreType.DMA((3, 3)),
        ],
        input_output_aliases={len(packs) + 1 + i: i for i in range(len(before))},
        compiler_params=pltpu.CompilerParams(vmem_limit_bytes=16 * MIB),
        cost_estimate=pl.CostEstimate(
            flops=6 * toks * step_rows * own_width * blocks,
            bytes_accessed=6 * step_rows * own_width * blocks,
            transcendentals=0,
        ),
        name="weight_pass",
    )(*packs, rows, *before, *after)


def add_arrived(kept_ref, gain_ref, arrived, extra, held, gain_out_ref):
    gain = gain_ref[...] + (extra[0:1] + extra[1:2])
    held[...] = kept_ref[...] + arrived
    gain_out_ref[...] = gain
    return gain


def fold_kernel(
    kept_ref, gain_ref, arrived_ref, _, keep_ref, gain_out_ref, send_ref, send_gain_ref, held
):
    count = kept_ref.shape[0]
    arrived = arrived_ref[...].astype(jnp.float32)
    gain = add_arrived(kept_ref, gain_ref, arrived[:count], arrived[count:], held, gain_out_ref)
    keep_ref[...] = held[: count // 2, :]
    send_ref[...] = held[count // 2 :, :].astype(jnp.bfloat16)
    send_gain_ref[:1, :] = high_part(gain)
    send_gain_ref[1:, :] = low_part(gain)


def spread_kernel(rows, kept_ref, gain_ref, arrived_ref, extra_ref, _, own_ref, gain_out_ref, *refs):
    outs, held = refs[:-1], refs[-1]
    arrived, extra = arrived_ref[...].astype(jnp.float32), extra_ref[...].astype(jnp.float32)
    gain = add_arrived(kept_ref, gain_ref, arrived, extra, held, gain_out_ref)
    own_ref[...] = held[:rows, :]
    for k, out in enumerate(outs):
        out[:rows, :] = held[rows * (k + 1) : rows * (k + 2), :].astype(jnp.bfloat16)
        out[rows : rows + 1, :] = high_part(gain)
        out[rows + 1 :, :] = low_part(gain)


def add_rows(kernel, kept, gain, arrived, written, kept_rows, sent_rows, name):
    count, model = kept.shape
    return pl.pallas_call(
        kernel,
        out_shape=(
            jax.ShapeDtypeStruct((kept_rows, model), jnp.float32),
            jax.ShapeDtypeStruct((1, model), jnp.float32),
        )
        + tuple(jax.ShapeDtypeStruct((n, model), jnp.bfloat16) for n in sent_rows),
        in_specs=[VMEM_SPEC] * (2 + len(arrived)) + [ANY_SPEC],
        out_specs=(VMEM_SPEC,) * (2 + len(sent_rows)),
        scratch_shapes=[pltpu.VMEM((count, model), jnp.float32)],
        compiler_params=pltpu.CompilerParams(vmem_limit_bytes=8 * MIB),
        name=name,
    )(kept, gain, *arrived, written)


def finish_kernel(rows, tokens_ref, incoming_ref, norm_gain_ref, own_ref, gain_ref, *refs):
    pieces, input_ref, gain_out_ref = refs[:-2], refs[-2], refs[-1]
    grad_normed, gain = own_ref[...], gain_ref[...]
    for piece in pieces:
        value = piece[...].astype(jnp.float32)
        grad_normed = grad_normed + value[:rows]
        gain = gain + (value[rows : rows + 1] + value[rows + 1 : rows + 2])
    gain_out_ref[...] = gain
    values = tokens_ref[...].astype(jnp.float32)
    inverse = lax.rsqrt(jnp.mean(values * values, axis=-1, keepdims=True) + EPSILON)
    scaled = values * inverse
    grad_scaled = grad_normed * norm_gain_ref[...]
    projected = jnp.mean(grad_scaled * scaled, axis=-1, keepdims=True)
    result = incoming_ref[...].astype(jnp.float32) + inverse * (grad_scaled - scaled * projected)
    input_ref[...] = result.astype(jnp.bfloat16)


def finish(rows, tokens, incoming, norm_gain, own, gain, pieces):
    model = tokens.shape[1]
    return pl.pallas_call(
        functools.partial(finish_kernel, rows),
        out_shape=(
            jax.ShapeDtypeStruct((rows, model), jnp.bfloat16),
            jax.ShapeDtypeStruct((1, model), jnp.float32),
        ),
        in_specs=[VMEM_SPEC] * (5 + len(pieces)),
        out_specs=(VMEM_SPEC,) * 2,
        compiler_params=pltpu.CompilerParams(vmem_limit_bytes=8 * MIB),
        name="finish",
    )(tokens, incoming, norm_gain, own, gain, *pieces)


def small_body(tokens, norm_gain, gate_weight, up_weight, down_weight, cotangent):
    rows, model = tokens.shape[1] * tokens.shape[2], tokens.shape[3]
    ffw = down_weight.shape[0]
    tp_count = lax.axis_size("tp")
    own_tokens, own_incoming = tokens.reshape(rows, model), cotangent.reshape(rows, model)
    gain_hbm = norm_gain.reshape(1, model)

    weights = (gate_weight.T, up_weight.T, down_weight)
    step_rows = 80
    blocks = ffw // 2 // step_rows
    piece = jnp.concatenate([own_tokens, own_incoming], axis=0)
    near = exchange(piece, "tp", 1)
    along = [exchange(piece, "tp", bits) for bits in ALONG_Z]
    fetched, gain_row, done = fetch_weights(weights, gain_hbm, 0, 2, (piece,))
    along = relay(along, done)
    across = [exchange(arrived, "tp", 1) for arrived in along]
    more, _, done = fetch_weights(weights, gain_hbm, 2, 1, (along[0],))
    own = sort_rows(rows, [piece, *along, near, *across], done)
    peer = exchange(own, "dp", 1)
    packed, kept, send, gain, all_rows = hidden_pass(own, peer, gain_row, weights, fetched + more)
    arrived = exchange(send, "dp", 1)
    peer_packed = exchange(packed, "dp", 1)
    cut, turn = blocks // 2, blocks // 3
    *grads, written = weight_pass([packed], all_rows, ffw, step_rows, [(False, 0, cut)])
    kept, gain, send, send_gain = add_rows(
        fold_kernel, kept, gain, [arrived], written, kept.shape[0] // 2, (kept.shape[0] // 2, 2), "fold"
    )
    arrived = [exchange(send, "tp", 1), exchange(send_gain, "tp", 1)]
    *grads, written = weight_pass(
        [packed, peer_packed], all_rows, ffw, step_rows,
        [(False, cut, blocks), (True, 0, turn)], grads, (send,),
    )
    kept, gain, *sends = add_rows(
        functools.partial(spread_kernel, rows), kept, gain, arrived, written, rows, (rows + 2,) * 3,
        "spread",
    )
    arrived = [exchange(send, "tp", bits) for send, bits in zip(sends, ALONG_Z)]
    gate_t, up_t, down_grad, _ = weight_pass(
        [peer_packed], all_rows, ffw, step_rows, [(True, turn, blocks)], grads, (sends[0],)
    )
    input_rows, gain_grad = finish(
        rows, own_tokens, own_incoming, gain_row, kept, gain, arrived
    )
    return (
        input_rows.reshape(tokens.shape),
        gain_grad.reshape(model),
        gate_t.T,
        up_t.T,
        down_grad,
    )


def body(tokens, norm_gain, gate_weight, up_weight, down_weight, cotangent):
    tp_count, dp_count = lax.axis_size("tp"), lax.axis_size("dp")
    ffw, model = down_weight.shape
    toks = tokens.shape[1] * tokens.shape[2] * tp_count * dp_count
    small = (
        dp_count == 2
        and tp_count == 8
        and toks == 32
        and model % 1024 == 0
        and ffw % 320 == 0
        and 3 * ffw * model <= 40 * MIB
    )
    chosen = small_body if small else general_body
    return chosen(tokens, norm_gain, gate_weight, up_weight, down_weight, cotangent)


def solution(mesh):
    placed = (
        P(("groups", "dp"), None, "tp", None),
        P(),
        P(None, "tp"),
        P(None, "tp"),
        P("tp", None),
        P(("groups", "dp"), None, "tp", None),
    )
    return jax.shard_map(
        body,
        mesh=mesh,
        in_specs=placed,
        out_specs=(
            P(("groups", "dp"), None, "tp", None),
            P("groups"),
            P(("groups", "dp"), "tp"),
            P(("groups", "dp"), "tp"),
            P("tp", ("groups", "dp")),
        ),
        check_vma=False,
    )
```
